128 devices in a mesh: ctx: 32 (over y_hi, z, x), head: 4 (over y_lo, core).
Axes of the slice: x: 4, y: 4 (y_hi: 2, y_lo: 2; y = y_hi * 2 + y_lo), z: 4, core: 2. Of those that a mesh axis runs over, the one named last changes fastest.
Arguments:
- queries: bfloat16 [8192, 32, 128], P('ctx', 'head'), may hold values from -40 to 40
- key_rows: bfloat16 [8192, 4, 128], P('ctx', 'head'), may hold values from -4 to 4
- value_matrix: bfloat16 [8192, 4, 128], P('ctx', 'head'), may hold values from -6 to 6
- out_weight: bfloat16 [4096, 5120], P('head'), may hold values from -0.09375 to 0.09375
- cotangent: bfloat16 [8192, 5120], P(('ctx', 'head')), may hold values from -6 to 6
Outputs:
- output: bfloat16 [8192, 5120], P(('ctx', 'head'))
- grad_queries: bfloat16 [8192, 32, 128], P('ctx', 'head')
- grad_keys: bfloat16 [8192, 4, 128], P('ctx', 'head')
- grad_values: bfloat16 [8192, 4, 128], P('ctx', 'head')
The draws below stay inside these ranges and needn't reach their ends.
All inputs are finite; a program needn't handle non-finite values.
Results may differ from the reference program's by a relative error of at most 0.039.
Values may be sent and summed in bfloat16 or wider, within the bound.
A program may use at most 128 MiB of HBM per device.

```python
import math
import jax
import jax.numpy as jnp
from jax import lax

D = 5120
QUERY_HEADS = 32
KEY_VALUE_HEADS = 4
HEAD_SIZE = 128
SEQUENCE_TOKENS = 8192


def shared_keys(key):
    unmasked = jax.random.truncated_normal(jax.random.fold_in(key, 101), -4.0, 4.0, (SEQUENCE_TOKENS, KEY_VALUE_HEADS, HEAD_SIZE), jnp.float32)
    base = unmasked
    tied = (jnp.arange(SEQUENCE_TOKENS) % 97 == 51)[:, None, None]
    return jnp.where(tied, base, base)


def draw_key_rows(key, part):
    return shared_keys(key).astype(jnp.bfloat16)


def draw_queries(key, part):
    own = jax.random.fold_in(key, 7)
    head_scale = jnp.exp(jax.random.uniform(jax.random.fold_in(own, 1), (QUERY_HEADS,), jnp.float32, math.log(0.5), math.log(2.5)))
    noise = jax.random.truncated_normal(jax.random.fold_in(own, 2), -4.0, 4.0, (SEQUENCE_TOKENS, QUERY_HEADS, HEAD_SIZE), jnp.float32)
    return (noise * head_scale[None, :, None]).astype(jnp.bfloat16)


def block_scale(rng, shape, pieces, least, largest):
    def one(position, parts):
        draws = jax.random.uniform(jax.random.fold_in(jax.random.fold_in(rng, 6), position), (parts,), jnp.float32, least / len(pieces), largest / len(pieces))
        return jnp.repeat(jnp.exp(draws), shape[position] // parts).reshape((-1,) + (1,) * (len(shape) - position - 1))

    factor_of = one(*pieces[0])
    for cut in pieces[1:]:
        factor_of = factor_of * one(*cut)
    return factor_of


def bell_draw(rng, shape, scale, bound, shards=(), held_as=jnp.bfloat16):
    values = scale * jax.random.normal(rng, shape, jnp.float32)
    if shards:
        values = values * block_scale(rng, shape, shards, -0.22, 0.18)
    return jnp.clip(values, -bound, bound).astype(held_as)


def setup_inputs(seed: int = 0) -> dict:
    key_of = jax.random.split(jax.random.key(seed), 6)
    return {
        "queries": draw_queries(jax.random.fold_in(key_of[5], 71), 0),
        "key_rows": draw_key_rows(jax.random.fold_in(key_of[5], 71), 0),
        "value_matrix": bell_draw(key_of[2], (SEQUENCE_TOKENS, KEY_VALUE_HEADS, HEAD_SIZE), 1.0, 6.0, ((0, 32), (1, 4))),
        "out_weight": bell_draw(key_of[3], (QUERY_HEADS * HEAD_SIZE, D), (QUERY_HEADS * HEAD_SIZE) ** -0.5, 0.09375, ((0, 4),)),
        "cotangent": bell_draw(key_of[4], (SEQUENCE_TOKENS, D), 1.0, 6.0, ((0, 128),)),
    }


def lowered(values):
    return lax.optimization_barrier(values.astype(jnp.bfloat16)).astype(jnp.float32)

def reference(queries, key_rows, value_matrix, out_weight, cotangent):
    tokens, q_heads, head_dim = queries.shape
    kv_heads = key_rows.shape[1]
    group = q_heads // kv_heads
    scale = 1.0 / math.sqrt(head_dim)
    block = min(256, tokens)
    count = tokens // block
    query_all = queries.astype(jnp.float32).reshape(tokens, kv_heads, group, head_dim)
    key_all = key_rows.astype(jnp.float32)
    value_all = value_matrix.astype(jnp.float32)
    key_pos = jnp.arange(tokens, dtype=jnp.int32)

    def scores_of(index):
        start = (index * block).astype(jnp.int32)
        query_block = lax.dynamic_slice_in_dim(query_all, start, block, 0)
        scores = jnp.einsum('rkgd,jkd->kgrj', query_block, key_all) * scale
        query_pos = start + jnp.arange(block, dtype=jnp.int32)
        visible = key_pos[None, :] <= query_pos[:, None]
        return (query_block, jnp.where(visible, scores, -jnp.inf))

    def forward_block(index):
        query_block, scores = scores_of(index)
        top = lax.optimization_barrier(jnp.max(scores, axis=-1))
        lse = top + jnp.log(lax.optimization_barrier(jnp.sum(jnp.exp(scores - top[..., None]), axis=-1)))
        weight_tensors = lowered(jnp.exp(scores - lse[..., None]))
        attn = jnp.einsum('kgrj,jkd->rkgd', weight_tensors, value_all).astype(jnp.bfloat16)
        return (attn, lse)
    attn_blocks, lse_blocks = lax.map(forward_block, jnp.arange(count, dtype=jnp.int32))
    attn = attn_blocks.reshape(tokens, q_heads * head_dim)
    output = jnp.dot(attn, out_weight, preferred_element_type=jnp.float32).astype(jnp.bfloat16)
    grad_attn = jnp.dot(cotangent, out_weight.T, preferred_element_type=jnp.float32).astype(jnp.bfloat16)
    grad_all = grad_attn.astype(jnp.float32).reshape(tokens, kv_heads, group, head_dim)
    attn_all = attn.astype(jnp.float32).reshape(tokens, kv_heads, group, head_dim)
    delta = lax.optimization_barrier(jnp.sum(grad_all * attn_all, axis=-1))

    def backward_block(carry, index):
        key_sum, value_sum = carry
        query_block, scores = scores_of(index)
        start = (index * block).astype(jnp.int32)
        probs = jnp.exp(scores - lse_blocks[index][..., None])
        grad_block = lax.dynamic_slice_in_dim(grad_all, start, block, 0)
        delta_block = jnp.transpose(lax.dynamic_slice_in_dim(delta, start, block, 0), (1, 2, 0))
        grad_weights = jnp.einsum('rkgd,jkd->kgrj', grad_block, value_all)
        score_gradient = lowered(probs * (grad_weights - delta_block[..., None]) * scale)
        grad_query = jnp.einsum('kgrj,jkd->rkgd', score_gradient, key_all).astype(jnp.bfloat16)
        key_sum = key_sum + jnp.einsum('kgrj,rkgd->jkd', score_gradient, query_block)
        value_sum = value_sum + jnp.einsum('kgrj,rkgd->jkd', lowered(probs), grad_block)
        return ((key_sum, value_sum), grad_query)
    zeros = jnp.zeros((tokens, kv_heads, head_dim), jnp.float32)
    (key_sum, value_sum), grad_blocks = lax.scan(backward_block, (zeros, zeros), jnp.arange(count, dtype=jnp.int32))
    grad_queries = grad_blocks.reshape(tokens, q_heads, head_dim)
    return (output, grad_queries, key_sum.astype(jnp.bfloat16), value_sum.astype(jnp.bfloat16))
```

```python
import functools
import math

import jax
import jax.numpy as jnp
from jax import lax
from jax.experimental import pallas as pl
from jax.experimental.pallas import tpu as pltpu
from jax.sharding import PartitionSpec as P

BF = jnp.bfloat16
F32 = jnp.float32
MESH = pl.DeviceIdType.MESH
YS, ZS, XS = 2, 4, 4
NCTX = YS * ZS * XS
HEAD = 128
GROUP = 8
BLOCK = 256
UNIT = 256
UNIT_POS = UNIT // GROUP
OWN = BLOCK * GROUP // UNIT
GIVE = 4
WORK = (OWN + GIVE) * UNIT
LOW = -1e30
VMEM_LIMIT = 60 * 1024 * 1024

NT = (((1,), (1,)), ((), ()))
NN = (((1,), (0,)), ((), ()))
TN = (((0,), (0,)), ((), ()))


def dot(a, b, dims):
    return lax.dot_general(a, b, dims, preferred_element_type=F32)


def share():
    c = lax.axis_index("ctx")
    low = jnp.minimum(c, NCTX - 1 - c)
    given = jnp.where(
        low <= 2, 4, jnp.where(low <= 8, 3, jnp.where(low <= 11, 2, jnp.where(low <= 14, 1, 0)))
    )
    return c, c < NCTX // 2, given


def place():
    c = lax.axis_index("ctx")
    return c // (ZS * XS), (c // XS) % ZS, c % XS


def ctx_of(y, z, x):
    return (y * ZS + z) * XS + x


def neighbours():
    y, z, x = place()
    xs = [ctx_of(y, z, (x + d) % XS) for d in (1, XS - 1)]
    zs = [ctx_of(y, (z + d) % ZS, x) for d in (1, ZS - 1)]
    return ctx_of(1 - y, z, x), xs, zs


def greet(ctx_list, head_list):
    barrier = pltpu.get_barrier_semaphore()
    for other in ctx_list:
        pl.semaphore_signal(barrier, inc=1, device_id={"ctx": other}, device_id_type=MESH)
    for other in head_list:
        pl.semaphore_signal(barrier, inc=1, device_id={"head": other}, device_id_type=MESH)
    pl.semaphore_wait(barrier, len(ctx_list) + len(head_list))


class Courier:
    def __init__(self, send, recv):
        self.send, self.recv, self.made = send, recv, {}

    def plan(self, name, axis, other, src, dst):
        n = len(self.made)
        self.made[name] = lambda: pltpu.make_async_remote_copy(
            src_ref=src,
            dst_ref=dst,
            send_sem=self.send.at[n],
            recv_sem=self.recv.at[n],
            device_id={axis: other},
            device_id_type=MESH,
        )

    def go(self, *names):
        for name in names:
            self.made[name]().start()

    def got(self, *names):
        for name in names:
            self.made[name]().wait_recv()

    def finish(self):
        for copy in self.made.values():
            copy().wait_send()


class Handover:
    def __init__(self, send, recv, src, src_unit, dst, dst_unit, from_low):
        c, is_low, given = share()
        self.given = given
        self.sends = is_low if from_low else jnp.logical_not(is_low)
        self.takes = jnp.logical_not(self.sends)

        def copy(i):
            return pltpu.make_async_remote_copy(
                src_ref=src.at[pl.ds((src_unit + i) * UNIT, UNIT)],
                dst_ref=dst.at[pl.ds((dst_unit + i) * UNIT, UNIT)],
                send_sem=send.at[i],
                recv_sem=recv.at[i],
                device_id={"ctx": NCTX - 1 - c},
                device_id_type=MESH,
            )

        self.copy = copy

    def each(self, who, act):
        for i in range(GIVE):

            @pl.when(jnp.logical_and(who, i < self.given))
            def _():
                act(i)

    def start(self):
        self.each(self.sends, lambda i: self.copy(i).start())

    def wait_recv(self):
        self.each(self.takes, lambda i: self.copy(i).wait_recv())

    def wait_send(self):
        self.each(self.sends, lambda i: self.copy(i).wait_send())


def tail_of(x):
    one = x.astype(BF).astype(F32)
    rest = x - one
    two = rest.astype(BF).astype(F32)
    three = rest - two
    lane = lax.broadcasted_iota(jnp.int32, x.shape, 1)
    return jnp.where(
        lane == 0, -one, jnp.where(lane == 1, -two, jnp.where(lane == 2, -three, 0.0))
    ).astype(BF)


def layer_kernel(
    unit, scale,
    k_ref, v_ref, cot_ref, q_ref, w_hbm,
    dq_ref, gk_ref, gv_ref, o_ref,
    w_ref, wsem, kv_ref, ca_ref, qw_ref, ga_ref, attn_ref, m_row, l_row, acc_ref,
    attn_far, dq_par, dq_far, af_ref, flat_ref, opart, ocore, osum, orow,
    qx_ref, gx_ref, kx_ref, vx_ref, dqs_ref, dk_ref, dv_ref,
    p_ref, t_ref, r_ref, m_ref, t2_ref, r2_ref, s_ref, y_ref,
    send, recv, hsend, hrecv,
):
    y, z, x = place()
    c, is_low, given = share()
    h = lax.axis_index("head")
    core, row = h ^ 1, h ^ 2
    mine, up = h % 2, h // 2
    partner, xs, zs = neighbours()
    w_copy = pltpu.make_async_copy(w_hbm, w_ref, wsem)
    w_copy.start()
    greet([partner] + xs + zs + [NCTX - 1 - c], [core, row])
    mail = Courier(send, recv)

    def hand(i, *what):
        return Handover(hsend.at[i], hrecv.at[i], *what)

    kv_ref[c, 0] = k_ref[...]
    kv_ref[c, 1] = v_ref[...]
    mail.plan("pair", "ctx", partner, kv_ref.at[c], kv_ref.at[c])
    mail.go("pair")
    qs = hand(0, q_ref, 0, qw_ref, OWN, False)
    gs = hand(1, ga_ref, 0, ga_ref, OWN, False)
    attn_home = hand(2, attn_ref, OWN, attn_far, 0, True)
    dq_home = hand(3, dq_par, 0, dq_far, 0, True)
    qs.start()
    ca_ref[h] = cot_ref[...]
    for name, o, i in (("cot row", row, h), ("cot core", core, h), ("cot relay", core, row)):
        mail.plan(name, "head", o, ca_ref.at[i], ca_ref.at[i])
    mail.go("cot row", "cot core")

    routes = ((z, x, zs, xs), (x, z, xs, zs))
    for n, (a, b, an, bn) in enumerate(routes):

        def slot(i, j, n=n):
            return kv_ref.at[jnp.where(n == 0, 16 + i * 4 + j, j * 4 + i)]

        for d in range(2):
            mail.plan((n, "beside", d), "ctx", an[d], slot(a, b), slot(a, b))
            part = slot((a + (3, 1)[d]) % 4, b).at[d]
            mail.plan((n, "on", d), "ctx", an[d], part, part)
            for s, off in enumerate((0, 3, 1, 2)):
                i = (a + off) % 4
                mail.plan((n, "third", s, d), "ctx", bn[d], slot(i, b), slot(i, b))
                part = slot(i, (b + (3, 1)[d]) % 4).at[d]
                mail.plan((n, "last", s, d), "ctx", bn[d], part, part)

    def pass_on(n, s):
        for d in range(2):
            mail.got((n, "third", s, d))
            mail.go((n, "last", s, d))

    for n, (a, an, b, bn) in enumerate(((x, xs, z, zs), (z, zs, x, xs))):
        steps = (
            (1, p_ref.at[n], a, an, t_ref.at[n], r_ref.at[n]),
            (2, m_ref.at[n], b, bn, t2_ref.at[n], r2_ref.at[n]),
        )
        for stage, piece, at, to, t, r in steps:
            for d in range(2):
                nxt = (at + (1, 3)[d]) % 4
                mail.plan((n, stage, "far", d), "ctx", to[d], piece.at[(at + 2) % 4, d], t.at[d])
                mail.plan(
                    (n, stage, "near", d), "ctx", to[d], piece.at[nxt, 1 - d], r.at[d, 1 - d]
                )
                mail.plan((n, stage, "sum", d), "ctx", to[d], t.at[d], r.at[d, d])
    mail.plan("y", "ctx", partner, s_ref.at[y], y_ref)
    for i in range(2):
        mail.plan(("core", i), "head", core, opart.at[2 * i + 1 - mine], ocore.at[i])
    mail.plan("row", "head", row, osum.at[1 - up], orow)

    def far(n, stage):
        mail.go((n, stage, "far", 0), (n, stage, "far", 1))

    def near(n, stage, d):
        mail.go((n, stage, "near", d))

    def relay(n, stage):
        piece, at, t = (
            (p_ref.at[n], (x, z)[n], t_ref.at[n])
            if stage == 1
            else (m_ref.at[n], (z, x)[n], t2_ref.at[n])
        )
        for d in range(2):
            nxt = (at + (1, 3)[d]) % 4
            mail.got((n, stage, "far", d))
            t[d] = (piece[nxt, d].astype(F32) + t[d].astype(F32)).astype(BF)
            mail.go((n, stage, "sum", d))

    def arrived(n, stage):
        for d in range(2):
            mail.got((n, stage, "near", d), (n, stage, "sum", d))

    def total_first(n):
        arrived(n, 1)
        at = (x, z)[n]
        for kv in range(2):
            for j in range(4):
                m_ref[n, j, kv] = (
                    p_ref[n, at, kv, j].astype(F32)
                    + r_ref[n, 0, kv, j].astype(F32)
                    + r_ref[n, 1, kv, j].astype(F32)
                ).astype(BF)
        far(n, 2)
        near(n, 2, 0)
        near(n, 2, 1)

    def total_second(n):
        arrived(n, 2)
        at = (z, x)[n]
        s_ref[n] = (
            m_ref[n, at].astype(F32) + r2_ref[n, 0].astype(F32) + r2_ref[n, 1].astype(F32)
        ).astype(BF)

    def output_projection():
        attn_home.wait_recv()
        own = OWN * UNIT
        af_ref[...] = attn_ref[pl.ds(0, own), :].astype(F32)

        def place_far(i):
            rows = pl.ds(i * UNIT, UNIT)
            af_ref[rows, :] = attn_far[rows, :].astype(F32)

        attn_home.each(attn_home.takes, place_far)
        for i in range(GROUP):
            flat_ref[:, i * HEAD : (i + 1) * HEAD] = af_ref[
                pl.ds(i, BLOCK, stride=GROUP), :
            ].astype(BF)
        wide = 512

        def chunk(n, carry):
            cols = pl.ds(pl.multiple_of(n * wide, wide), wide)
            part = dot(flat_ref[...], w_ref[:, cols], NN).astype(BF)
            opart[:, :, cols] = part.reshape(4, BLOCK // 4, wide)
            return carry

        lax.fori_loop(0, w_ref.shape[1] // wide, chunk, 0)
        mail.go(("core", 0), ("core", 1))

    def output_core():
        for i in range(2):
            mail.got(("core", i))
            osum[i] = (opart[2 * i + mine].astype(F32) + ocore[i].astype(F32)).astype(BF)
        mail.go("row")

    begin = jnp.where(is_low, 0, given)
    taken = OWN + jnp.where(is_low, given, 0)

    def block_of(n, at, j):
        return jnp.where(n == 0, 16 + 4 * j + at, 4 * at + j)

    def over_group(n, at, tile, between=None):
        def row_set(own, carry):
            mine_now = own == 1
            u0 = jnp.where(mine_now, begin, OWN)
            u1 = jnp.where(mine_now, OWN, taken)
            qb = jnp.where(mine_now, c, NCTX - 1 - c)
            pos0 = jnp.where(mine_now, 0, OWN)
            twos = (u1 - u0) // 2
            odd = (u1 - u0) % 2

            def key_pair(jp, carry):
                whole = qb > block_of(n, at, 2 * jp + 1)

                def full(i, carry):
                    tile(u0 + 2 * i, 2, 2 * jp, 2, None)
                    return carry

                lax.fori_loop(0, jnp.where(whole, twos, 0), full, 0)

                @pl.when(jnp.logical_and(whole, odd == 1))
                def _():
                    tile(u1 - 1, 1, 2 * jp, 2, None)

                def single_block(j, carry):
                    ahead = (qb - block_of(n, at, j)) * BLOCK
                    some = jnp.logical_and(jnp.logical_not(whole), ahead >= 0)

                    def part(i, carry):
                        u = u0 + 2 * i
                        tile(u, 2, j, 1, ahead + (u - pos0) * UNIT_POS)
                        return carry

                    lax.fori_loop(0, jnp.where(some, twos, 0), part, 0)

                    @pl.when(jnp.logical_and(some, odd == 1))
                    def _():
                        u = u1 - 1
                        tile(u, 1, j, 1, ahead + (u - pos0) * UNIT_POS)

                    return carry

                lax.fori_loop(2 * jp, 2 * jp + 2, single_block, 0)
                return carry

            lax.fori_loop(0, 2, key_pair, 0)
            if between is not None:
                between(own)
            return carry

        lax.fori_loop(0, 2, row_set, 0)

    def rows_of(first, units):
        return pl.ds(pl.multiple_of(first * UNIT, UNIT), units * UNIT)

    def mask(keys, n, ahead):
        qpos = ahead + lax.broadcasted_iota(jnp.int32, (keys, n), 1) // GROUP
        return lax.broadcasted_iota(jnp.int32, (keys, n), 0) <= qpos

    def forward_group(s, carry):
        n = 1 - s % 2
        i = s // 2
        off = jnp.where(i == 0, 0, jnp.where(i == 1, 3, jnp.where(i == 2, 1, 2)))
        at = (jnp.where(n == 0, x, z) + off) % 4

        @pl.when(s == 1)
        def _():
            for step in range(2):
                pass_on(1, step)
                pass_on(0, step)

        @pl.when(s == 2)
        def _():
            pass_on(1, 2)
            pass_on(1, 3)
            mail.got("cot row")
            mail.go("cot relay")

        @pl.when(s == 3)
        def _():
            pass_on(0, 2)
            pass_on(0, 3)

        @pl.when(s == 5)
        def _():
            project_cotangent()

        for n_now in range(2):

            @pl.when(s == 7 - n_now)
            def _():
                for step in range(4):
                    mail.got((n_now, "last", step, 0), (n_now, "last", step, 1))

        def tile(first, units, j, blocks, ahead):
            rows = rows_of(first, units)
            held = [block_of(n, at, j + i) for i in range(blocks)]
            keys = jnp.concatenate([kv_ref[b, 0] for b in held], axis=0)
            values = jnp.concatenate([kv_ref[b, 1] for b in held], axis=0)
            sc = dot(keys, qw_ref[rows, :], NT)
            if ahead is not None:
                sc = jnp.where(mask(sc.shape[0], sc.shape[1], ahead), sc, LOW)
            top = m_row[:, rows]
            new = jnp.maximum(top, jnp.max(sc, axis=0, keepdims=True))
            alpha = jnp.exp2((top - new) * unit)
            p = jnp.exp2((sc - new) * unit)
            m_row[:, rows] = new
            l_row[:, rows] = l_row[:, rows] * alpha + jnp.sum(p, axis=0, keepdims=True)
            acc_ref[:, rows] = acc_ref[:, rows] * alpha + dot(values, p.astype(BF), TN)

        over_group(n, at, tile)
        return carry

    def project_cotangent():
        mail.got("cot core", "cot relay")
        w_copy.wait()

        def project(n, carry):
            wide = 1024
            total = jnp.zeros((BLOCK, 2 * HEAD), F32)
            for i in range(cot_ref.shape[1] // wide):
                cols = pl.ds(i * wide, wide)
                total += dot(
                    ca_ref[:, :, cols].reshape(BLOCK, wide),
                    w_ref[pl.ds(pl.multiple_of(n * 2 * HEAD, 2 * HEAD), 2 * HEAD), cols],
                    NT,
                )
            for i in range(2):
                af_ref[pl.ds(2 * n + i, BLOCK, stride=GROUP), :] = total[
                    :, i * HEAD : (i + 1) * HEAD
                ]
            return carry

        lax.fori_loop(0, GROUP // 2, project, 0)
        ga_ref[pl.ds(0, OWN * UNIT), :] = af_ref[...].astype(BF)
        gs.start()

    qw_ref[pl.ds(0, OWN * UNIT), :] = q_ref[...]
    m_row[...] = jnp.full_like(m_row, LOW)
    l_row[...] = jnp.zeros_like(l_row)
    acc_ref[...] = jnp.zeros_like(acc_ref)
    mail.got("pair")
    for n in range(2):
        mail.go((n, "beside", 0), (n, "beside", 1), (n, "third", 0, 0), (n, "third", 0, 1))
    for n in range(2):
        for d in range(2):
            mail.got((n, "beside", d))
            mail.go((n, "on", d), (n, "third", 1 + d, 0), (n, "third", 1 + d, 1))
    for n in range(2):
        mail.got((n, "on", 0), (n, "on", 1))
        mail.go((n, "third", 3, 0), (n, "third", 3, 1))
    qs.wait_recv()
    lax.fori_loop(0, 8, forward_group, 0)

    def finish_forward(i, carry):
        rows = pl.ds(pl.multiple_of(i * 512, 512), 512)
        l = l_row[:, rows]
        attn_ref[rows, :] = jnp.transpose(acc_ref[:, rows] / l).astype(BF)
        lse = m_row[:, rows] + jnp.log2(l) / unit
        one = lse.astype(BF).astype(F32)
        rest = lse - one
        two = rest.astype(BF).astype(F32)
        three = rest - two
        which = lax.broadcasted_iota(jnp.int32, (HEAD, 512), 0)
        pieces = jnp.where(
            which == 0, -one, jnp.where(which == 1, -two, jnp.where(which == 2, -three, 0.0))
        )
        qx_ref[rows, :HEAD] = qw_ref[rows, :]
        qx_ref[rows, HEAD:] = jnp.transpose(pieces).astype(BF)
        return carry

    lax.fori_loop(0, WORK // 512, finish_forward, 0)
    attn_home.start()
    gs.wait_recv()

    def prepare(i, carry):
        rows = pl.ds(pl.multiple_of(i * 512, 512), 512)
        ga = ga_ref[rows, :]
        delta = jnp.sum(ga.astype(F32) * attn_ref[rows, :].astype(F32), axis=1, keepdims=True)
        gx_ref[rows, :HEAD] = ga
        gx_ref[rows, HEAD:] = tail_of(jnp.broadcast_to(delta, (512, HEAD)))
        dqs_ref[rows, :] = jnp.zeros((512, HEAD), F32)
        return carry

    lax.fori_loop(0, WORK // 512, prepare, 0)
    lane = lax.broadcasted_iota(jnp.int32, (4 * BLOCK, HEAD), 1)
    ones = jnp.where(lane < 3, 1.0, 0.0).astype(BF)
    kx_ref[:, HEAD:] = ones
    vx_ref[:, HEAD:] = ones

    def backward_group(s, carry):
        n = s % 2
        i = s // 2
        off = jnp.where(i == 0, 2, jnp.where(i == 1, 1, jnp.where(i == 2, 3, 0)))
        at = (jnp.where(n == 0, x, z) + off) % 4

        for j in range(4):
            ks = pl.ds(j * BLOCK, BLOCK)
            kx_ref[ks, :HEAD] = kv_ref[block_of(n, at, j), 0]
            vx_ref[ks, :HEAD] = kv_ref[block_of(n, at, j), 1]
        dk_ref[...] = jnp.zeros_like(dk_ref)
        dv_ref[...] = jnp.zeros_like(dv_ref)

        def tile(first, units, j, blocks, ahead):
            rows = rows_of(first, units)
            ks = pl.ds(pl.multiple_of(j * BLOCK, BLOCK), blocks * BLOCK)
            p = jnp.exp2(dot(kx_ref[ks, :], qx_ref[rows, :], NT) * unit)
            if ahead is not None:
                p = jnp.where(mask(p.shape[0], p.shape[1], ahead), p, 0.0)
            g = dot(vx_ref[ks, :], gx_ref[rows, :], NT)
            ds = (p * g).astype(BF)
            dv_ref[ks, :] += dot(p.astype(BF), gx_ref[rows, :HEAD], NN)
            dk_ref[ks, :] += dot(ds, qx_ref[rows, :HEAD], NN)
            dqs_ref[rows, :] += dot(ds, kx_ref[ks, :HEAD], TN)

        def between(own):
            @pl.when(jnp.logical_and(s == 7, own == 0))
            def _():
                dq_par[...] = (dqs_ref[pl.ds(OWN * UNIT, GIVE * UNIT), :] * scale).astype(BF)
                dq_home.start()

        over_group(n, at, tile, between)
        for j in range(4):
            ks = pl.ds(j * BLOCK, BLOCK)
            p_ref[n, at, 0, j] = (dk_ref[ks, :] * scale).astype(BF)
            p_ref[n, at, 1, j] = dv_ref[ks, :].astype(BF)

        @pl.when(s == 0)
        def _():
            far(0, 1)

        @pl.when(s == 1)
        def _():
            far(1, 1)

        @pl.when(s == 2)
        def _():
            near(0, 1, 0)
            output_projection()

        @pl.when(s == 3)
        def _():
            near(1, 1, 0)

        @pl.when(s == 4)
        def _():
            near(0, 1, 1)
            relay(0, 1)
            output_core()

        @pl.when(s == 5)
        def _():
            near(1, 1, 1)
            relay(1, 1)

        @pl.when(s == 6)
        def _():
            total_first(0)

        return carry

    lax.fori_loop(0, 8, backward_group, 0)
    total_first(1)
    relay(0, 2)
    dq_ref[...] = (dqs_ref[pl.ds(0, OWN * UNIT), :] * scale).astype(BF)
    relay(1, 2)
    total_second(0)

    @pl.when(y == 0)
    def _():
        mail.go("y")

    total_second(1)

    @pl.when(y == 1)
    def _():
        mail.go("y")

    mail.got("row")
    o_ref[...] = (osum[up].astype(F32) + orow[...].astype(F32)).astype(BF)
    dq_home.wait_recv()

    def place_dq(i):
        rows = pl.ds(i * UNIT, UNIT)
        dq_ref[rows, :] = dq_far[rows, :]

    dq_home.each(dq_home.takes, place_dq)
    mail.got("y")
    gk_ref[...] = (s_ref[1 - y, 0].astype(F32) + y_ref[0].astype(F32)).astype(BF)
    gv_ref[...] = (s_ref[1 - y, 1].astype(F32) + y_ref[1].astype(F32)).astype(BF)
    mail.finish()
    for hand in (qs, gs, attn_home, dq_home):
        hand.wait_send()


COPIES = 1 + 3 + 2 * 20 + 2 * 2 * 6 + 1 + 3


def layer(unit, scale, k, v, cot, q, w):
    vm, dma = pltpu.VMEM, pltpu.SemaphoreType.DMA
    part = (BLOCK // 4, w.shape[1])
    return pl.pallas_call(
        functools.partial(layer_kernel, unit, scale),
        out_shape=(
            jax.ShapeDtypeStruct((OWN * UNIT, HEAD), BF),
            jax.ShapeDtypeStruct((BLOCK, HEAD), BF),
            jax.ShapeDtypeStruct((BLOCK, HEAD), BF),
            jax.ShapeDtypeStruct(part, BF),
        ),
        in_specs=vmem_specs(4) + [pl.BlockSpec(memory_space=pl.ANY)],
        out_specs=tuple(vmem_specs(4)),
        scratch_shapes=[
            vm(w.shape, BF),
            dma,
            vm((NCTX, 2, BLOCK, HEAD), BF),
            vm((4,) + cot.shape, BF),
            vm((WORK, HEAD), BF),
            vm((WORK, HEAD), BF),
            vm((WORK, HEAD), BF),
            vm((1, WORK), F32),
            vm((1, WORK), F32),
            vm((HEAD, WORK), F32),
            vm((GIVE * UNIT, HEAD), BF),
            vm((GIVE * UNIT, HEAD), BF),
            vm((GIVE * UNIT, HEAD), BF),
            vm((OWN * UNIT, HEAD), F32),
            vm((BLOCK, GROUP * HEAD), BF),
            vm((4,) + part, BF),
            vm((2,) + part, BF),
            vm((2,) + part, BF),
            vm(part, BF),
            vm((WORK, 2 * HEAD), BF),
            vm((WORK, 2 * HEAD), BF),
            vm((4 * BLOCK, 2 * HEAD), BF),
            vm((4 * BLOCK, 2 * HEAD), BF),
            vm((WORK, HEAD), F32),
            vm((4 * BLOCK, HEAD), F32),
            vm((4 * BLOCK, HEAD), F32),
            vm((2, 4, 2, 4, BLOCK, HEAD), BF),
            vm((2, 2, 4, BLOCK, HEAD), BF),
            vm((2, 2, 2, 4, BLOCK, HEAD), BF),
            vm((2, 4, 2, BLOCK, HEAD), BF),
            vm((2, 2, BLOCK, HEAD), BF),
            vm((2, 2, 2, BLOCK, HEAD), BF),
            vm((2, 2, BLOCK, HEAD), BF),
            vm((2, BLOCK, HEAD), BF),
            dma((COPIES,)),
            dma((COPIES,)),
            dma((4, GIVE)),
            dma((4, GIVE)),
        ],
        compiler_params=pltpu.CompilerParams(
            collective_id=0, has_side_effects=True, vmem_limit_bytes=VMEM_LIMIT
        ),
        name="layer",
    )(k, v, cot, q, w)


def vmem_specs(n):
    return [pl.BlockSpec(memory_space=pltpu.VMEM)] * n


def local(queries, key_rows, value_matrix, out_weight, cotangent):
    rows, heads, head = queries.shape
    scale = 1.0 / math.sqrt(head)
    unit = scale * math.log2(math.e)
    grad_queries, grad_keys, grad_values, output = layer(
        unit,
        scale,
        key_rows.reshape(rows, head),
        value_matrix.reshape(rows, head),
        cotangent,
        queries.reshape(rows * heads, head),
        out_weight,
    )
    return (
        output,
        grad_queries.reshape(rows, heads, head),
        grad_keys.reshape(rows, 1, head),
        grad_values.reshape(rows, 1, head),
    )


def solution(mesh):
    return jax.shard_map(
        local,
        mesh=mesh,
        in_specs=(
            P("ctx", "head", None),
            P("ctx", "head", None),
            P("ctx", "head", None),
            P("head", None),
            P(("ctx", "head"), None),
        ),
        out_specs=(
            P(("ctx", "head"), None),
            P("ctx", "head", None),
            P("ctx", "head", None),
            P("ctx", "head", None),
        ),
        check_vma=False,
    )
```

```python
import functools
import math

import jax
import jax.numpy as jnp
from jax import lax
from jax.experimental import pallas as pl
from jax.experimental.pallas import tpu as pltpu
from jax.sharding import PartitionSpec as P

BF = jnp.bfloat16
F32 = jnp.float32
MESH = pl.DeviceIdType.MESH
YS, ZS, XS = 2, 4, 4
NCTX = YS * ZS * XS
HEAD = 128
GROUP = 8
BLOCK = 256
UNIT = 256
UNIT_POS = UNIT // GROUP
OWN = BLOCK * GROUP // UNIT
GIVE = 4
WORK = (OWN + GIVE) * UNIT
LOW = -1e30
VMEM_LIMIT = 60 * 1024 * 1024

NT = (((1,), (1,)), ((), ()))
NN = (((1,), (0,)), ((), ()))
TN = (((0,), (0,)), ((), ()))


def dot(a, b, dims):
    return lax.dot_general(a, b, dims, preferred_element_type=F32)


def share():
    c = lax.axis_index("ctx")
    low = jnp.minimum(c, NCTX - 1 - c)
    given = jnp.where(
        low <= 2, 4, jnp.where(low <= 8, 3, jnp.where(low <= 11, 2, jnp.where(low <= 14, 1, 0)))
    )
    return c, c < NCTX // 2, given


def place():
    c = lax.axis_index("ctx")
    return c // (ZS * XS), (c // XS) % ZS, c % XS


def ctx_of(y, z, x):
    return (y * ZS + z) * XS + x


def neighbours():
    y, z, x = place()
    xs = [ctx_of(y, z, (x + d) % XS) for d in (1, XS - 1)]
    zs = [ctx_of(y, (z + d) % ZS, x) for d in (1, ZS - 1)]
    return ctx_of(1 - y, z, x), xs, zs


def greet(ctx_list, head_list):
    barrier = pltpu.get_barrier_semaphore()
    for other in ctx_list:
        pl.semaphore_signal(barrier, inc=1, device_id={"ctx": other}, device_id_type=MESH)
    for other in head_list:
        pl.semaphore_signal(barrier, inc=1, device_id={"head": other}, device_id_type=MESH)
    pl.semaphore_wait(barrier, len(ctx_list) + len(head_list))


class Courier:
    def __init__(self, send, recv):
        self.send, self.recv, self.made = send, recv, {}

    def plan(self, name, axis, other, src, dst):
        n = len(self.made)
        self.made[name] = lambda: pltpu.make_async_remote_copy(
            src_ref=src,
            dst_ref=dst,
            send_sem=self.send.at[n],
            recv_sem=self.recv.at[n],
            device_id={axis: other},
            device_id_type=MESH,
        )

    def go(self, *names):
        for name in names:
            self.made[name]().start()

    def got(self, *names):
        for name in names:
            self.made[name]().wait_recv()

    def finish(self):
        for copy in self.made.values():
            copy().wait_send()


class Handover:
    def __init__(self, send, recv, src, src_unit, dst, dst_unit, from_low):
        c, is_low, given = share()
        self.given = given
        self.sends = is_low if from_low else jnp.logical_not(is_low)
        self.takes = jnp.logical_not(self.sends)

        def copy(i):
            return pltpu.make_async_remote_copy(
                src_ref=src.at[pl.ds((src_unit + i) * UNIT, UNIT)],
                dst_ref=dst.at[pl.ds((dst_unit + i) * UNIT, UNIT)],
                send_sem=send.at[i],
                recv_sem=recv.at[i],
                device_id={"ctx": NCTX - 1 - c},
                device_id_type=MESH,
            )

        self.copy = copy

    def each(self, who, act):
        for i in range(GIVE):

            @pl.when(jnp.logical_and(who, i < self.given))
            def _():
                act(i)

    def start(self):
        self.each(self.sends, lambda i: self.copy(i).start())

    def wait_recv(self):
        self.each(self.takes, lambda i: self.copy(i).wait_recv())

    def wait_send(self):
        self.each(self.sends, lambda i: self.copy(i).wait_send())


def tail_of(x):
    one = x.astype(BF).astype(F32)
    rest = x - one
    two = rest.astype(BF).astype(F32)
    three = rest - two
    lane = lax.broadcasted_iota(jnp.int32, x.shape, 1)
    return jnp.where(
        lane == 0, -one, jnp.where(lane == 1, -two, jnp.where(lane == 2, -three, 0.0))
    ).astype(BF)


def layer_kernel(
    unit, scale,
    k_ref, v_ref, cot_ref, q_ref, w_hbm,
    dq_ref, gk_ref, gv_ref, o_ref,
    w_ref, wsem, kv_ref, ca_ref, gt_ref, qw_ref, ga_ref, attn_ref, m_row, l_row, acc_ref,
    attn_far, dq_par, dq_far, af_ref, flat_ref, opart, ocore, osum, orow,
    qx_ref, gx_ref, kx_ref, vx_ref, dqs_ref, dk_ref, dv_ref,
    p_ref, t_ref, r_ref, m_ref, t2_ref, r2_ref, s_ref, y_ref,
    send, recv, hsend, hrecv,
):
    y, z, x = place()
    c, is_low, given = share()
    h = lax.axis_index("head")
    core, row = h ^ 1, h ^ 2
    mine, up = h % 2, h // 2
    partner, xs, zs = neighbours()
    w_copy = pltpu.make_async_copy(w_hbm, w_ref, wsem)
    w_copy.start()
    greet([partner] + xs + zs + [NCTX - 1 - c], [core, row])
    mail = Courier(send, recv)

    def hand(i, *what):
        return Handover(hsend.at[i], hrecv.at[i], *what)

    kv_ref[c, 0] = k_ref[...]
    kv_ref[c, 1] = v_ref[...]
    mail.plan("pair", "ctx", partner, kv_ref.at[c], kv_ref.at[c])
    mail.go("pair")
    qs = hand(0, q_ref, 0, qw_ref, OWN, False)
    gs = hand(1, ga_ref, 0, ga_ref, OWN, False)
    attn_home = hand(2, attn_ref, OWN, attn_far, 0, True)
    dq_home = hand(3, dq_par, 0, dq_far, 0, True)
    qs.start()
    ca_ref[h] = cot_ref[...]
    for name, o, i in (("cot row", row, h), ("cot core", core, h), ("cot relay", core, row)):
        mail.plan(name, "head", o, ca_ref.at[i], ca_ref.at[i])

    routes = ((z, x, zs, xs), (x, z, xs, zs))
    for n, (a, b, an, bn) in enumerate(routes):

        def slot(i, j, n=n):
            return kv_ref.at[jnp.where(n == 0, 16 + i * 4 + j, j * 4 + i)]

        for d in range(2):
            mail.plan((n, "beside", d), "ctx", an[d], slot(a, b), slot(a, b))
            part = slot((a + (3, 1)[d]) % 4, b).at[d]
            mail.plan((n, "on", d), "ctx", an[d], part, part)
            for s, off in enumerate((0, 3, 1, 2)):
                i = (a + off) % 4
                mail.plan((n, "third", s, d), "ctx", bn[d], slot(i, b), slot(i, b))
                part = slot(i, (b + (3, 1)[d]) % 4).at[d]
                mail.plan((n, "last", s, d), "ctx", bn[d], part, part)

    def pass_on(n, s):
        for d in range(2):
            mail.got((n, "third", s, d))
            mail.go((n, "last", s, d))

    for n, (a, an, b, bn) in enumerate(((x, xs, z, zs), (z, zs, x, xs))):
        steps = (
            (1, p_ref.at[n], a, an, t_ref.at[n], r_ref.at[n]),
            (2, m_ref.at[n], b, bn, t2_ref.at[n], r2_ref.at[n]),
        )
        for stage, piece, at, to, t, r in steps:
            for d in range(2):
                nxt = (at + (1, 3)[d]) % 4
                mail.plan((n, stage, "far", d), "ctx", to[d], piece.at[(at + 2) % 4, d], t.at[d])
                mail.plan(
                    (n, stage, "near", d), "ctx", to[d], piece.at[nxt, 1 - d], r.at[d, 1 - d]
                )
                mail.plan((n, stage, "sum", d), "ctx", to[d], t.at[d], r.at[d, d])
    mail.plan("y", "ctx", partner, s_ref.at[y], y_ref)
    for i in range(2):
        mail.plan(("core", i), "head", core, opart.at[2 * i + 1 - mine], ocore.at[i])
    mail.plan("row", "head", row, osum.at[1 - up], orow)

    def far(n, stage):
        mail.go((n, stage, "far", 0), (n, stage, "far", 1))

    def near(n, stage, d):
        mail.go((n, stage, "near", d))

    def relay(n, stage):
        piece, at, t = (
            (p_ref.at[n], (x, z)[n], t_ref.at[n])
            if stage == 1
            else (m_ref.at[n], (z, x)[n], t2_ref.at[n])
        )
        for d in range(2):
            nxt = (at + (1, 3)[d]) % 4
            mail.got((n, stage, "far", d))
            t[d] = (piece[nxt, d].astype(F32) + t[d].astype(F32)).astype(BF)
            mail.go((n, stage, "sum", d))

    def arrived(n, stage):
        for d in range(2):
            mail.got((n, stage, "near", d), (n, stage, "sum", d))

    def total_first(n):
        arrived(n, 1)
        at = (x, z)[n]
        for kv in range(2):
            for j in range(4):
                m_ref[n, j, kv] = (
                    p_ref[n, at, kv, j].astype(F32)
                    + r_ref[n, 0, kv, j].astype(F32)
                    + r_ref[n, 1, kv, j].astype(F32)
                ).astype(BF)
        far(n, 2)
        near(n, 2, 0)
        near(n, 2, 1)

    def total_second(n):
        arrived(n, 2)
        at = (z, x)[n]
        s_ref[n] = (
            m_ref[n, at].astype(F32) + r2_ref[n, 0].astype(F32) + r2_ref[n, 1].astype(F32)
        ).astype(BF)

    def output_projection():
        attn_home.wait_recv()
        own = OWN * UNIT
        af_ref[...] = attn_ref[pl.ds(0, own), :].astype(F32)

        def place_far(i):
            rows = pl.ds(i * UNIT, UNIT)
            af_ref[rows, :] = attn_far[rows, :].astype(F32)

        attn_home.each(attn_home.takes, place_far)
        for i in range(GROUP):
            flat_ref[:, i * HEAD : (i + 1) * HEAD] = af_ref[
                pl.ds(i, BLOCK, stride=GROUP), :
            ].astype(BF)
        wide = 512

        def chunk(n, carry):
            cols = pl.ds(pl.multiple_of(n * wide, wide), wide)
            part = dot(flat_ref[...], w_ref[:, cols], NN).astype(BF)
            opart[:, :, cols] = part.reshape(4, BLOCK // 4, wide)
            return carry

        lax.fori_loop(0, w_ref.shape[1] // wide, chunk, 0)
        mail.go(("core", 0), ("core", 1))

    def output_core():
        for i in range(2):
            mail.got(("core", i))
            osum[i] = (opart[2 * i + mine].astype(F32) + ocore[i].astype(F32)).astype(BF)
        mail.go("row")

    begin = jnp.where(is_low, 0, given)
    taken = OWN + jnp.where(is_low, given, 0)

    def block_of(n, at, j):
        return jnp.where(n == 0, 16 + 4 * j + at, 4 * at + j)

    def over_group(n, at, tile, own_first, between):
        def row_set(turn, carry):
            mine_now = turn == (0 if own_first else 1)
            u0 = jnp.where(mine_now, begin, OWN)
            u1 = jnp.where(mine_now, OWN, taken)
            qb = jnp.where(mine_now, c, NCTX - 1 - c)
            pos0 = jnp.where(mine_now, 0, OWN)
            count = u1 - u0

            def key_pair(jp, carry):
                whole = qb > block_of(n, at, 2 * jp + 1)

                def rows(on, j, blocks, ahead):
                    def many(i, carry):
                        tile(u0 + 4 * i, (2, 2), j, blocks, ahead, u0 + 4 * i - pos0)
                        return carry

                    lax.fori_loop(0, jnp.where(on, count // 4, 0), many, 0)
                    rest = jnp.where(on, count % 4, 0)
                    for k, chains in ((3, (2, 1)), (2, (1, 1)), (1, (1,))):

                        @pl.when(rest == k)
                        def _():
                            tile(u1 - k, chains, j, blocks, ahead, u1 - k - pos0)

                rows(whole, 2 * jp, 2, None)

                def single_block(j, carry):
                    ahead = (qb - block_of(n, at, j)) * BLOCK
                    some = jnp.logical_and(jnp.logical_not(whole), ahead >= 0)
                    rows(some, j, 1, ahead)
                    return carry

                lax.fori_loop(2 * jp, 2 * jp + 2, single_block, 0)
                return carry

            lax.fori_loop(0, 2, key_pair, 0)

            @pl.when(turn == 0)
            def _():
                between()

            return carry

        lax.fori_loop(0, 2, row_set, 0)

    def rows_of(first, units):
        return pl.ds(pl.multiple_of(first * UNIT, UNIT), units * UNIT)

    def mask(keys, n, ahead):
        qpos = ahead + lax.broadcasted_iota(jnp.int32, (keys, n), 1) // GROUP
        return lax.broadcasted_iota(jnp.int32, (keys, n), 0) <= qpos

    def forward_group(s, carry):
        n = (1 - y + s) % 2
        i = s // 2
        off = jnp.where(i == 0, 0, jnp.where(i == 1, 3, jnp.where(i == 2, 1, 2)))
        at = (jnp.where(n == 0, x, z) + off) % 4

        @pl.when(s == 1)
        def _():
            each_pass(True, lambda n: (pass_on(n, 0), pass_on(n, 1)))

        @pl.when(s == 2)
        def _():
            each_pass(True, lambda n: (pass_on(n, 2), pass_on(n, 3)))
            each_pass(False, lambda n: (pass_on(n, 0), pass_on(n, 1)))
            mail.got("cot row")
            mail.go("cot relay")

        @pl.when(s == 3)
        def _():
            each_pass(False, lambda n: (pass_on(n, 2), pass_on(n, 3)))

        @pl.when(s == 5)
        def _():
            project_cotangent()

        def arrived_last(n):
            for step in range(4):
                mail.got((n, "last", step, 0), (n, "last", step, 1))

        @pl.when(s == 6)
        def _():
            each_pass(True, arrived_last)

        @pl.when(s == 7)
        def _():
            each_pass(False, arrived_last)

        def tile(first, chains, j, blocks, ahead, unit_at):
            held = [block_of(n, at, j + i) for i in range(blocks)]
            keys = jnp.concatenate([kv_ref[b, 0] for b in held], axis=0)
            values = jnp.concatenate([kv_ref[b, 1] for b in held], axis=0)
            offsets = [sum(chains[:i]) for i in range(len(chains))]
            sets = [rows_of(first + o, units) for o, units in zip(offsets, chains)]
            scores = [dot(keys, qw_ref[rows, :], NT) for rows in sets]
            for rows, o, sc in zip(sets, offsets, scores):
                if ahead is not None:
                    past = ahead + (unit_at + o) * UNIT_POS
                    sc = jnp.where(mask(sc.shape[0], sc.shape[1], past), sc, LOW)
                top = m_row[:, rows]
                new = jnp.maximum(top, jnp.max(sc, axis=0, keepdims=True))
                alpha = jnp.exp2((top - new) * unit)
                p = jnp.exp2((sc - new) * unit)
                m_row[:, rows] = new
                l_row[:, rows] = l_row[:, rows] * alpha + jnp.sum(p, axis=0, keepdims=True)
                acc_ref[:, rows] = acc_ref[:, rows] * alpha + dot(values, p.astype(BF), TN)

        def between():
            @pl.when(s == 0)
            def _():
                qs.wait_recv()

        over_group(n, at, tile, True, between)
        return carry

    def project_cotangent():
        mail.got("cot core", "cot relay")
        w_copy.wait()

        wide = 1024
        gt_ref[...] = jnp.zeros_like(gt_ref)

        def project(n, carry):
            cols = pl.ds(pl.multiple_of(n * wide, wide), wide)
            gt_ref[...] += dot(w_ref[:, cols], ca_ref[:, :, cols].reshape(BLOCK, wide), NT)
            return carry

        lax.fori_loop(0, w_ref.shape[1] // wide, project, 0)
        for i in range(GROUP):
            af_ref[pl.ds(i, BLOCK, stride=GROUP), :] = jnp.transpose(
                gt_ref[i * HEAD : (i + 1) * HEAD, :]
            )
        ga_ref[pl.ds(0, OWN * UNIT), :] = af_ref[...].astype(BF)
        gs.start()

    def each_pass(first, act):
        for n in range(2):

            @pl.when(y == (1 - n if first else n))
            def _():
                act(n)

    def start(n):
        mail.go((n, "beside", 0), (n, "beside", 1), (n, "third", 0, 0), (n, "third", 0, 1))

    def front(n):
        for d in range(2):
            mail.got((n, "beside", d))
            mail.go((n, "on", d), (n, "third", 1 + d, 0), (n, "third", 1 + d, 1))
        mail.got((n, "on", 0), (n, "on", 1))
        mail.go((n, "third", 3, 0), (n, "third", 3, 1))

    each_pass(True, start)
    qw_ref[pl.ds(0, OWN * UNIT), :] = q_ref[...]
    m_row[...] = jnp.full_like(m_row, LOW)
    l_row[...] = jnp.zeros_like(l_row)
    acc_ref[...] = jnp.zeros_like(acc_ref)
    mail.got("pair")
    each_pass(False, start)
    mail.go("cot row", "cot core")
    each_pass(True, front)
    each_pass(False, front)
    lax.fori_loop(0, 8, forward_group, 0)

    def finish_forward(i, carry):
        rows = pl.ds(pl.multiple_of(i * 512, 512), 512)
        l = l_row[:, rows]
        attn_ref[rows, :] = jnp.transpose(acc_ref[:, rows] / l).astype(BF)
        lse = m_row[:, rows] + jnp.log2(l) / unit
        one = lse.astype(BF).astype(F32)
        rest = lse - one
        two = rest.astype(BF).astype(F32)
        three = rest - two
        which = lax.broadcasted_iota(jnp.int32, (HEAD, 512), 0)
        pieces = jnp.where(
            which == 0, -one, jnp.where(which == 1, -two, jnp.where(which == 2, -three, 0.0))
        )
        qx_ref[rows, :HEAD] = qw_ref[rows, :]
        qx_ref[rows, HEAD:] = jnp.transpose(pieces).astype(BF)
        return carry

    lax.fori_loop(0, WORK // 512, finish_forward, 0)
    attn_home.start()
    gs.wait_recv()

    def prepare(i, carry):
        rows = pl.ds(pl.multiple_of(i * 512, 512), 512)
        ga = ga_ref[rows, :]
        delta = jnp.sum(ga.astype(F32) * attn_ref[rows, :].astype(F32), axis=1, keepdims=True)
        gx_ref[rows, :HEAD] = ga
        gx_ref[rows, HEAD:] = tail_of(jnp.broadcast_to(delta, (512, HEAD)))
        dqs_ref[rows, :] = jnp.zeros((512, HEAD), F32)
        return carry

    lax.fori_loop(0, WORK // 512, prepare, 0)
    lane = lax.broadcasted_iota(jnp.int32, (4 * BLOCK, HEAD), 1)
    ones = jnp.where(lane < 3, 1.0, 0.0).astype(BF)
    kx_ref[:, HEAD:] = ones
    vx_ref[:, HEAD:] = ones

    def backward_group(s, carry):
        n = s % 2
        i = s // 2
        off = jnp.where(i == 0, 2, jnp.where(i == 1, 1, jnp.where(i == 2, 3, 0)))
        at = (jnp.where(n == 0, x, z) + off) % 4

        for j in range(4):
            ks = pl.ds(j * BLOCK, BLOCK)
            kx_ref[ks, :HEAD] = kv_ref[block_of(n, at, j), 0]
            vx_ref[ks, :HEAD] = kv_ref[block_of(n, at, j), 1]
        dk_ref[...] = jnp.zeros_like(dk_ref)
        dv_ref[...] = jnp.zeros_like(dv_ref)

        def tile(first, chains, j, blocks, ahead, unit_at):
            ks = pl.ds(pl.multiple_of(j * BLOCK, BLOCK), blocks * BLOCK)
            offsets = [sum(chains[:i]) for i in range(len(chains))]
            sets = [rows_of(first + o, units) for o, units in zip(offsets, chains)]
            scores = [dot(kx_ref[ks, :], qx_ref[rows, :], NT) for rows in sets]
            grads = [dot(vx_ref[ks, :], gx_ref[rows, :], NT) for rows in sets]
            dv, dk = 0.0, 0.0
            for rows, o, sc, g in zip(sets, offsets, scores, grads):
                p = jnp.exp2(sc * unit)
                if ahead is not None:
                    past = ahead + (unit_at + o) * UNIT_POS
                    p = jnp.where(mask(p.shape[0], p.shape[1], past), p, 0.0)
                ds = (p * g).astype(BF)
                dv += dot(p.astype(BF), gx_ref[rows, :HEAD], NN)
                dk += dot(ds, qx_ref[rows, :HEAD], NN)
                dqs_ref[rows, :] += dot(ds, kx_ref[ks, :HEAD], TN)
            dv_ref[ks, :] += dv
            dk_ref[ks, :] += dk

        def between():
            @pl.when(s == 7)
            def _():
                dq_par[...] = (dqs_ref[pl.ds(OWN * UNIT, GIVE * UNIT), :] * scale).astype(BF)
                dq_home.start()
                relay(0, 2)

        over_group(n, at, tile, False, between)
        for j in range(4):
            ks = pl.ds(j * BLOCK, BLOCK)
            p_ref[n, at, 0, j] = (dk_ref[ks, :] * scale).astype(BF)
            p_ref[n, at, 1, j] = dv_ref[ks, :].astype(BF)

        @pl.when(s == 0)
        def _():
            far(0, 1)

        @pl.when(s == 1)
        def _():
            far(1, 1)

        @pl.when(s == 2)
        def _():
            near(0, 1, 0)
            output_projection()

        @pl.when(s == 3)
        def _():
            near(1, 1, 0)

        @pl.when(s == 4)
        def _():
            near(0, 1, 1)
            relay(0, 1)
            output_core()

        @pl.when(s == 5)
        def _():
            near(1, 1, 1)
            relay(1, 1)

        @pl.when(s == 6)
        def _():
            total_first(0)

        return carry

    lax.fori_loop(0, 8, backward_group, 0)
    total_first(1)
    dq_ref[...] = (dqs_ref[pl.ds(0, OWN * UNIT), :] * scale).astype(BF)
    relay(1, 2)
    total_second(0)

    @pl.when(y == 0)
    def _():
        mail.go("y")

    total_second(1)

    @pl.when(y == 1)
    def _():
        mail.go("y")

    mail.got("row")
    o_ref[...] = (osum[up].astype(F32) + orow[...].astype(F32)).astype(BF)
    dq_home.wait_recv()

    def place_dq(i):
        rows = pl.ds(i * UNIT, UNIT)
        dq_ref[rows, :] = dq_far[rows, :]

    dq_home.each(dq_home.takes, place_dq)
    mail.got("y")
    gk_ref[...] = (s_ref[1 - y, 0].astype(F32) + y_ref[0].astype(F32)).astype(BF)
    gv_ref[...] = (s_ref[1 - y, 1].astype(F32) + y_ref[1].astype(F32)).astype(BF)
    mail.finish()
    for hand in (qs, gs, attn_home, dq_home):
        hand.wait_send()


COPIES = 1 + 3 + 2 * 20 + 2 * 2 * 6 + 1 + 3


def layer(unit, scale, k, v, cot, q, w):
    vm, dma = pltpu.VMEM, pltpu.SemaphoreType.DMA
    part = (BLOCK // 4, w.shape[1])
    return pl.pallas_call(
        functools.partial(layer_kernel, unit, scale),
        out_shape=(
            jax.ShapeDtypeStruct((OWN * UNIT, HEAD), BF),
            jax.ShapeDtypeStruct((BLOCK, HEAD), BF),
            jax.ShapeDtypeStruct((BLOCK, HEAD), BF),
            jax.ShapeDtypeStruct(part, BF),
        ),
        in_specs=vmem_specs(4) + [pl.BlockSpec(memory_space=pl.ANY)],
        out_specs=tuple(vmem_specs(4)),
        scratch_shapes=[
            vm(w.shape, BF),
            dma,
            vm((NCTX, 2, BLOCK, HEAD), BF),
            vm((4,) + cot.shape, BF),
            vm((GROUP * HEAD, BLOCK), F32),
            vm((WORK, HEAD), BF),
            vm((WORK, HEAD), BF),
            vm((WORK, HEAD), BF),
            vm((1, WORK), F32),
            vm((1, WORK), F32),
            vm((HEAD, WORK), F32),
            vm((GIVE * UNIT, HEAD), BF),
            vm((GIVE * UNIT, HEAD), BF),
            vm((GIVE * UNIT, HEAD), BF),
            vm((OWN * UNIT, HEAD), F32),
            vm((BLOCK, GROUP * HEAD), BF),
            vm((4,) + part, BF),
            vm((2,) + part, BF),
            vm((2,) + part, BF),
            vm(part, BF),
            vm((WORK, 2 * HEAD), BF),
            vm((WORK, 2 * HEAD), BF),
            vm((4 * BLOCK, 2 * HEAD), BF),
            vm((4 * BLOCK, 2 * HEAD), BF),
            vm((WORK, HEAD), F32),
            vm((4 * BLOCK, HEAD), F32),
            vm((4 * BLOCK, HEAD), F32),
            vm((2, 4, 2, 4, BLOCK, HEAD), BF),
            vm((2, 2, 4, BLOCK, HEAD), BF),
            vm((2, 2, 2, 4, BLOCK, HEAD), BF),
            vm((2, 4, 2, BLOCK, HEAD), BF),
            vm((2, 2, BLOCK, HEAD), BF),
            vm((2, 2, 2, BLOCK, HEAD), BF),
            vm((2, 2, BLOCK, HEAD), BF),
            vm((2, BLOCK, HEAD), BF),
            dma((COPIES,)),
            dma((COPIES,)),
            dma((4, GIVE)),
            dma((4, GIVE)),
        ],
        compiler_params=pltpu.CompilerParams(
            collective_id=0, has_side_effects=True, vmem_limit_bytes=VMEM_LIMIT
        ),
        name="layer",
    )(k, v, cot, q, w)


def results_kernel(*refs):
    n = len(refs) // 2
    for i in range(n):
        refs[n + i][...] = refs[i][...]


def results(*arrays):
    n = len(arrays)
    return pl.pallas_call(
        results_kernel,
        out_shape=tuple(jax.ShapeDtypeStruct(a.shape, a.dtype) for a in arrays),
        in_specs=vmem_specs(n),
        out_specs=tuple(vmem_specs(n)),
        compiler_params=pltpu.CompilerParams(vmem_limit_bytes=VMEM_LIMIT),
        name="results",
    )(*arrays)


def vmem_specs(n):
    return [pl.BlockSpec(memory_space=pltpu.VMEM)] * n


def local(queries, key_rows, value_matrix, out_weight, cotangent):
    rows, heads, head = queries.shape
    scale = 1.0 / math.sqrt(head)
    unit = scale * math.log2(math.e)
    made = layer(
        unit,
        scale,
        key_rows.reshape(rows, head),
        value_matrix.reshape(rows, head),
        cotangent,
        queries.reshape(rows * heads, head),
        out_weight,
    )
    grad_queries, grad_keys, grad_values, output = results(*made)
    return (
        output,
        grad_queries.reshape(rows, heads, head),
        grad_keys.reshape(rows, 1, head),
        grad_values.reshape(rows, 1, head),
    )


def solution(mesh):
    return jax.shard_map(
        local,
        mesh=mesh,
        in_specs=(
            P("ctx", "head", None),
            P("ctx", "head", None),
            P("ctx", "head", None),
            P("head", None),
            P(("ctx", "head"), None),
        ),
        out_specs=(
            P(("ctx", "head"), None),
            P("ctx", "head", None),
            P("ctx", "head", None),
            P("ctx", "head", None),
        ),
        check_vma=False,
    )
```

```python
import functools
import math

import jax
import jax.numpy as jnp
from jax import lax
from jax.experimental import pallas as pl
from jax.experimental.pallas import tpu as pltpu
from jax.sharding import PartitionSpec as P

BF = jnp.bfloat16
F32 = jnp.float32
MESH = pl.DeviceIdType.MESH
YS, ZS, XS = 2, 4, 4
NCTX = YS * ZS * XS
HEAD = 128
GROUP = 8
BLOCK = 256
UNIT = 256
UNIT_POS = UNIT // GROUP
OWN = BLOCK * GROUP // UNIT
GIVE = 4
WORK = (OWN + GIVE) * UNIT
LOW = -1e30
VMEM_LIMIT = 60 * 1024 * 1024

NT = (((1,), (1,)), ((), ()))
NN = (((1,), (0,)), ((), ()))


def dot(a, b, dims):
    return lax.dot_general(a, b, dims, preferred_element_type=F32)


def share():
    c = lax.axis_index("ctx")
    low = jnp.minimum(c, NCTX - 1 - c)
    given = jnp.where(
        low <= 2, 4, jnp.where(low <= 8, 3, jnp.where(low <= 11, 2, jnp.where(low <= 14, 1, 0)))
    )
    return c, c < NCTX // 2, given


def place():
    c = lax.axis_index("ctx")
    return c // (ZS * XS), (c // XS) % ZS, c % XS


def ctx_of(y, z, x):
    return (y * ZS + z) * XS + x


def neighbours():
    y, z, x = place()
    xs = [ctx_of(y, z, (x + d) % XS) for d in (1, XS - 1)]
    zs = [ctx_of(y, (z + d) % ZS, x) for d in (1, ZS - 1)]
    return ctx_of(1 - y, z, x), xs, zs


def greet(ctx_list, head_list):
    barrier = pltpu.get_barrier_semaphore()
    for other in ctx_list:
        pl.semaphore_signal(barrier, inc=1, device_id={"ctx": other}, device_id_type=MESH)
    for other in head_list:
        pl.semaphore_signal(barrier, inc=1, device_id={"head": other}, device_id_type=MESH)
    pl.semaphore_wait(barrier, len(ctx_list) + len(head_list))


class Courier:
    def __init__(self, send, recv):
        self.send, self.recv, self.made = send, recv, {}

    def plan(self, name, axis, other, src, dst):
        n = len(self.made)
        self.made[name] = lambda: pltpu.make_async_remote_copy(
            src_ref=src,
            dst_ref=dst,
            send_sem=self.send.at[n],
            recv_sem=self.recv.at[n],
            device_id={axis: other},
            device_id_type=MESH,
        )

    def go(self, *names):
        for name in names:
            self.made[name]().start()

    def got(self, *names):
        for name in names:
            self.made[name]().wait_recv()

    def finish(self):
        for copy in self.made.values():
            copy().wait_send()


class Handover:
    def __init__(self, send, recv, src, src_unit, dst, dst_unit, from_low):
        c, is_low, given = share()
        self.given = given
        self.sends = is_low if from_low else jnp.logical_not(is_low)
        self.takes = jnp.logical_not(self.sends)

        def copy(i):
            return pltpu.make_async_remote_copy(
                src_ref=src.at[pl.ds((src_unit + i) * UNIT, UNIT)],
                dst_ref=dst.at[pl.ds((dst_unit + i) * UNIT, UNIT)],
                send_sem=send.at[i],
                recv_sem=recv.at[i],
                device_id={"ctx": NCTX - 1 - c},
                device_id_type=MESH,
            )

        self.copy = copy

    def each(self, who, act):
        for i in range(GIVE):

            @pl.when(jnp.logical_and(who, i < self.given))
            def _():
                act(i)

    def start(self):
        self.each(self.sends, lambda i: self.copy(i).start())

    def wait_recv(self):
        self.each(self.takes, lambda i: self.copy(i).wait_recv())

    def wait_send(self):
        self.each(self.sends, lambda i: self.copy(i).wait_send())


def tail_of(x):
    one = x.astype(BF).astype(F32)
    rest = x - one
    two = rest.astype(BF).astype(F32)
    three = rest - two
    lane = lax.broadcasted_iota(jnp.int32, x.shape, 1)
    return jnp.where(
        lane == 0, -one, jnp.where(lane == 1, -two, jnp.where(lane == 2, -three, 0.0))
    ).astype(BF)


def layer_kernel(
    unit, scale,
    k_ref, v_ref, cot_ref, q_ref, w_hbm,
    dq_ref, gk_ref, gv_ref, o_ref,
    w_ref, wsem, kv_ref, ca_ref, gt_ref, qw_ref, ga_ref, attn_ref, m_row, l_row, acc_ref,
    attn_far, dq_par, dq_far, af_ref, flat_ref, opart, ocore, osum, orow,
    qx_ref, gx_ref, kx_ref, vx_ref, xt_ref, dqs_ref, dk_ref, dv_ref,
    p_ref, t_ref, r_ref, m_ref, t2_ref, r2_ref, s_ref, y_ref,
    send, recv, hsend, hrecv,
):
    y, z, x = place()
    c, is_low, given = share()
    h = lax.axis_index("head")
    core, row = h ^ 1, h ^ 2
    mine, up = h % 2, h // 2
    partner, xs, zs = neighbours()
    w_copy = pltpu.make_async_copy(w_hbm, w_ref, wsem)
    w_copy.start()
    greet([partner] + xs + zs + [NCTX - 1 - c], [core, row])
    mail = Courier(send, recv)

    def hand(i, *what):
        return Handover(hsend.at[i], hrecv.at[i], *what)

    kv_ref[c, 0] = k_ref[...]
    kv_ref[c, 1] = v_ref[...]
    mail.plan("pair", "ctx", partner, kv_ref.at[c], kv_ref.at[c])
    mail.go("pair")
    qs = hand(0, q_ref, 0, qw_ref, OWN, False)
    gs = hand(1, ga_ref, 0, ga_ref, OWN, False)
    attn_home = hand(2, attn_ref, OWN, attn_far, 0, True)
    dq_home = hand(3, dq_par, 0, dq_far, 0, True)
    qs.start()
    ca_ref[h] = cot_ref[...]
    for name, o, i in (("cot row", row, h), ("cot core", core, h), ("cot relay", core, row)):
        mail.plan(name, "head", o, ca_ref.at[i], ca_ref.at[i])

    routes = ((z, x, zs, xs), (x, z, xs, zs))
    for n, (a, b, an, bn) in enumerate(routes):

        def slot(i, j, n=n):
            return kv_ref.at[jnp.where(n == 0, 16 + i * 4 + j, j * 4 + i)]

        for d in range(2):
            mail.plan((n, "beside", d), "ctx", an[d], slot(a, b), slot(a, b))
            part = slot((a + (3, 1)[d]) % 4, b).at[d]
            mail.plan((n, "on", d), "ctx", an[d], part, part)
            for s, off in enumerate((0, 3, 1, 2)):
                i = (a + off) % 4
                mail.plan((n, "third", s, d), "ctx", bn[d], slot(i, b), slot(i, b))
                part = slot(i, (b + (3, 1)[d]) % 4).at[d]
                mail.plan((n, "last", s, d), "ctx", bn[d], part, part)

    def pass_on(n, s):
        for d in range(2):
            mail.got((n, "third", s, d))
            mail.go((n, "last", s, d))

    for n, (a, an, b, bn) in enumerate(((x, xs, z, zs), (z, zs, x, xs))):
        steps = (
            (1, p_ref.at[n], a, an, t_ref.at[n], r_ref.at[n]),
            (2, m_ref.at[n], b, bn, t2_ref.at[n], r2_ref.at[n]),
        )
        for stage, piece, at, to, t, r in steps:
            for d in range(2):
                nxt = (at + (1, 3)[d]) % 4
                mail.plan((n, stage, "far", d), "ctx", to[d], piece.at[(at + 2) % 4, d], t.at[d])
                mail.plan(
                    (n, stage, "near", d), "ctx", to[d], piece.at[nxt, 1 - d], r.at[d, 1 - d]
                )
                mail.plan((n, stage, "sum", d), "ctx", to[d], t.at[d], r.at[d, d])
    mail.plan("y", "ctx", partner, s_ref.at[y], y_ref)
    for i in range(2):
        mail.plan(("core", i), "head", core, opart.at[2 * i + 1 - mine], ocore.at[i])
    mail.plan("row", "head", row, osum.at[1 - up], orow)

    def far(n, stage):
        mail.go((n, stage, "far", 0), (n, stage, "far", 1))

    def near(n, stage, d):
        mail.go((n, stage, "near", d))

    def relay(n, stage):
        piece, at, t = (
            (p_ref.at[n], (x, z)[n], t_ref.at[n])
            if stage == 1
            else (m_ref.at[n], (z, x)[n], t2_ref.at[n])
        )
        for d in range(2):
            nxt = (at + (1, 3)[d]) % 4
            mail.got((n, stage, "far", d))
            t[d] = (piece[nxt, d].astype(F32) + t[d].astype(F32)).astype(BF)
            mail.go((n, stage, "sum", d))

    def arrived(n, stage):
        for d in range(2):
            mail.got((n, stage, "near", d), (n, stage, "sum", d))

    def total_first(n):
        arrived(n, 1)
        at = (x, z)[n]
        for kv in range(2):
            for j in range(4):
                m_ref[n, j, kv] = (
                    p_ref[n, at, kv, j].astype(F32)
                    + r_ref[n, 0, kv, j].astype(F32)
                    + r_ref[n, 1, kv, j].astype(F32)
                ).astype(BF)
        far(n, 2)
        near(n, 2, 0)
        near(n, 2, 1)

    def total_second(n):
        arrived(n, 2)
        at = (z, x)[n]
        s_ref[n] = (
            m_ref[n, at].astype(F32) + r2_ref[n, 0].astype(F32) + r2_ref[n, 1].astype(F32)
        ).astype(BF)

    def output_projection():
        attn_home.wait_recv()
        own = OWN * UNIT
        af_ref[...] = attn_ref[pl.ds(0, own), :].astype(F32)

        def place_far(i):
            rows = pl.ds(i * UNIT, UNIT)
            af_ref[rows, :] = attn_far[rows, :].astype(F32)

        attn_home.each(attn_home.takes, place_far)
        for i in range(GROUP):
            flat_ref[:, i * HEAD : (i + 1) * HEAD] = af_ref[
                pl.ds(i, BLOCK, stride=GROUP), :
            ].astype(BF)
        wide = 1024

        def chunk(n, carry):
            cols = pl.ds(pl.multiple_of(n * wide, wide), wide)
            part = dot(flat_ref[...], w_ref[:, cols], NN).astype(BF)
            opart[:, :, cols] = part.reshape(4, BLOCK // 4, wide)
            return carry

        lax.fori_loop(0, w_ref.shape[1] // wide, chunk, 0)
        mail.go(("core", 0), ("core", 1))

    def output_core():
        for i in range(2):
            mail.got(("core", i))
            osum[i] = (opart[2 * i + mine].astype(F32) + ocore[i].astype(F32)).astype(BF)
        mail.go("row")

    begin = jnp.where(is_low, 0, given)
    taken = OWN + jnp.where(is_low, given, 0)

    def block_of(n, at, j):
        return jnp.where(n == 0, 16 + 4 * j + at, 4 * at + j)

    def over_group(n, at, tile, own_first, between):
        def row_set(turn, carry):
            mine_now = turn == (0 if own_first else 1)
            u0 = jnp.where(mine_now, begin, OWN)
            u1 = jnp.where(mine_now, OWN, taken)
            qb = jnp.where(mine_now, c, NCTX - 1 - c)
            pos0 = jnp.where(mine_now, 0, OWN)
            count = u1 - u0

            def key_pair(jp, carry):
                whole = qb > block_of(n, at, 2 * jp + 1)

                def rows(on, j, blocks, ahead):
                    def many(i, carry):
                        tile(u0 + 4 * i, (2, 2), j, blocks, ahead, u0 + 4 * i - pos0)
                        return carry

                    lax.fori_loop(0, jnp.where(on, count // 4, 0), many, 0)
                    rest = jnp.where(on, count % 4, 0)
                    for k, chains in ((3, (2, 1)), (2, (1, 1)), (1, (1,))):

                        @pl.when(rest == k)
                        def _():
                            tile(u1 - k, chains, j, blocks, ahead, u1 - k - pos0)

                rows(whole, 2 * jp, 2, None)

                def single_block(j, carry):
                    ahead = (qb - block_of(n, at, j)) * BLOCK
                    some = jnp.logical_and(jnp.logical_not(whole), ahead >= 0)
                    rows(some, j, 1, ahead)
                    return carry

                lax.fori_loop(2 * jp, 2 * jp + 2, single_block, 0)
                return carry

            lax.fori_loop(0, 2, key_pair, 0)

            @pl.when(turn == 0)
            def _():
                between()

            return carry

        lax.fori_loop(0, 2, row_set, 0)

    def rows_of(first, units):
        return pl.ds(pl.multiple_of(first * UNIT, UNIT), units * UNIT)

    def mask(keys, n, ahead):
        qpos = ahead + lax.broadcasted_iota(jnp.int32, (keys, n), 1) // GROUP
        return lax.broadcasted_iota(jnp.int32, (keys, n), 0) <= qpos

    def forward_group(s, carry):
        n = (1 - y + s) % 2
        i = s // 2
        off = jnp.where(i == 0, 0, jnp.where(i == 1, 3, jnp.where(i == 2, 1, 2)))
        at = (jnp.where(n == 0, x, z) + off) % 4

        @pl.when(s == 1)
        def _():
            each_pass(True, lambda n: (pass_on(n, 0), pass_on(n, 1)))

        @pl.when(s == 2)
        def _():
            each_pass(True, lambda n: (pass_on(n, 2), pass_on(n, 3)))
            each_pass(False, lambda n: (pass_on(n, 0), pass_on(n, 1)))

        @pl.when(s == 3)
        def _():
            each_pass(False, lambda n: (pass_on(n, 2), pass_on(n, 3)))

        @pl.when(s == 4)
        def _():
            mail.got("cot row")
            mail.go("cot relay")

        @pl.when(s == 5)
        def _():
            project_cotangent()

        def arrived_last(n):
            for step in range(4):
                mail.got((n, "last", step, 0), (n, "last", step, 1))

        @pl.when(s == 6)
        def _():
            each_pass(True, arrived_last)

        @pl.when(s == 7)
        def _():
            each_pass(False, arrived_last)

        for j in range(4):
            xt_ref[:, j * BLOCK : (j + 1) * BLOCK] = jnp.transpose(kv_ref[block_of(n, at, j), 1])

        def tile(first, chains, j, blocks, ahead, unit_at):
            held = [block_of(n, at, j + i) for i in range(blocks)]
            keys = jnp.concatenate([kv_ref[b, 0] for b in held], axis=0)
            values = xt_ref[:, pl.ds(pl.multiple_of(j * BLOCK, BLOCK), blocks * BLOCK)]
            offsets = [sum(chains[:i]) for i in range(len(chains))]
            sets = [rows_of(first + o, units) for o, units in zip(offsets, chains)]
            scores = [dot(keys, qw_ref[rows, :], NT) for rows in sets]
            for rows, o, sc in zip(sets, offsets, scores):
                if ahead is not None:
                    past = ahead + (unit_at + o) * UNIT_POS
                    sc = jnp.where(mask(sc.shape[0], sc.shape[1], past), sc, LOW)
                top = m_row[:, rows]
                new = jnp.maximum(top, jnp.max(sc, axis=0, keepdims=True))
                alpha = jnp.exp2((top - new) * unit)
                p = jnp.exp2((sc - new) * unit)
                m_row[:, rows] = new
                l_row[:, rows] = l_row[:, rows] * alpha + jnp.sum(p, axis=0, keepdims=True)
                acc_ref[:, rows] = acc_ref[:, rows] * alpha + dot(values, p.astype(BF), NN)

        def between():
            @pl.when(s == 0)
            def _():
                qs.wait_recv()

        over_group(n, at, tile, True, between)
        return carry

    def project_cotangent():
        mail.got("cot core", "cot relay")
        w_copy.wait()

        wide = 1024
        gt_ref[...] = jnp.zeros_like(gt_ref)

        def project(n, carry):
            cols = pl.ds(pl.multiple_of(n * wide, wide), wide)
            gt_ref[...] += dot(w_ref[:, cols], ca_ref[:, :, cols].reshape(BLOCK, wide), NT)
            return carry

        lax.fori_loop(0, w_ref.shape[1] // wide, project, 0)
        for i in range(GROUP):
            af_ref[pl.ds(i, BLOCK, stride=GROUP), :] = jnp.transpose(
                gt_ref[i * HEAD : (i + 1) * HEAD, :]
            )
        ga_ref[pl.ds(0, OWN * UNIT), :] = af_ref[...].astype(BF)
        gs.start()

    def each_pass(first, act):
        for n in range(2):

            @pl.when(y == (1 - n if first else n))
            def _():
                act(n)

    def start(n):
        mail.go((n, "beside", 0), (n, "beside", 1), (n, "third", 0, 0), (n, "third", 0, 1))

    def front(n):
        for d in range(2):
            mail.got((n, "beside", d))
            mail.go((n, "on", d), (n, "third", 1 + d, 0), (n, "third", 1 + d, 1))
        mail.got((n, "on", 0), (n, "on", 1))
        mail.go((n, "third", 3, 0), (n, "third", 3, 1))

    each_pass(True, start)
    mail.go("cot row", "cot core")
    qw_ref[pl.ds(0, OWN * UNIT), :] = q_ref[...]
    m_row[...] = jnp.full_like(m_row, LOW)
    l_row[...] = jnp.zeros_like(l_row)
    acc_ref[...] = jnp.zeros_like(acc_ref)
    mail.got("pair")
    each_pass(False, start)
    each_pass(True, front)
    each_pass(False, front)
    lax.fori_loop(0, 8, forward_group, 0)

    def finish_forward(i, carry):
        rows = pl.ds(pl.multiple_of(i * 512, 512), 512)
        l = l_row[:, rows]
        attn_ref[rows, :] = jnp.transpose(acc_ref[:, rows] / l).astype(BF)
        lse = m_row[:, rows] + jnp.log2(l) / unit
        one = lse.astype(BF).astype(F32)
        rest = lse - one
        two = rest.astype(BF).astype(F32)
        three = rest - two
        which = lax.broadcasted_iota(jnp.int32, (HEAD, 512), 0)
        pieces = jnp.where(
            which == 0, -one, jnp.where(which == 1, -two, jnp.where(which == 2, -three, 0.0))
        )
        qx_ref[rows, :HEAD] = qw_ref[rows, :]
        qx_ref[rows, HEAD:] = jnp.transpose(pieces).astype(BF)
        return carry

    lax.fori_loop(0, WORK // 512, finish_forward, 0)
    attn_home.start()
    gs.wait_recv()

    def prepare(i, carry):
        rows = pl.ds(pl.multiple_of(i * 512, 512), 512)
        ga = ga_ref[rows, :]
        delta = jnp.sum(ga.astype(F32) * attn_ref[rows, :].astype(F32), axis=1, keepdims=True)
        gx_ref[rows, :HEAD] = ga
        gx_ref[rows, HEAD:] = tail_of(jnp.broadcast_to(delta, (512, HEAD)))
        dqs_ref[:, rows] = jnp.zeros((HEAD, 512), F32)
        return carry

    lax.fori_loop(0, WORK // 512, prepare, 0)
    lane = lax.broadcasted_iota(jnp.int32, (4 * BLOCK, HEAD), 1)
    ones = jnp.where(lane < 3, 1.0, 0.0).astype(BF)
    kx_ref[:, HEAD:] = ones
    vx_ref[:, HEAD:] = ones

    def backward_group(s, carry):
        n = s % 2
        i = s // 2
        off = jnp.where(i == 0, 2, jnp.where(i == 1, 1, jnp.where(i == 2, 3, 0)))
        at = (jnp.where(n == 0, x, z) + off) % 4

        for j in range(4):
            ks = pl.ds(j * BLOCK, BLOCK)
            kx_ref[ks, :HEAD] = kv_ref[block_of(n, at, j), 0]
            vx_ref[ks, :HEAD] = kv_ref[block_of(n, at, j), 1]
            xt_ref[:, j * BLOCK : (j + 1) * BLOCK] = jnp.transpose(kv_ref[block_of(n, at, j), 0])
        dk_ref[...] = jnp.zeros_like(dk_ref)
        dv_ref[...] = jnp.zeros_like(dv_ref)

        def tile(first, chains, j, blocks, ahead, unit_at):
            ks = pl.ds(pl.multiple_of(j * BLOCK, BLOCK), blocks * BLOCK)
            offsets = [sum(chains[:i]) for i in range(len(chains))]
            sets = [rows_of(first + o, units) for o, units in zip(offsets, chains)]
            scores = [dot(kx_ref[ks, :], qx_ref[rows, :], NT) for rows in sets]
            grads = [dot(vx_ref[ks, :], gx_ref[rows, :], NT) for rows in sets]
            dv, dk = 0.0, 0.0
            for rows, o, sc, g in zip(sets, offsets, scores, grads):
                p = jnp.exp2(sc * unit)
                if ahead is not None:
                    past = ahead + (unit_at + o) * UNIT_POS
                    p = jnp.where(mask(p.shape[0], p.shape[1], past), p, 0.0)
                ds = (p * g).astype(BF)
                dv += dot(p.astype(BF), gx_ref[rows, :HEAD], NN)
                dk += dot(ds, qx_ref[rows, :HEAD], NN)
                dqs_ref[:, rows] += dot(xt_ref[:, ks], ds, NN)
            dv_ref[ks, :] += dv
            dk_ref[ks, :] += dk

        def between():
            @pl.when(s == 7)
            def _():
                dq_par[...] = jnp.transpose(
                    dqs_ref[:, pl.ds(OWN * UNIT, GIVE * UNIT)] * scale
                ).astype(BF)
                dq_home.start()
                relay(0, 2)

        over_group(n, at, tile, False, between)
        for j in range(4):
            ks = pl.ds(j * BLOCK, BLOCK)
            p_ref[n, at, 0, j] = (dk_ref[ks, :] * scale).astype(BF)
            p_ref[n, at, 1, j] = dv_ref[ks, :].astype(BF)

        @pl.when(s == 0)
        def _():
            far(0, 1)

        @pl.when(s == 1)
        def _():
            far(1, 1)

        @pl.when(s == 2)
        def _():
            near(0, 1, 0)
            output_projection()

        @pl.when(s == 3)
        def _():
            near(1, 1, 0)

        @pl.when(s == 4)
        def _():
            near(0, 1, 1)
            relay(0, 1)
            output_core()

        @pl.when(s == 5)
        def _():
            near(1, 1, 1)
            relay(1, 1)

        @pl.when(s == 6)
        def _():
            total_first(0)

        return carry

    lax.fori_loop(0, 8, backward_group, 0)
    total_first(1)
    dq_ref[...] = jnp.transpose(dqs_ref[:, pl.ds(0, OWN * UNIT)] * scale).astype(BF)
    relay(1, 2)
    total_second(0)

    @pl.when(y == 0)
    def _():
        mail.go("y")

    total_second(1)

    @pl.when(y == 1)
    def _():
        mail.go("y")

    mail.got("row")
    o_ref[...] = (osum[up].astype(F32) + orow[...].astype(F32)).astype(BF)
    dq_home.wait_recv()

    def place_dq(i):
        rows = pl.ds(i * UNIT, UNIT)
        dq_ref[rows, :] = dq_far[rows, :]

    dq_home.each(dq_home.takes, place_dq)
    mail.got("y")
    gk_ref[...] = (s_ref[1 - y, 0].astype(F32) + y_ref[0].astype(F32)).astype(BF)
    gv_ref[...] = (s_ref[1 - y, 1].astype(F32) + y_ref[1].astype(F32)).astype(BF)
    mail.finish()
    for hand in (qs, gs, attn_home, dq_home):
        hand.wait_send()


COPIES = 1 + 3 + 2 * 20 + 2 * 2 * 6 + 1 + 3


def layer(unit, scale, k, v, cot, q, w):
    vm, dma = pltpu.VMEM, pltpu.SemaphoreType.DMA
    part = (BLOCK // 4, w.shape[1])
    return pl.pallas_call(
        functools.partial(layer_kernel, unit, scale),
        out_shape=(
            jax.ShapeDtypeStruct((OWN * UNIT, HEAD), BF),
            jax.ShapeDtypeStruct((BLOCK, HEAD), BF),
            jax.ShapeDtypeStruct((BLOCK, HEAD), BF),
            jax.ShapeDtypeStruct(part, BF),
        ),
        in_specs=vmem_specs(4) + [pl.BlockSpec(memory_space=pl.ANY)],
        out_specs=tuple(vmem_specs(4)),
        scratch_shapes=[
            vm(w.shape, BF),
            dma,
            vm((NCTX, 2, BLOCK, HEAD), BF),
            vm((4,) + cot.shape, BF),
            vm((GROUP * HEAD, BLOCK), F32),
            vm((WORK, HEAD), BF),
            vm((WORK, HEAD), BF),
            vm((WORK, HEAD), BF),
            vm((1, WORK), F32),
            vm((1, WORK), F32),
            vm((HEAD, WORK), F32),
            vm((GIVE * UNIT, HEAD), BF),
            vm((GIVE * UNIT, HEAD), BF),
            vm((GIVE * UNIT, HEAD), BF),
            vm((OWN * UNIT, HEAD), F32),
            vm((BLOCK, GROUP * HEAD), BF),
            vm((4,) + part, BF),
            vm((2,) + part, BF),
            vm((2,) + part, BF),
            vm(part, BF),
            vm((WORK, 2 * HEAD), BF),
            vm((WORK, 2 * HEAD), BF),
            vm((4 * BLOCK, 2 * HEAD), BF),
            vm((4 * BLOCK, 2 * HEAD), BF),
            vm((HEAD, 4 * BLOCK), BF),
            vm((HEAD, WORK), F32),
            vm((4 * BLOCK, HEAD), F32),
            vm((4 * BLOCK, HEAD), F32),
            vm((2, 4, 2, 4, BLOCK, HEAD), BF),
            vm((2, 2, 4, BLOCK, HEAD), BF),
            vm((2, 2, 2, 4, BLOCK, HEAD), BF),
            vm((2, 4, 2, BLOCK, HEAD), BF),
            vm((2, 2, BLOCK, HEAD), BF),
            vm((2, 2, 2, BLOCK, HEAD), BF),
            vm((2, 2, BLOCK, HEAD), BF),
            vm((2, BLOCK, HEAD), BF),
            dma((COPIES,)),
            dma((COPIES,)),
            dma((4, GIVE)),
            dma((4, GIVE)),
        ],
        compiler_params=pltpu.CompilerParams(
            collective_id=0, has_side_effects=True, vmem_limit_bytes=VMEM_LIMIT
        ),
        name="layer",
    )(k, v, cot, q, w)


def results_kernel(*refs):
    n = len(refs) // 2
    for i in range(n):
        refs[n + i][...] = refs[i][...]


def results(*arrays):
    n = len(arrays)
    return pl.pallas_call(
        results_kernel,
        out_shape=tuple(jax.ShapeDtypeStruct(a.shape, a.dtype) for a in arrays),
        in_specs=vmem_specs(n),
        out_specs=tuple(vmem_specs(n)),
        compiler_params=pltpu.CompilerParams(vmem_limit_bytes=VMEM_LIMIT),
        name="results",
    )(*arrays)


def vmem_specs(n):
    return [pl.BlockSpec(memory_space=pltpu.VMEM)] * n


def local(queries, key_rows, value_matrix, out_weight, cotangent):
    rows, heads, head = queries.shape
    scale = 1.0 / math.sqrt(head)
    unit = scale * math.log2(math.e)
    made = layer(
        unit,
        scale,
        key_rows.reshape(rows, head),
        value_matrix.reshape(rows, head),
        cotangent,
        queries.reshape(rows * heads, head),
        out_weight,
    )
    grad_queries, grad_keys, grad_values, output = results(*made)
    return (
        output,
        grad_queries.reshape(rows, heads, head),
        grad_keys.reshape(rows, 1, head),
        grad_values.reshape(rows, 1, head),
    )


def solution(mesh):
    return jax.shard_map(
        local,
        mesh=mesh,
        in_specs=(
            P("ctx", "head", None),
            P("ctx", "head", None),
            P("ctx", "head", None),
            P("head", None),
            P(("ctx", "head"), None),
        ),
        out_specs=(
            P(("ctx", "head"), None),
            P("ctx", "head", None),
            P("ctx", "head", None),
            P("ctx", "head", None),
        ),
        check_vma=False,
    )
```

```python
import functools
import math

import jax
import jax.numpy as jnp
from jax import lax
from jax.experimental import pallas as pl
from jax.experimental.pallas import tpu as pltpu
from jax.sharding import PartitionSpec as P

BF = jnp.bfloat16
F32 = jnp.float32
MESH = pl.DeviceIdType.MESH
YS, ZS, XS = 2, 4, 4
NCTX = YS * ZS * XS
HEAD = 128
GROUP = 8
BLOCK = 256
UNIT = 256
UNIT_POS = UNIT // GROUP
OWN = BLOCK * GROUP // UNIT
GIVE = 4
WORK = (OWN + GIVE) * UNIT
LOW = -1e30
VMEM_LIMIT = 60 * 1024 * 1024

NT = (((1,), (1,)), ((), ()))
NN = (((1,), (0,)), ((), ()))


def dot(a, b, dims):
    return lax.dot_general(a, b, dims, preferred_element_type=F32)


def share():
    c = lax.axis_index("ctx")
    low = jnp.minimum(c, NCTX - 1 - c)
    given = jnp.where(
        low <= 2, 4, jnp.where(low <= 8, 3, jnp.where(low <= 11, 2, jnp.where(low <= 14, 1, 0)))
    )
    return c, c < NCTX // 2, given


def place():
    c = lax.axis_index("ctx")
    return c // (ZS * XS), (c // XS) % ZS, c % XS


def ctx_of(y, z, x):
    return (y * ZS + z) * XS + x


def neighbours():
    y, z, x = place()
    xs = [ctx_of(y, z, (x + d) % XS) for d in (1, XS - 1)]
    zs = [ctx_of(y, (z + d) % ZS, x) for d in (1, ZS - 1)]
    return ctx_of(1 - y, z, x), xs, zs


def greet(ctx_list, head_list):
    barrier = pltpu.get_barrier_semaphore()
    for other in ctx_list:
        pl.semaphore_signal(barrier, inc=1, device_id={"ctx": other}, device_id_type=MESH)
    for other in head_list:
        pl.semaphore_signal(barrier, inc=1, device_id={"head": other}, device_id_type=MESH)
    pl.semaphore_wait(barrier, len(ctx_list) + len(head_list))


class Courier:
    def __init__(self, send, recv):
        self.send, self.recv, self.made = send, recv, {}

    def plan(self, name, axis, other, src, dst):
        n = len(self.made)
        self.made[name] = lambda: pltpu.make_async_remote_copy(
            src_ref=src,
            dst_ref=dst,
            send_sem=self.send.at[n],
            recv_sem=self.recv.at[n],
            device_id={axis: other},
            device_id_type=MESH,
        )

    def go(self, *names):
        for name in names:
            self.made[name]().start()

    def got(self, *names):
        for name in names:
            self.made[name]().wait_recv()

    def finish(self):
        for copy in self.made.values():
            copy().wait_send()


class Handover:
    def __init__(self, send, recv, src, src_unit, dst, dst_unit, from_low):
        c, is_low, given = share()
        self.given = given
        self.sends = is_low if from_low else jnp.logical_not(is_low)
        self.takes = jnp.logical_not(self.sends)

        def copy(i):
            return pltpu.make_async_remote_copy(
                src_ref=src.at[pl.ds((src_unit + i) * UNIT, UNIT)],
                dst_ref=dst.at[pl.ds((dst_unit + i) * UNIT, UNIT)],
                send_sem=send.at[i],
                recv_sem=recv.at[i],
                device_id={"ctx": NCTX - 1 - c},
                device_id_type=MESH,
            )

        self.copy = copy

    def each(self, who, act):
        for i in range(GIVE):

            @pl.when(jnp.logical_and(who, i < self.given))
            def _():
                act(i)

    def start(self):
        self.each(self.sends, lambda i: self.copy(i).start())

    def wait_recv(self):
        self.each(self.takes, lambda i: self.copy(i).wait_recv())

    def wait_send(self):
        self.each(self.sends, lambda i: self.copy(i).wait_send())


def tail_of(x):
    one = x.astype(BF).astype(F32)
    rest = x - one
    two = rest.astype(BF).astype(F32)
    three = rest - two
    lane = lax.broadcasted_iota(jnp.int32, x.shape, 1)
    return jnp.where(
        lane == 0, -one, jnp.where(lane == 1, -two, jnp.where(lane == 2, -three, 0.0))
    ).astype(BF)


def layer_kernel(
    unit, scale,
    k_ref, v_ref, cot_ref, q_ref, w_hbm,
    dq_ref, gk_ref, gv_ref, o_ref,
    w_ref, wsem, kv_ref, ca_ref, qw_ref, ga_ref, attn_ref, m_row, l_row, acc_ref,
    attn_far, dq_par, dq_far, af_ref, flat_ref, opart, ocore, osum, orow,
    qx_ref, gx_ref, kx_ref, vx_ref, xt_ref, dqs_ref, dk_ref, dv_ref,
    p_ref, t_ref, r_ref, m_ref, t2_ref, r2_ref, s_ref, y_ref,
    send, recv, hsend, hrecv,
):
    y, z, x = place()
    c, is_low, given = share()
    h = lax.axis_index("head")
    core, row = h ^ 1, h ^ 2
    mine, up = h % 2, h // 2
    partner, xs, zs = neighbours()
    w_copy = pltpu.make_async_copy(w_hbm, w_ref, wsem)
    w_copy.start()
    greet([partner] + xs + zs + [NCTX - 1 - c], [core, row])
    mail = Courier(send, recv)

    def hand(i, *what):
        return Handover(hsend.at[i], hrecv.at[i], *what)

    kv_ref[c, 0] = k_ref[...]
    kv_ref[c, 1] = v_ref[...]
    mail.plan("pair", "ctx", partner, kv_ref.at[c], kv_ref.at[c])
    mail.go("pair")
    qs = hand(0, q_ref, 0, qw_ref, OWN, False)
    gs = hand(1, ga_ref, 0, ga_ref, OWN, False)
    attn_home = hand(2, attn_ref, OWN, attn_far, 0, True)
    dq_home = hand(3, dq_par, 0, dq_far, 0, True)
    qs.start()
    ca_ref[h] = cot_ref[...]
    for name, o, i in (("cot row", row, h), ("cot core", core, h), ("cot relay", core, row)):
        mail.plan(name, "head", o, ca_ref.at[i], ca_ref.at[i])
    mail.go("cot row", "cot core")

    routes = ((z, x, zs, xs), (x, z, xs, zs))
    for n, (a, b, an, bn) in enumerate(routes):

        def slot(i, j, n=n):
            return kv_ref.at[jnp.where(n == 0, 16 + i * 4 + j, j * 4 + i)]

        for d in range(2):
            mail.plan((n, "beside", d), "ctx", an[d], slot(a, b), slot(a, b))
            part = slot((a + (3, 1)[d]) % 4, b).at[d]
            mail.plan((n, "on", d), "ctx", an[d], part, part)
            for s, off in enumerate((0, 3, 1, 2)):
                i = (a + off) % 4
                mail.plan((n, "third", s, d), "ctx", bn[d], slot(i, b), slot(i, b))
                part = slot(i, (b + (3, 1)[d]) % 4).at[d]
                mail.plan((n, "last", s, d), "ctx", bn[d], part, part)

    def pass_on(n, s):
        for d in range(2):
            mail.got((n, "third", s, d))
            mail.go((n, "last", s, d))

    for n, (a, an, b, bn) in enumerate(((x, xs, z, zs), (z, zs, x, xs))):
        steps = (
            (1, p_ref.at[n], a, an, t_ref.at[n], r_ref.at[n]),
            (2, m_ref.at[n], b, bn, t2_ref.at[n], r2_ref.at[n]),
        )
        for stage, piece, at, to, t, r in steps:
            for d in range(2):
                nxt = (at + (1, 3)[d]) % 4
                mail.plan((n, stage, "far", d), "ctx", to[d], piece.at[(at + 2) % 4, d], t.at[d])
                mail.plan(
                    (n, stage, "near", d), "ctx", to[d], piece.at[nxt, 1 - d], r.at[d, 1 - d]
                )
                mail.plan((n, stage, "sum", d), "ctx", to[d], t.at[d], r.at[d, d])
    mail.plan("y", "ctx", partner, s_ref.at[y], y_ref)
    for i in range(2):
        mail.plan(("core", i), "head", core, opart.at[2 * i + 1 - mine], ocore.at[i])
    mail.plan("row", "head", row, osum.at[1 - up], orow)

    def far(n, stage):
        mail.go((n, stage, "far", 0), (n, stage, "far", 1))

    def near(n, stage, d):
        mail.go((n, stage, "near", d))

    def relay(n, stage):
        piece, at, t = (
            (p_ref.at[n], (x, z)[n], t_ref.at[n])
            if stage == 1
            else (m_ref.at[n], (z, x)[n], t2_ref.at[n])
        )
        for d in range(2):
            nxt = (at + (1, 3)[d]) % 4
            mail.got((n, stage, "far", d))
            t[d] = (piece[nxt, d].astype(F32) + t[d].astype(F32)).astype(BF)
            mail.go((n, stage, "sum", d))

    def arrived(n, stage):
        for d in range(2):
            mail.got((n, stage, "near", d), (n, stage, "sum", d))

    def total_first(n):
        arrived(n, 1)
        at = (x, z)[n]
        for kv in range(2):
            for j in range(4):
                m_ref[n, j, kv] = (
                    p_ref[n, at, kv, j].astype(F32)
                    + r_ref[n, 0, kv, j].astype(F32)
                    + r_ref[n, 1, kv, j].astype(F32)
                ).astype(BF)
        far(n, 2)
        near(n, 2, 0)
        near(n, 2, 1)

    def total_second(n):
        arrived(n, 2)
        at = (z, x)[n]
        s_ref[n] = (
            m_ref[n, at].astype(F32) + r2_ref[n, 0].astype(F32) + r2_ref[n, 1].astype(F32)
        ).astype(BF)

    def output_projection():
        attn_home.wait_recv()
        own = OWN * UNIT
        af_ref[...] = attn_ref[pl.ds(0, own), :].astype(F32)

        def place_far(i):
            rows = pl.ds(i * UNIT, UNIT)
            af_ref[rows, :] = attn_far[rows, :].astype(F32)

        attn_home.each(attn_home.takes, place_far)
        for i in range(GROUP):
            flat_ref[:, i * HEAD : (i + 1) * HEAD] = af_ref[
                pl.ds(i, BLOCK, stride=GROUP), :
            ].astype(BF)
        wide = 512

        def chunk(n, carry):
            cols = pl.ds(pl.multiple_of(n * wide, wide), wide)
            part = dot(flat_ref[...], w_ref[:, cols], NN).astype(BF)
            opart[:, :, cols] = part.reshape(4, BLOCK // 4, wide)
            return carry

        lax.fori_loop(0, w_ref.shape[1] // wide, chunk, 0)
        mail.go(("core", 0), ("core", 1))

    def output_core():
        for i in range(2):
            mail.got(("core", i))
            osum[i] = (opart[2 * i + mine].astype(F32) + ocore[i].astype(F32)).astype(BF)
        mail.go("row")

    begin = jnp.where(is_low, 0, given)
    taken = OWN + jnp.where(is_low, given, 0)

    def block_of(n, at, j):
        return jnp.where(n == 0, 16 + 4 * j + at, 4 * at + j)

    def over_group(n, at, tile, between=None):
        def row_set(own, carry):
            mine_now = own == 1
            u0 = jnp.where(mine_now, begin, OWN)
            u1 = jnp.where(mine_now, OWN, taken)
            qb = jnp.where(mine_now, c, NCTX - 1 - c)
            pos0 = jnp.where(mine_now, 0, OWN)
            twos = (u1 - u0) // 2
            odd = (u1 - u0) % 2

            def key_pair(jp, carry):
                whole = qb > block_of(n, at, 2 * jp + 1)

                def full(i, carry):
                    tile(u0 + 2 * i, 2, 2 * jp, 2, None)
                    return carry

                lax.fori_loop(0, jnp.where(whole, twos, 0), full, 0)

                @pl.when(jnp.logical_and(whole, odd == 1))
                def _():
                    tile(u1 - 1, 1, 2 * jp, 2, None)

                def single_block(j, carry):
                    ahead = (qb - block_of(n, at, j)) * BLOCK
                    some = jnp.logical_and(jnp.logical_not(whole), ahead >= 0)

                    def part(i, carry):
                        u = u0 + 2 * i
                        tile(u, 2, j, 1, ahead + (u - pos0) * UNIT_POS)
                        return carry

                    lax.fori_loop(0, jnp.where(some, twos, 0), part, 0)

                    @pl.when(jnp.logical_and(some, odd == 1))
                    def _():
                        u = u1 - 1
                        tile(u, 1, j, 1, ahead + (u - pos0) * UNIT_POS)

                    return carry

                lax.fori_loop(2 * jp, 2 * jp + 2, single_block, 0)
                return carry

            lax.fori_loop(0, 2, key_pair, 0)
            if between is not None:
                between(own)
            return carry

        lax.fori_loop(0, 2, row_set, 0)

    def rows_of(first, units):
        return pl.ds(pl.multiple_of(first * UNIT, UNIT), units * UNIT)

    def mask(keys, n, ahead):
        qpos = ahead + lax.broadcasted_iota(jnp.int32, (keys, n), 1) // GROUP
        return lax.broadcasted_iota(jnp.int32, (keys, n), 0) <= qpos

    def forward_group(s, carry):
        n = 1 - s % 2
        i = s // 2
        off = jnp.where(i == 0, 0, jnp.where(i == 1, 3, jnp.where(i == 2, 1, 2)))
        at = (jnp.where(n == 0, x, z) + off) % 4

        @pl.when(s == 1)
        def _():
            for step in range(2):
                pass_on(1, step)
                pass_on(0, step)

        @pl.when(s == 2)
        def _():
            pass_on(1, 2)
            pass_on(1, 3)

        @pl.when(s == 3)
        def _():
            pass_on(0, 2)
            pass_on(0, 3)

        @pl.when(s == 4)
        def _():
            mail.got("cot row")
            mail.go("cot relay")

        @pl.when(s == 5)
        def _():
            project_cotangent()

        for n_now in range(2):

            @pl.when(s == 7 - n_now)
            def _():
                for step in range(4):
                    mail.got((n_now, "last", step, 0), (n_now, "last", step, 1))

        for j in range(4):
            xt_ref[:, j * BLOCK : (j + 1) * BLOCK] = jnp.transpose(kv_ref[block_of(n, at, j), 1])

        def tile(first, units, j, blocks, ahead):
            rows = rows_of(first, units)
            held = [block_of(n, at, j + i) for i in range(blocks)]
            keys = jnp.concatenate([kv_ref[b, 0] for b in held], axis=0)
            values = xt_ref[:, pl.ds(pl.multiple_of(j * BLOCK, BLOCK), blocks * BLOCK)]
            sc = dot(keys, qw_ref[rows, :], NT)
            if ahead is not None:
                sc = jnp.where(mask(sc.shape[0], sc.shape[1], ahead), sc, LOW)
            top = m_row[:, rows]
            new = jnp.maximum(top, jnp.max(sc, axis=0, keepdims=True))
            alpha = jnp.exp2((top - new) * unit)
            p = jnp.exp2((sc - new) * unit)
            m_row[:, rows] = new
            l_row[:, rows] = l_row[:, rows] * alpha + jnp.sum(p, axis=0, keepdims=True)
            acc_ref[:, rows] = acc_ref[:, rows] * alpha + dot(values, p.astype(BF), NN)

        over_group(n, at, tile)
        return carry

    def project_cotangent():
        mail.got("cot core", "cot relay")
        w_copy.wait()

        def project(n, carry):
            wide = 1024
            total = jnp.zeros((BLOCK, 2 * HEAD), F32)
            for i in range(cot_ref.shape[1] // wide):
                cols = pl.ds(i * wide, wide)
                total += dot(
                    ca_ref[:, :, cols].reshape(BLOCK, wide),
                    w_ref[pl.ds(pl.multiple_of(n * 2 * HEAD, 2 * HEAD), 2 * HEAD), cols],
                    NT,
                )
            for i in range(2):
                af_ref[pl.ds(2 * n + i, BLOCK, stride=GROUP), :] = total[
                    :, i * HEAD : (i + 1) * HEAD
                ]
            return carry

        lax.fori_loop(0, GROUP // 2, project, 0)
        ga_ref[pl.ds(0, OWN * UNIT), :] = af_ref[...].astype(BF)
        gs.start()

    qw_ref[pl.ds(0, OWN * UNIT), :] = q_ref[...]
    m_row[...] = jnp.full_like(m_row, LOW)
    l_row[...] = jnp.zeros_like(l_row)
    acc_ref[...] = jnp.zeros_like(acc_ref)
    mail.got("pair")
    for n in range(2):
        mail.go((n, "beside", 0), (n, "beside", 1), (n, "third", 0, 0), (n, "third", 0, 1))
    for n in range(2):
        for d in range(2):
            mail.got((n, "beside", d))
            mail.go((n, "on", d), (n, "third", 1 + d, 0), (n, "third", 1 + d, 1))
    for n in range(2):
        mail.got((n, "on", 0), (n, "on", 1))
        mail.go((n, "third", 3, 0), (n, "third", 3, 1))
    qs.wait_recv()
    lax.fori_loop(0, 8, forward_group, 0)

    def finish_forward(i, carry):
        rows = pl.ds(pl.multiple_of(i * 512, 512), 512)
        l = l_row[:, rows]
        attn_ref[rows, :] = jnp.transpose(acc_ref[:, rows] / l).astype(BF)
        lse = m_row[:, rows] + jnp.log2(l) / unit
        one = lse.astype(BF).astype(F32)
        rest = lse - one
        two = rest.astype(BF).astype(F32)
        three = rest - two
        which = lax.broadcasted_iota(jnp.int32, (HEAD, 512), 0)
        pieces = jnp.where(
            which == 0, -one, jnp.where(which == 1, -two, jnp.where(which == 2, -three, 0.0))
        )
        qx_ref[rows, :HEAD] = qw_ref[rows, :]
        qx_ref[rows, HEAD:] = jnp.transpose(pieces).astype(BF)
        return carry

    lax.fori_loop(0, WORK // 512, finish_forward, 0)
    attn_home.start()
    gs.wait_recv()

    def prepare(i, carry):
        rows = pl.ds(pl.multiple_of(i * 512, 512), 512)
        ga = ga_ref[rows, :]
        delta = jnp.sum(ga.astype(F32) * attn_ref[rows, :].astype(F32), axis=1, keepdims=True)
        gx_ref[rows, :HEAD] = ga
        gx_ref[rows, HEAD:] = tail_of(jnp.broadcast_to(delta, (512, HEAD)))
        dqs_ref[:, rows] = jnp.zeros((HEAD, 512), F32)
        return carry

    lax.fori_loop(0, WORK // 512, prepare, 0)
    lane = lax.broadcasted_iota(jnp.int32, (4 * BLOCK, HEAD), 1)
    ones = jnp.where(lane < 3, 1.0, 0.0).astype(BF)
    kx_ref[:, HEAD:] = ones
    vx_ref[:, HEAD:] = ones

    def backward_group(s, carry):
        n = s % 2
        i = s // 2
        off = jnp.where(i == 0, 2, jnp.where(i == 1, 1, jnp.where(i == 2, 3, 0)))
        at = (jnp.where(n == 0, x, z) + off) % 4

        for j in range(4):
            ks = pl.ds(j * BLOCK, BLOCK)
            kx_ref[ks, :HEAD] = kv_ref[block_of(n, at, j), 0]
            vx_ref[ks, :HEAD] = kv_ref[block_of(n, at, j), 1]
            xt_ref[:, j * BLOCK : (j + 1) * BLOCK] = jnp.transpose(kv_ref[block_of(n, at, j), 0])
        dk_ref[...] = jnp.zeros_like(dk_ref)
        dv_ref[...] = jnp.zeros_like(dv_ref)

        def tile(first, units, j, blocks, ahead):
            rows = rows_of(first, units)
            ks = pl.ds(pl.multiple_of(j * BLOCK, BLOCK), blocks * BLOCK)
            p = jnp.exp2(dot(kx_ref[ks, :], qx_ref[rows, :], NT) * unit)
            if ahead is not None:
                p = jnp.where(mask(p.shape[0], p.shape[1], ahead), p, 0.0)
            g = dot(vx_ref[ks, :], gx_ref[rows, :], NT)
            ds = (p * g).astype(BF)
            dv_ref[ks, :] += dot(p.astype(BF), gx_ref[rows, :HEAD], NN)
            dk_ref[ks, :] += dot(ds, qx_ref[rows, :HEAD], NN)
            dqs_ref[:, rows] += dot(xt_ref[:, ks], ds, NN)

        def between(own):
            @pl.when(jnp.logical_and(s == 7, own == 0))
            def _():
                dq_par[...] = jnp.transpose(
                    dqs_ref[:, pl.ds(OWN * UNIT, GIVE * UNIT)] * scale
                ).astype(BF)
                dq_home.start()

        over_group(n, at, tile, between)
        for j in range(4):
            ks = pl.ds(j * BLOCK, BLOCK)
            p_ref[n, at, 0, j] = (dk_ref[ks, :] * scale).astype(BF)
            p_ref[n, at, 1, j] = dv_ref[ks, :].astype(BF)

        @pl.when(s == 0)
        def _():
            far(0, 1)

        @pl.when(s == 1)
        def _():
            far(1, 1)

        @pl.when(s == 2)
        def _():
            near(0, 1, 0)
            output_projection()

        @pl.when(s == 3)
        def _():
            near(1, 1, 0)

        @pl.when(s == 4)
        def _():
            near(0, 1, 1)
            relay(0, 1)
            output_core()

        @pl.when(s == 5)
        def _():
            near(1, 1, 1)
            relay(1, 1)

        @pl.when(s == 6)
        def _():
            total_first(0)

        return carry

    lax.fori_loop(0, 8, backward_group, 0)
    total_first(1)
    relay(0, 2)
    dq_ref[...] = jnp.transpose(dqs_ref[:, pl.ds(0, OWN * UNIT)] * scale).astype(BF)
    relay(1, 2)
    total_second(0)

    @pl.when(y == 0)
    def _():
        mail.go("y")

    total_second(1)

    @pl.when(y == 1)
    def _():
        mail.go("y")

    mail.got("row")
    o_ref[...] = (osum[up].astype(F32) + orow[...].astype(F32)).astype(BF)
    dq_home.wait_recv()

    def place_dq(i):
        rows = pl.ds(i * UNIT, UNIT)
        dq_ref[rows, :] = dq_far[rows, :]

    dq_home.each(dq_home.takes, place_dq)
    mail.got("y")
    gk_ref[...] = (s_ref[1 - y, 0].astype(F32) + y_ref[0].astype(F32)).astype(BF)
    gv_ref[...] = (s_ref[1 - y, 1].astype(F32) + y_ref[1].astype(F32)).astype(BF)
    mail.finish()
    for hand in (qs, gs, attn_home, dq_home):
        hand.wait_send()


COPIES = 1 + 3 + 2 * 20 + 2 * 2 * 6 + 1 + 3


def layer(unit, scale, k, v, cot, q, w):
    vm, dma = pltpu.VMEM, pltpu.SemaphoreType.DMA
    part = (BLOCK // 4, w.shape[1])
    return pl.pallas_call(
        functools.partial(layer_kernel, unit, scale),
        out_shape=(
            jax.ShapeDtypeStruct((OWN * UNIT, HEAD), BF),
            jax.ShapeDtypeStruct((BLOCK, HEAD), BF),
            jax.ShapeDtypeStruct((BLOCK, HEAD), BF),
            jax.ShapeDtypeStruct(part, BF),
        ),
        in_specs=vmem_specs(4) + [pl.BlockSpec(memory_space=pl.ANY)],
        out_specs=tuple(vmem_specs(4)),
        scratch_shapes=[
            vm(w.shape, BF),
            dma,
            vm((NCTX, 2, BLOCK, HEAD), BF),
            vm((4,) + cot.shape, BF),
            vm((WORK, HEAD), BF),
            vm((WORK, HEAD), BF),
            vm((WORK, HEAD), BF),
            vm((1, WORK), F32),
            vm((1, WORK), F32),
            vm((HEAD, WORK), F32),
            vm((GIVE * UNIT, HEAD), BF),
            vm((GIVE * UNIT, HEAD), BF),
            vm((GIVE * UNIT, HEAD), BF),
            vm((OWN * UNIT, HEAD), F32),
            vm((BLOCK, GROUP * HEAD), BF),
            vm((4,) + part, BF),
            vm((2,) + part, BF),
            vm((2,) + part, BF),
            vm(part, BF),
            vm((WORK, 2 * HEAD), BF),
            vm((WORK, 2 * HEAD), BF),
            vm((4 * BLOCK, 2 * HEAD), BF),
            vm((4 * BLOCK, 2 * HEAD), BF),
            vm((HEAD, 4 * BLOCK), BF),
            vm((HEAD, WORK), F32),
            vm((4 * BLOCK, HEAD), F32),
            vm((4 * BLOCK, HEAD), F32),
            vm((2, 4, 2, 4, BLOCK, HEAD), BF),
            vm((2, 2, 4, BLOCK, HEAD), BF),
            vm((2, 2, 2, 4, BLOCK, HEAD), BF),
            vm((2, 4, 2, BLOCK, HEAD), BF),
            vm((2, 2, BLOCK, HEAD), BF),
            vm((2, 2, 2, BLOCK, HEAD), BF),
            vm((2, 2, BLOCK, HEAD), BF),
            vm((2, BLOCK, HEAD), BF),
            dma((COPIES,)),
            dma((COPIES,)),
            dma((4, GIVE)),
            dma((4, GIVE)),
        ],
        compiler_params=pltpu.CompilerParams(
            collective_id=0, has_side_effects=True, vmem_limit_bytes=VMEM_LIMIT
        ),
        name="layer",
    )(k, v, cot, q, w)


def results_kernel(*refs):
    n = len(refs) // 2
    for i in range(n):
        refs[n + i][...] = refs[i][...]


def results(*arrays):
    n = len(arrays)
    return pl.pallas_call(
        results_kernel,
        out_shape=tuple(jax.ShapeDtypeStruct(a.shape, a.dtype) for a in arrays),
        in_specs=vmem_specs(n),
        out_specs=tuple(vmem_specs(n)),
        compiler_params=pltpu.CompilerParams(vmem_limit_bytes=VMEM_LIMIT),
        name="results",
    )(*arrays)


def vmem_specs(n):
    return [pl.BlockSpec(memory_space=pltpu.VMEM)] * n


def local(queries, key_rows, value_matrix, out_weight, cotangent):
    rows, heads, head = queries.shape
    scale = 1.0 / math.sqrt(head)
    unit = scale * math.log2(math.e)
    made = layer(
        unit,
        scale,
        key_rows.reshape(rows, head),
        value_matrix.reshape(rows, head),
        cotangent,
        queries.reshape(rows * heads, head),
        out_weight,
    )
    grad_queries, grad_keys, grad_values, output = results(*made)
    return (
        output,
        grad_queries.reshape(rows, heads, head),
        grad_keys.reshape(rows, 1, head),
        grad_values.reshape(rows, 1, head),
    )


def solution(mesh):
    return jax.shard_map(
        local,
        mesh=mesh,
        in_specs=(
            P("ctx", "head", None),
            P("ctx", "head", None),
            P("ctx", "head", None),
            P("head", None),
            P(("ctx", "head"), None),
        ),
        out_specs=(
            P(("ctx", "head"), None),
            P("ctx", "head", None),
            P("ctx", "head", None),
            P("ctx", "head", None),
        ),
        check_vma=False,
    )
```

```python
import functools
import math

import jax
import jax.numpy as jnp
from jax import lax
from jax.experimental import pallas as pl
from jax.experimental.pallas import tpu as pltpu
from jax.sharding import PartitionSpec as P

BF = jnp.bfloat16
F32 = jnp.float32
MESH = pl.DeviceIdType.MESH
YS, ZS, XS = 2, 4, 4
NCTX = YS * ZS * XS
HEAD = 128
GROUP = 8
BLOCK = 256
UNIT = 256
UNIT_POS = UNIT // GROUP
OWN = BLOCK * GROUP // UNIT
GIVE = 4
WORK = (OWN + GIVE) * UNIT
LOW = -1e30
WIDE = 1024
SLOTS = 146
VMEM_LIMIT = 60 * 1024 * 1024

NT = (((1,), (1,)), ((), ()))
NN = (((1,), (0,)), ((), ()))
TN = (((0,), (0,)), ((), ()))


def dot(a, b, dims):
    return lax.dot_general(a, b, dims, preferred_element_type=F32)


def share():
    c = lax.axis_index("ctx")
    low = jnp.minimum(c, NCTX - 1 - c)
    given = jnp.where(
        low <= 2, 4, jnp.where(low <= 7, 3, jnp.where(low <= 11, 2, jnp.where(low <= 14, 1, 0)))
    )
    return c, c < NCTX // 2, given


def place():
    c = lax.axis_index("ctx")
    return c // (ZS * XS), (c // XS) % ZS, c % XS


def ctx_of(y, z, x):
    return (y * ZS + z) * XS + x


def turned_back(own, i):
    return (own + jnp.where(i == 0, 0, jnp.where(i == 1, 1, jnp.where(i == 2, 3, 2)))) % 4


def turned(own, i):
    return (own + jnp.where(i == 0, 2, jnp.where(i == 1, 1, jnp.where(i == 2, 3, 0)))) % 4


def neighbours():
    y, z, x = place()
    xs = [ctx_of(y, z, (x + d) % XS) for d in (1, XS - 1)]
    zs = [ctx_of(y, (z + d) % ZS, x) for d in (1, ZS - 1)]
    return ctx_of(1 - y, z, x), xs, zs


def greet(ctx_list, head_list):
    barrier = pltpu.get_barrier_semaphore()
    for other in ctx_list:
        pl.semaphore_signal(barrier, inc=1, device_id={"ctx": other}, device_id_type=MESH)
    for other in head_list:
        pl.semaphore_signal(barrier, inc=1, device_id={"head": other}, device_id_type=MESH)
    pl.semaphore_wait(barrier, len(ctx_list) + len(head_list))


class Courier:
    def __init__(self, send, recv):
        self.send, self.recv, self.made, self.count = send, recv, {}, 0

    def plan(self, name, axis, other, src, dst):
        n = self.count
        self.count += 1
        self.made[name] = lambda: pltpu.make_async_remote_copy(
            src_ref=src,
            dst_ref=dst,
            send_sem=self.send.at[n],
            recv_sem=self.recv.at[n],
            device_id={axis: other},
            device_id_type=MESH,
        )

    def go(self, *names):
        for name in names:
            self.made[name]().start()

    def got(self, *names):
        for name in names:
            self.made[name]().wait_recv()

    def sent(self, *names):
        for name in names:
            self.made.pop(name)().wait_send()

    def finish(self):
        self.sent(*list(self.made))


class Handover:
    def __init__(self, send, recv, src, src_unit, dst, dst_unit, from_low):
        c, is_low, given = share()
        self.given = given
        self.sends = is_low if from_low else jnp.logical_not(is_low)
        self.takes = jnp.logical_not(self.sends)

        def copy(i):
            return pltpu.make_async_remote_copy(
                src_ref=src.at[pl.ds((src_unit + i) * UNIT, UNIT)],
                dst_ref=dst.at[pl.ds((dst_unit + i) * UNIT, UNIT)],
                send_sem=send.at[i],
                recv_sem=recv.at[i],
                device_id={"ctx": NCTX - 1 - c},
                device_id_type=MESH,
            )

        self.copy = copy

    def each(self, who, act):
        for i in range(GIVE):

            @pl.when(jnp.logical_and(who, i < self.given))
            def _():
                act(i)

    def start(self):
        self.each(self.sends, lambda i: self.copy(i).start())

    def wait_recv(self):
        self.each(self.takes, lambda i: self.copy(i).wait_recv())

    def wait_send(self):
        self.each(self.sends, lambda i: self.copy(i).wait_send())


def layer_kernel(
    unit, scale,
    k_ref, v_ref, cot_ref, q_ref, w_hbm,
    dq_ref, gk_ref, gv_ref, o_ref,
    w_ref, wsem, kv_ref, ca_ref, gt_ref, qw_ref, ga_ref, attn_ref, kept_ref, top_ref, m_row, l_row, acc_ref,
    attn_far, dq_par, dq_far, af_ref, flat_ref, ocore, osum, orow,
    dqs_ref, dk_ref, dv_ref,
    p_ref, t_ref, r_ref, m_ref, t2_ref, r2_ref, s_ref, y_ref,
    send, recv, hsend, hrecv,
):
    y, z, x = place()
    c, is_low, given = share()
    h = lax.axis_index("head")
    core, row = h ^ 1, h ^ 2
    mine, up = h % 2, h // 2
    partner, xs, zs = neighbours()

    def w_copy(i):
        cols = pl.ds(pl.multiple_of(i * WIDE, WIDE), WIDE)
        return pltpu.make_async_copy(w_hbm.at[:, cols], w_ref.at[i % 2], wsem.at[i % 2])

    def over_weight(act):
        chunks = w_hbm.shape[1] // WIDE

        def chunk(i, carry):
            w_copy(i).wait()
            act(i, w_ref.at[i % 2])

            @pl.when(i + 2 < chunks)
            def _():
                w_copy(i + 2).start()

            return carry

        lax.fori_loop(0, chunks, chunk, 0)

    w_copy(0).start()
    w_copy(1).start()
    greet([partner] + xs + zs + [NCTX - 1 - c], [core, row])
    mail = Courier(send, recv)

    def hand(i, *what):
        return Handover(hsend.at[i], hrecv.at[i], *what)

    kv_ref[c, 0] = k_ref[...]
    kv_ref[c, 1] = v_ref[...]
    mail.plan("pair", "ctx", partner, kv_ref.at[c], kv_ref.at[c])
    mail.go("pair")
    qs = hand(0, q_ref, 0, qw_ref, OWN, False)
    gs = hand(1, ga_ref, 0, ga_ref, OWN, False)
    attn_home = hand(2, attn_ref, OWN, attn_far, 0, True)
    dq_home = hand(3, dq_par, 0, dq_far, 0, True)
    ca_ref[h] = cot_ref[...]
    for name, o, i in (("cot row", row, h), ("cot core", core, h), ("cot relay", core, row)):
        mail.plan(name, "head", o, ca_ref.at[i], ca_ref.at[i])

    routes = ((z, x, zs, xs), (x, z, xs, zs))
    for n, (a, b, an, bn) in enumerate(routes):

        def slot(i, j, n=n):
            return kv_ref.at[jnp.where(n == 0, 16 + i * 4 + j, j * 4 + i)]

        for d in range(2):
            mail.plan((n, "beside", d), "ctx", an[d], slot(a, b), slot(a, b))
            part = slot((a + (3, 1)[d]) % 4, b).at[d]
            mail.plan((n, "on", d), "ctx", an[d], part, part)
            for s, off in enumerate((0, 3, 1, 2)):
                i = (a + off) % 4
                mail.plan((n, "third", s, d), "ctx", bn[d], slot(i, b), slot(i, b))
                part = slot(i, (b + (3, 1)[d]) % 4).at[d]
                mail.plan((n, "last", s, d), "ctx", bn[d], part, part)

    def pass_on(n, s):
        for d in range(2):
            mail.got((n, "third", s, d))
            mail.go((n, "last", s, d))

    for n, (a, an, b, bn) in enumerate(((x, xs, z, zs), (z, zs, x, xs))):
        steps = (
            (1, p_ref.at[n], a, an, t_ref.at[n], r_ref.at[n]),
            (2, m_ref.at[n], b, bn, t2_ref.at[n], r2_ref.at[n]),
        )
        for stage, piece, at, to, t, r in steps:
            for d in range(2):
                nxt = (at + (1, 3)[d]) % 4
                mail.plan((n, stage, "far", d), "ctx", to[d], piece.at[(at + 2) % 4, d], t.at[d])
                mail.plan(
                    (n, stage, "near", d), "ctx", to[d], piece.at[nxt, 1 - d], r.at[d, 1 - d]
                )
                mail.plan((n, stage, "sum", d), "ctx", to[d], t.at[d], r.at[d, d])
    mail.plan("y", "ctx", partner, s_ref.at[y], y_ref)
    for i in range(2):
        mail.plan(("core", i), "head", core, ca_ref.at[2 * i + 1 - mine], ocore.at[i])
    mail.plan("row", "head", row, osum.at[1 - up], orow)

    def far(n, stage):
        mail.go((n, stage, "far", 0), (n, stage, "far", 1))

    def near(n, stage, d):
        mail.go((n, stage, "near", d))

    def relay(n, stage, d):
        piece, at, t = (
            (p_ref.at[n], (x, z)[n], t_ref.at[n])
            if stage == 1
            else (m_ref.at[n], (z, x)[n], t2_ref.at[n])
        )
        nxt = (at + (1, 3)[d]) % 4
        mail.got((n, stage, "far", d))
        t[d] = (piece[nxt, d].astype(F32) + t[d].astype(F32)).astype(BF)
        mail.go((n, stage, "sum", d))

    def arrived(n, stage):
        for d in range(2):
            mail.got((n, stage, "near", d), (n, stage, "sum", d))

    def total_first(n, places):
        at = (x, z)[n]
        for place_now in places:
            j = turned((z, x)[n], place_now)
            for kv in range(2):
                m_ref[n, j, kv] = (
                    p_ref[n, at, kv, j].astype(F32)
                    + r_ref[n, 0, kv, j].astype(F32)
                    + r_ref[n, 1, kv, j].astype(F32)
                ).astype(BF)

    def total_second(n):
        arrived(n, 2)
        at = (z, x)[n]
        s_ref[n] = (
            m_ref[n, at].astype(F32) + r2_ref[n, 0].astype(F32) + r2_ref[n, 1].astype(F32)
        ).astype(BF)

    def output_projection():
        attn_home.wait_recv()
        own = OWN * UNIT
        af_ref[...] = attn_ref[pl.ds(0, own), :].astype(F32)

        def place_far(i):
            rows = pl.ds(i * UNIT, UNIT)
            af_ref[rows, :] = attn_far[rows, :].astype(F32)

        attn_home.each(attn_home.takes, place_far)
        for i in range(GROUP):
            flat_ref[:, i * HEAD : (i + 1) * HEAD] = af_ref[
                pl.ds(i, BLOCK, stride=GROUP), :
            ].astype(BF)
        mail.sent("cot row", "cot core", "cot relay")

        def project(i, w):
            cols = pl.ds(pl.multiple_of(i * WIDE, WIDE), WIDE)
            part = dot(flat_ref[...], w[...], NN).astype(BF)
            ca_ref[:, :, cols] = part.reshape(4, BLOCK // 4, WIDE)

        over_weight(project)
        mail.go(("core", 0), ("core", 1))

    def output_core():
        for i in range(2):
            mail.got(("core", i))
            osum[i] = (ca_ref[2 * i + mine].astype(F32) + ocore[i].astype(F32)).astype(BF)
        mail.go("row")

    begin = jnp.where(is_low, 0, given)
    taken = OWN + jnp.where(is_low, given, 0)

    def inner(n, i):
        return turned(jnp.where(n == 0, z, x), i)

    def block_of(n, at, i, own_first=False):
        j = turned_back(jnp.where(n == 0, z, x), i) if own_first else inner(n, i)
        return jnp.where(n == 0, 16 + 4 * j + at, 4 * at + j)

    def over_pair(n, at, jp, tile, own_first, between, turns=(0, 2)):
        last = jnp.maximum(
            block_of(n, at, 2 * jp, own_first), block_of(n, at, 2 * jp + 1, own_first)
        )

        def row_set(turn, carry):
            mine_now = turn == (0 if own_first else 1)
            u0 = jnp.where(mine_now, begin, OWN)
            u1 = jnp.where(mine_now, OWN, taken)
            qb = jnp.where(mine_now, c, NCTX - 1 - c)
            pos0 = jnp.where(mine_now, 0, OWN)
            twos = (u1 - u0) // 2
            odd = (u1 - u0) % 2
            whole = qb > last

            def full(i, carry):
                tile(u0 + 2 * i, 2, 2 * jp, 2, None)
                return carry

            lax.fori_loop(0, jnp.where(whole, twos, 0), full, 0)

            @pl.when(jnp.logical_and(whole, odd == 1))
            def _():
                tile(u1 - 1, 1, 2 * jp, 2, None)

            def single_block(j, carry):
                ahead = (qb - block_of(n, at, j, own_first)) * BLOCK
                some = jnp.logical_and(jnp.logical_not(whole), ahead >= 0)

                def part(i, carry):
                    u = u0 + 2 * i
                    tile(u, 2, j, 1, ahead + (u - pos0) * UNIT_POS)
                    return carry

                lax.fori_loop(0, jnp.where(some, twos, 0), part, 0)

                @pl.when(jnp.logical_and(some, odd == 1))
                def _():
                    u = u1 - 1
                    tile(u, 1, j, 1, ahead + (u - pos0) * UNIT_POS)

                return carry

            lax.fori_loop(2 * jp, 2 * jp + 2, single_block, 0)

            @pl.when(turn == 0)
            def _():
                between()

            return carry

        lax.fori_loop(turns[0], turns[1], row_set, 0)

    def slot_of(b, u):
        own = b * (OWN - begin) + u - begin
        far = (c + 1) * (OWN - begin) + b * (taken - OWN) + u - OWN
        return jnp.where(u < OWN, own, far)

    def parts(first, units, held):
        for k, b in enumerate(held):
            for i in range(units):
                yield (
                    slot_of(b, first + i),
                    slice(k * BLOCK, (k + 1) * BLOCK),
                    slice(i * UNIT, (i + 1) * UNIT),
                )

    def rows_of(first, units):
        return pl.ds(pl.multiple_of(first * UNIT, UNIT), units * UNIT)

    def mask(keys, n, ahead):
        qpos = ahead + lax.broadcasted_iota(jnp.int32, (keys, n), 1) // GROUP
        return lax.broadcasted_iota(jnp.int32, (keys, n), 0) <= qpos

    def forward_group(s, carry):
        n = (1 - y + s) % 2
        i = s % 8 // 2
        off = jnp.where(i == 0, 0, jnp.where(i == 1, 3, jnp.where(i == 2, 1, 2)))
        at = (jnp.where(n == 0, x, z) + off) % 4

        @pl.when(s == 1)
        def _():
            each_pass(False, front_end)
            each_pass(True, lambda n: (pass_on(n, 0), pass_on(n, 1)))

        @pl.when(s == 2)
        def _():
            each_pass(True, lambda n: (pass_on(n, 2), pass_on(n, 3)))
            each_pass(False, lambda n: (pass_on(n, 0), pass_on(n, 1)))
            qs.wait_recv()

        @pl.when(s == 3)
        def _():
            each_pass(False, lambda n: (pass_on(n, 2), pass_on(n, 3)))

        @pl.when(s == 5)
        def _():
            mail.got("cot row")
            mail.go("cot relay")

        def arrived_last(n):
            for step in range(4):
                mail.got((n, "last", step, 0), (n, "last", step, 1))

        @pl.when(s == 6)
        def _():
            project_cotangent()
            each_pass(True, arrived_last)

        @pl.when(s == 7)
        def _():
            each_pass(False, arrived_last)

        def tile(first, units, j, blocks, ahead):
            rows = rows_of(first, units)
            held = [block_of(n, at, j + i, True) for i in range(blocks)]
            keys = jnp.concatenate([kv_ref[b, 0] for b in held], axis=0)
            values = jnp.concatenate([kv_ref[b, 1] for b in held], axis=0)
            sc = dot(keys, qw_ref[rows, :], NT)
            if ahead is not None:
                sc = jnp.where(mask(sc.shape[0], sc.shape[1], ahead), sc, LOW)
            top = m_row[:, rows]
            new = jnp.maximum(top, jnp.max(sc, axis=0, keepdims=True))
            alpha = jnp.exp2((top - new) * unit)
            p = jnp.exp2((sc - new) * unit)
            m_row[:, rows] = new
            l_row[:, rows] = l_row[:, rows] * alpha + jnp.sum(p, axis=0, keepdims=True)
            p = p.astype(BF)
            acc_ref[:, rows] = acc_ref[:, rows] * alpha + dot(values, p, TN)
            for slot, ks, us in parts(first, units, held):
                kept_ref[slot] = p[ks, us]
                top_ref[slot] = new[:, us]

        def pair(jp, carry):
            turns = (jnp.where(s >= 8, 1, 0), jnp.where(s < 2, 1, 2))
            over_pair(n, at, jp, tile, True, lambda: None, turns)

            @pl.when(jnp.logical_and(s == 0, jp == 0))
            def _():
                each_pass(True, front_end)
                each_pass(False, front)
                mail.go("cot row", "cot core")

            return carry

        lax.fori_loop(0, 2, pair, 0)
        return carry

    def project_cotangent():
        mail.got("cot core", "cot relay")
        gt_ref[...] = jnp.zeros_like(gt_ref)

        def project(i, w):
            cols = pl.ds(pl.multiple_of(i * WIDE, WIDE), WIDE)
            gt_ref[...] += dot(w[...], ca_ref[:, :, cols].reshape(BLOCK, WIDE), NT)

        over_weight(project)
        w_copy(0).start()
        w_copy(1).start()
        for i in range(GROUP):
            af_ref[pl.ds(i, BLOCK, stride=GROUP), :] = jnp.transpose(
                gt_ref[i * HEAD : (i + 1) * HEAD, :]
            )
        ga_ref[pl.ds(0, OWN * UNIT), :] = af_ref[...].astype(BF)
        gs.start()

    def each_pass(first, act):
        for n in range(2):

            @pl.when(y == (1 - n if first else n))
            def _():
                act(n)

    def start(n):
        mail.go((n, "beside", 0), (n, "beside", 1), (n, "third", 0, 0), (n, "third", 0, 1))

    def front(n):
        for d in range(2):
            mail.got((n, "beside", d))
            mail.go((n, "on", d), (n, "third", 1 + d, 0), (n, "third", 1 + d, 1))

    def front_end(n):
        mail.got((n, "on", 0), (n, "on", 1))
        mail.go((n, "third", 3, 0), (n, "third", 3, 1))

    each_pass(True, start)
    qw_ref[pl.ds(0, OWN * UNIT), :] = q_ref[...]
    m_row[...] = jnp.full_like(m_row, LOW)
    l_row[...] = jnp.zeros_like(l_row)
    acc_ref[...] = jnp.zeros_like(acc_ref)
    mail.got("pair")
    each_pass(False, start)
    qs.start()
    each_pass(True, front)
    lax.fori_loop(0, 10, forward_group, 0)

    def finish_forward(i, carry):
        rows = pl.ds(pl.multiple_of(i * 512, 512), 512)
        l = l_row[:, rows]
        attn_ref[rows, :] = jnp.transpose(acc_ref[:, rows] / l).astype(BF)
        m_row[:, rows] = m_row[:, rows] * unit + jnp.log2(l)
        return carry

    lax.fori_loop(0, WORK // 512, finish_forward, 0)
    attn_home.start()
    gs.wait_recv()

    def prepare(i, carry):
        rows = pl.ds(pl.multiple_of(i * 512, 512), 512)
        products = ga_ref[rows, :].astype(F32) * attn_ref[rows, :].astype(F32)
        l_row[:, rows] = jnp.sum(jnp.transpose(products), axis=0, keepdims=True)
        dqs_ref[rows, :] = jnp.zeros((512, HEAD), F32)
        return carry

    lax.fori_loop(0, WORK // 512, prepare, 0)

    def backward_group(s, carry):
        n = s % 2
        i = s // 2
        off = jnp.where(i == 0, 2, jnp.where(i == 1, 1, jnp.where(i == 2, 3, 0)))
        at = (jnp.where(n == 0, x, z) + off) % 4

        def tile(first, units, j, blocks, ahead):
            rows = rows_of(first, units)
            held = [block_of(n, at, j + i) for i in range(blocks)]
            keys = jnp.concatenate([kv_ref[b, 0] for b in held], axis=0)
            values = jnp.concatenate([kv_ref[b, 1] for b in held], axis=0)
            q = qw_ref[rows, :]
            ga = ga_ref[rows, :]
            lse = m_row[:, rows]
            pieces = [
                kept_ref[slot].astype(F32) * jnp.exp2(top_ref[slot] * unit - lse[:, us])
                for slot, ks, us in parts(first, units, held)
            ]
            p = jnp.concatenate(
                [
                    jnp.concatenate(pieces[k * units : (k + 1) * units], axis=1)
                    for k in range(blocks)
                ],
                axis=0,
            )
            ds = (p * (dot(values, ga, NT) - l_row[:, rows])).astype(BF)
            ks = pl.ds(pl.multiple_of(j % 2 * BLOCK, BLOCK), blocks * BLOCK)
            dv_ref[ks, :] += dot(p.astype(BF), ga, NN)
            dk_ref[ks, :] += dot(ds, q, NN)
            dqs_ref[rows, :] += dot(ds, keys, TN)

        def pair(jp, carry):
            dk_ref[...] = jnp.zeros_like(dk_ref)
            dv_ref[...] = jnp.zeros_like(dv_ref)

            def between():
                @pl.when(jnp.logical_and(s == 7, jp == 1))
                def _():
                    far_rows = pl.ds(OWN * UNIT, GIVE * UNIT)
                    dq_par[...] = (dqs_ref[far_rows, :] * scale).astype(BF)
                    dq_home.start()
                    relay(0, 2, 0)
                    relay(0, 2, 1)

            over_pair(n, at, jp, tile, False, between)
            for i in range(2):
                ks = pl.ds(i * BLOCK, BLOCK)
                j = inner(n, 2 * jp + i)
                p_ref[n, at, 0, j] = (dk_ref[ks, :] * scale).astype(BF)
                p_ref[n, at, 1, j] = dv_ref[ks, :].astype(BF)

            @pl.when(jnp.logical_and(s == 7, jp == 0))
            def _():
                arrived(1, 1)
                total_first(1, (0, 1))
                far(1, 2)
                near(1, 2, 0)

            return carry

        lax.fori_loop(0, 2, pair, 0)

        @pl.when(s == 0)
        def _():
            far(0, 1)

        @pl.when(s == 1)
        def _():
            far(1, 1)

        @pl.when(s == 2)
        def _():
            near(0, 1, 0)
            relay(0, 1, 0)
            output_projection()

        @pl.when(s == 3)
        def _():
            near(1, 1, 0)
            relay(1, 1, 0)

        @pl.when(s == 4)
        def _():
            near(0, 1, 1)
            relay(0, 1, 1)
            output_core()

        @pl.when(s == 5)
        def _():
            near(1, 1, 1)
            relay(1, 1, 1)

        @pl.when(s == 6)
        def _():
            arrived(0, 1)
            total_first(0, range(4))
            far(0, 2)
            near(0, 2, 0)
            near(0, 2, 1)

        return carry

    lax.fori_loop(0, 8, backward_group, 0)
    total_first(1, (2, 3))
    near(1, 2, 1)
    dq_ref[...] = (dqs_ref[pl.ds(0, OWN * UNIT), :] * scale).astype(BF)
    relay(1, 2, 0)
    relay(1, 2, 1)
    total_second(0)

    @pl.when(y == 0)
    def _():
        mail.go("y")

    total_second(1)

    @pl.when(y == 1)
    def _():
        mail.go("y")

    mail.got("row")
    o_ref[...] = (osum[up].astype(F32) + orow[...].astype(F32)).astype(BF)
    dq_home.wait_recv()

    def place_dq(i):
        rows = pl.ds(i * UNIT, UNIT)
        dq_ref[rows, :] = dq_far[rows, :]

    dq_home.each(dq_home.takes, place_dq)
    mail.got("y")
    gk_ref[...] = (s_ref[1 - y, 0].astype(F32) + y_ref[0].astype(F32)).astype(BF)
    gv_ref[...] = (s_ref[1 - y, 1].astype(F32) + y_ref[1].astype(F32)).astype(BF)
    mail.finish()
    for hand in (qs, gs, attn_home, dq_home):
        hand.wait_send()


COPIES = 1 + 3 + 2 * 20 + 2 * 2 * 6 + 1 + 3


def layer(unit, scale, k, v, cot, q, w):
    vm, dma = pltpu.VMEM, pltpu.SemaphoreType.DMA
    part = (BLOCK // 4, w.shape[1])
    return pl.pallas_call(
        functools.partial(layer_kernel, unit, scale),
        out_shape=(
            jax.ShapeDtypeStruct((OWN * UNIT, HEAD), BF),
            jax.ShapeDtypeStruct((BLOCK, HEAD), BF),
            jax.ShapeDtypeStruct((BLOCK, HEAD), BF),
            jax.ShapeDtypeStruct(part, BF),
        ),
        in_specs=vmem_specs(4) + [pl.BlockSpec(memory_space=pl.ANY)],
        out_specs=tuple(vmem_specs(4)),
        scratch_shapes=[
            vm((2, w.shape[0], WIDE), BF),
            dma((2,)),
            vm((NCTX, 2, BLOCK, HEAD), BF),
            vm((4,) + cot.shape, BF),
            vm((GROUP * HEAD, BLOCK), F32),
            vm((WORK, HEAD), BF),
            vm((WORK, HEAD), BF),
            vm((WORK, HEAD), BF),
            vm((SLOTS, BLOCK, UNIT), BF),
            vm((SLOTS, 1, UNIT), F32),
            vm((1, WORK), F32),
            vm((1, WORK), F32),
            vm((HEAD, WORK), F32),
            vm((GIVE * UNIT, HEAD), BF),
            vm((GIVE * UNIT, HEAD), BF),
            vm((GIVE * UNIT, HEAD), BF),
            vm((OWN * UNIT, HEAD), F32),
            vm((BLOCK, GROUP * HEAD), BF),
            vm((2,) + part, BF),
            vm((2,) + part, BF),
            vm(part, BF),
            vm((WORK, HEAD), F32),
            vm((2 * BLOCK, HEAD), F32),
            vm((2 * BLOCK, HEAD), F32),
            vm((2, 4, 2, 4, BLOCK, HEAD), BF),
            vm((2, 2, 4, BLOCK, HEAD), BF),
            vm((2, 2, 2, 4, BLOCK, HEAD), BF),
            vm((2, 4, 2, BLOCK, HEAD), BF),
            vm((2, 2, BLOCK, HEAD), BF),
            vm((2, 2, 2, BLOCK, HEAD), BF),
            vm((2, 2, BLOCK, HEAD), BF),
            vm((2, BLOCK, HEAD), BF),
            dma((COPIES,)),
            dma((COPIES,)),
            dma((4, GIVE)),
            dma((4, GIVE)),
        ],
        compiler_params=pltpu.CompilerParams(
            collective_id=0, has_side_effects=True, vmem_limit_bytes=VMEM_LIMIT
        ),
        name="layer",
    )(k, v, cot, q, w)


def results_kernel(*refs):
    n = len(refs) // 2
    for i in range(n):
        refs[n + i][...] = refs[i][...]


def results(*arrays):
    n = len(arrays)
    return pl.pallas_call(
        results_kernel,
        out_shape=tuple(jax.ShapeDtypeStruct(a.shape, a.dtype) for a in arrays),
        in_specs=vmem_specs(n),
        out_specs=tuple(vmem_specs(n)),
        compiler_params=pltpu.CompilerParams(vmem_limit_bytes=VMEM_LIMIT),
        name="results",
    )(*arrays)


def vmem_specs(n):
    return [pl.BlockSpec(memory_space=pltpu.VMEM)] * n


def local(queries, key_rows, value_matrix, out_weight, cotangent):
    rows, heads, head = queries.shape
    scale = 1.0 / math.sqrt(head)
    unit = scale * math.log2(math.e)
    made = layer(
        unit,
        scale,
        key_rows.reshape(rows, head),
        value_matrix.reshape(rows, head),
        cotangent,
        queries.reshape(rows * heads, head),
        out_weight,
    )
    grad_queries, grad_keys, grad_values, output = results(*made)
    return (
        output,
        grad_queries.reshape(rows, heads, head),
        grad_keys.reshape(rows, 1, head),
        grad_values.reshape(rows, 1, head),
    )


def solution(mesh):
    return jax.shard_map(
        local,
        mesh=mesh,
        in_specs=(
            P("ctx", "head", None),
            P("ctx", "head", None),
            P("ctx", "head", None),
            P("head", None),
            P(("ctx", "head"), None),
        ),
        out_specs=(
            P(("ctx", "head"), None),
            P("ctx", "head", None),
            P("ctx", "head", None),
            P("ctx", "head", None),
        ),
        check_vma=False,
    )
```

```python
import functools
import math

import jax
import jax.numpy as jnp
from jax import lax
from jax.experimental import pallas as pl
from jax.experimental.pallas import tpu as pltpu
from jax.sharding import PartitionSpec as P

BF = jnp.bfloat16
F32 = jnp.float32
MESH = pl.DeviceIdType.MESH
YS, ZS, XS = 2, 4, 4
NCTX = YS * ZS * XS
HEAD = 128
GROUP = 8
BLOCK = 256
UNIT = 256
UNIT_POS = UNIT // GROUP
OWN = BLOCK * GROUP // UNIT
GIVE = 4
WORK = (OWN + GIVE) * UNIT
LOW = -1e30
CUT = (0, 3, 5)
WIDE = 1024
SLOTS = 146
VMEM_LIMIT = 60 * 1024 * 1024

NT = (((1,), (1,)), ((), ()))
NN = (((1,), (0,)), ((), ()))
TN = (((0,), (0,)), ((), ()))


def dot(a, b, dims):
    return lax.dot_general(a, b, dims, preferred_element_type=F32)


def share():
    c = lax.axis_index("ctx")
    low = jnp.minimum(c, NCTX - 1 - c)
    given = jnp.where(
        low <= 2, 4, jnp.where(low <= 7, 3, jnp.where(low <= 11, 2, jnp.where(low <= 14, 1, 0)))
    )
    return c, c < NCTX // 2, given


def place():
    c = lax.axis_index("ctx")
    return c // (ZS * XS), (c // XS) % ZS, c % XS


def ctx_of(y, z, x):
    return (y * ZS + z) * XS + x


def turned_back(own, i):
    return (own + jnp.where(i == 0, 0, jnp.where(i == 1, 1, jnp.where(i == 2, 3, 2)))) % 4


def turned(own, i):
    return (own + jnp.where(i == 0, 2, jnp.where(i == 1, 1, jnp.where(i == 2, 3, 0)))) % 4


def neighbours():
    y, z, x = place()
    xs = [ctx_of(y, z, (x + d) % XS) for d in (1, XS - 1)]
    zs = [ctx_of(y, (z + d) % ZS, x) for d in (1, ZS - 1)]
    return ctx_of(1 - y, z, x), xs, zs


def greet(ctx_list, head_list):
    barrier = pltpu.get_barrier_semaphore()
    for other in ctx_list:
        pl.semaphore_signal(barrier, inc=1, device_id={"ctx": other}, device_id_type=MESH)
    for other in head_list:
        pl.semaphore_signal(barrier, inc=1, device_id={"head": other}, device_id_type=MESH)
    pl.semaphore_wait(barrier, len(ctx_list) + len(head_list))


class Courier:
    def __init__(self, send, recv):
        self.send, self.recv, self.made, self.count = send, recv, {}, 0

    def plan(self, name, axis, other, src, dst):
        n = self.count
        self.count += 1
        self.made[name] = lambda: pltpu.make_async_remote_copy(
            src_ref=src,
            dst_ref=dst,
            send_sem=self.send.at[n],
            recv_sem=self.recv.at[n],
            device_id={axis: other},
            device_id_type=MESH,
        )

    def go(self, *names):
        for name in names:
            self.made[name]().start()

    def got(self, *names):
        for name in names:
            self.made[name]().wait_recv()

    def sent(self, *names):
        for name in names:
            self.made.pop(name)().wait_send()

    def finish(self):
        self.sent(*list(self.made))


class Handover:
    def __init__(self, send, recv, src, src_unit, dst, dst_unit, from_low):
        c, is_low, given = share()
        self.given = given
        self.sends = is_low if from_low else jnp.logical_not(is_low)
        self.takes = jnp.logical_not(self.sends)

        def copy(i):
            return pltpu.make_async_remote_copy(
                src_ref=src.at[pl.ds((src_unit + i) * UNIT, UNIT)],
                dst_ref=dst.at[pl.ds((dst_unit + i) * UNIT, UNIT)],
                send_sem=send.at[i],
                recv_sem=recv.at[i],
                device_id={"ctx": NCTX - 1 - c},
                device_id_type=MESH,
            )

        self.copy = copy

    def each(self, who, act):
        for i in range(GIVE):

            @pl.when(jnp.logical_and(who, i < self.given))
            def _():
                act(i)

    def start(self):
        self.each(self.sends, lambda i: self.copy(i).start())

    def wait_recv(self):
        self.each(self.takes, lambda i: self.copy(i).wait_recv())

    def wait_send(self):
        self.each(self.sends, lambda i: self.copy(i).wait_send())


def layer_kernel(
    unit, scale,
    k_ref, v_ref, cot_ref, q_ref, w_hbm,
    dq_ref, gk_ref, gv_ref, o_ref,
    w_ref, wsem, kv_ref, ca_ref, gt_ref, qw_ref, ga_ref, attn_ref, kept_ref, top_ref, m_row, l_row, acc_ref,
    attn_far, dq_par, dq_far, af_ref, flat_ref, ocore, osum, orow,
    dqs_ref, dk_ref, dv_ref,
    p_ref, t_ref, r_ref, m_ref, t2_ref, r2_ref, s_ref, y_ref,
    send, recv, hsend, hrecv,
):
    y, z, x = place()
    c, is_low, given = share()
    h = lax.axis_index("head")
    core, row = h ^ 1, h ^ 2
    mine, up = h % 2, h // 2
    partner, xs, zs = neighbours()

    def w_copy(i):
        cols = pl.ds(pl.multiple_of(i * WIDE, WIDE), WIDE)
        return pltpu.make_async_copy(w_hbm.at[:, cols], w_ref.at[i % 2], wsem.at[i % 2])

    def over_weight(act, first, last):
        chunks = w_hbm.shape[1] // WIDE

        def chunk(i, carry):
            w_copy(i).wait()
            act(i, w_ref.at[i % 2])

            @pl.when(i + 2 < chunks)
            def _():
                w_copy(i + 2).start()

            return carry

        lax.fori_loop(first, last, chunk, 0)

    w_copy(0).start()
    w_copy(1).start()
    greet([partner] + xs + zs + [NCTX - 1 - c], [core, row])
    mail = Courier(send, recv)

    def hand(i, *what):
        return Handover(hsend.at[i], hrecv.at[i], *what)

    kv_ref[c, 0] = k_ref[...]
    kv_ref[c, 1] = v_ref[...]
    mail.plan("pair", "ctx", partner, kv_ref.at[c], kv_ref.at[c])
    mail.go("pair")
    qs = hand(0, q_ref, 0, qw_ref, OWN, False)
    gs = hand(1, ga_ref, 0, ga_ref, OWN, False)
    attn_home = hand(2, attn_ref, OWN, attn_far, 0, True)
    dq_home = hand(3, dq_par, 0, dq_far, 0, True)
    ca_ref[h] = cot_ref[...]
    for name, o, i in (("cot row", row, h), ("cot core", core, h), ("cot relay", core, row)):
        mail.plan(name, "head", o, ca_ref.at[i], ca_ref.at[i])

    routes = ((z, x, zs, xs), (x, z, xs, zs))
    for n, (a, b, an, bn) in enumerate(routes):

        def slot(i, j, n=n):
            return kv_ref.at[jnp.where(n == 0, 16 + i * 4 + j, j * 4 + i)]

        for d in range(2):
            mail.plan((n, "beside", d), "ctx", an[d], slot(a, b), slot(a, b))
            part = slot((a + (3, 1)[d]) % 4, b).at[d]
            mail.plan((n, "on", d), "ctx", an[d], part, part)
            for s, off in enumerate((0, 3, 1, 2)):
                i = (a + off) % 4
                mail.plan((n, "third", s, d), "ctx", bn[d], slot(i, b), slot(i, b))
                part = slot(i, (b + (3, 1)[d]) % 4).at[d]
                mail.plan((n, "last", s, d), "ctx", bn[d], part, part)

    def pass_on(n, s):
        for d in range(2):
            mail.got((n, "third", s, d))
            mail.go((n, "last", s, d))

    for n, (a, an, b, bn) in enumerate(((x, xs, z, zs), (z, zs, x, xs))):
        steps = (
            (1, p_ref.at[n], a, an, t_ref.at[n], r_ref.at[n]),
            (2, m_ref.at[n], b, bn, t2_ref.at[n], r2_ref.at[n]),
        )
        for stage, piece, at, to, t, r in steps:
            for d in range(2):
                nxt = (at + (1, 3)[d]) % 4
                mail.plan((n, stage, "far", d), "ctx", to[d], piece.at[(at + 2) % 4, d], t.at[d])
                mail.plan(
                    (n, stage, "near", d), "ctx", to[d], piece.at[nxt, 1 - d], r.at[d, 1 - d]
                )
                mail.plan((n, stage, "sum", d), "ctx", to[d], t.at[d], r.at[d, d])
    mail.plan("y", "ctx", partner, s_ref.at[y], y_ref)
    part_cols = [pl.ds(CUT[k] * WIDE, (CUT[k + 1] - CUT[k]) * WIDE) for k in range(2)]
    for k, cols in enumerate(part_cols):
        for i in range(2):
            src = ca_ref.at[2 * i + 1 - mine, :, cols]
            mail.plan(("core", k, i), "head", core, src, ocore.at[i, :, cols])
        mail.plan(("row", k), "head", row, osum.at[1 - up, :, cols], orow.at[:, cols])

    def far(n, stage):
        mail.go((n, stage, "far", 0), (n, stage, "far", 1))

    def near(n, stage, d):
        mail.go((n, stage, "near", d))

    def relay(n, stage, d):
        piece, at, t = (
            (p_ref.at[n], (x, z)[n], t_ref.at[n])
            if stage == 1
            else (m_ref.at[n], (z, x)[n], t2_ref.at[n])
        )
        nxt = (at + (1, 3)[d]) % 4
        mail.got((n, stage, "far", d))
        t[d] = (piece[nxt, d].astype(F32) + t[d].astype(F32)).astype(BF)
        mail.go((n, stage, "sum", d))

    def arrived(n, stage):
        for d in range(2):
            mail.got((n, stage, "near", d), (n, stage, "sum", d))

    def total_first(n, places):
        at = (x, z)[n]
        for place_now in places:
            j = turned((z, x)[n], place_now)
            for kv in range(2):
                m_ref[n, j, kv] = (
                    p_ref[n, at, kv, j].astype(F32)
                    + r_ref[n, 0, kv, j].astype(F32)
                    + r_ref[n, 1, kv, j].astype(F32)
                ).astype(BF)

    def total_second(n):
        arrived(n, 2)
        at = (z, x)[n]
        s_ref[n] = (
            m_ref[n, at].astype(F32) + r2_ref[n, 0].astype(F32) + r2_ref[n, 1].astype(F32)
        ).astype(BF)

    def output_projection(k):
        if k == 0:
            attn_home.wait_recv()
            own = OWN * UNIT
            af_ref[...] = attn_ref[pl.ds(0, own), :].astype(F32)

            def place_far(i):
                rows = pl.ds(i * UNIT, UNIT)
                af_ref[rows, :] = attn_far[rows, :].astype(F32)

            attn_home.each(attn_home.takes, place_far)
            for i in range(GROUP):
                flat_ref[:, i * HEAD : (i + 1) * HEAD] = af_ref[
                    pl.ds(i, BLOCK, stride=GROUP), :
                ].astype(BF)
            mail.sent("cot row", "cot core", "cot relay")

        def project(i, w):
            cols = pl.ds(pl.multiple_of(i * WIDE, WIDE), WIDE)
            part = dot(flat_ref[...], w[...], NN).astype(BF)
            ca_ref[:, :, cols] = part.reshape(4, BLOCK // 4, WIDE)

        over_weight(project, CUT[k], CUT[k + 1])
        mail.go(("core", k, 0), ("core", k, 1))

    def output_core(k):
        cols = part_cols[k]
        for i in range(2):
            mail.got(("core", k, i))
            osum[i, :, cols] = (
                ca_ref[2 * i + mine, :, cols].astype(F32) + ocore[i, :, cols].astype(F32)
            ).astype(BF)
        mail.go(("row", k))

    begin = jnp.where(is_low, 0, given)
    taken = OWN + jnp.where(is_low, given, 0)

    def inner(n, i):
        return turned(jnp.where(n == 0, z, x), i)

    def block_of(n, at, i, own_first=False):
        j = turned_back(jnp.where(n == 0, z, x), i) if own_first else inner(n, i)
        return jnp.where(n == 0, 16 + 4 * j + at, 4 * at + j)

    def over_pair(n, at, jp, tile, own_first, between, turns=(0, 2)):
        last = jnp.maximum(
            block_of(n, at, 2 * jp, own_first), block_of(n, at, 2 * jp + 1, own_first)
        )

        def row_set(turn, carry):
            mine_now = turn == (0 if own_first else 1)
            u0 = jnp.where(mine_now, begin, OWN)
            u1 = jnp.where(mine_now, OWN, taken)
            qb = jnp.where(mine_now, c, NCTX - 1 - c)
            pos0 = jnp.where(mine_now, 0, OWN)
            twos = (u1 - u0) // 2
            odd = (u1 - u0) % 2
            whole = qb > last

            def full(i, carry):
                tile(u0 + 2 * i, 2, 2 * jp, 2, None)
                return carry

            lax.fori_loop(0, jnp.where(whole, twos, 0), full, 0)

            @pl.when(jnp.logical_and(whole, odd == 1))
            def _():
                tile(u1 - 1, 1, 2 * jp, 2, None)

            def single_block(j, carry):
                ahead = (qb - block_of(n, at, j, own_first)) * BLOCK
                some = jnp.logical_and(jnp.logical_not(whole), ahead >= 0)

                def part(i, carry):
                    u = u0 + 2 * i
                    tile(u, 2, j, 1, ahead + (u - pos0) * UNIT_POS)
                    return carry

                lax.fori_loop(0, jnp.where(some, twos, 0), part, 0)

                @pl.when(jnp.logical_and(some, odd == 1))
                def _():
                    u = u1 - 1
                    tile(u, 1, j, 1, ahead + (u - pos0) * UNIT_POS)

                return carry

            lax.fori_loop(2 * jp, 2 * jp + 2, single_block, 0)

            @pl.when(turn == 0)
            def _():
                between()

            return carry

        lax.fori_loop(turns[0], turns[1], row_set, 0)

    def slot_of(b, u):
        own = b * (OWN - begin) + u - begin
        far = (c + 1) * (OWN - begin) + b * (taken - OWN) + u - OWN
        return jnp.where(u < OWN, own, far)

    def parts(first, units, held):
        for k, b in enumerate(held):
            for i in range(units):
                yield (
                    slot_of(b, first + i),
                    slice(k * BLOCK, (k + 1) * BLOCK),
                    slice(i * UNIT, (i + 1) * UNIT),
                )

    def rows_of(first, units):
        return pl.ds(pl.multiple_of(first * UNIT, UNIT), units * UNIT)

    def mask(keys, n, ahead):
        qpos = ahead + lax.broadcasted_iota(jnp.int32, (keys, n), 1) // GROUP
        return lax.broadcasted_iota(jnp.int32, (keys, n), 0) <= qpos

    def forward_group(s, carry):
        n = (1 - y + s) % 2
        i = s % 8 // 2
        off = jnp.where(i == 0, 0, jnp.where(i == 1, 3, jnp.where(i == 2, 1, 2)))
        at = (jnp.where(n == 0, x, z) + off) % 4

        @pl.when(s == 1)
        def _():
            each_pass(False, front_end)
            each_pass(True, lambda n: (pass_on(n, 0), pass_on(n, 1)))

        @pl.when(s == 2)
        def _():
            each_pass(True, lambda n: (pass_on(n, 2), pass_on(n, 3)))
            each_pass(False, lambda n: (pass_on(n, 0), pass_on(n, 1)))
            qs.wait_recv()

        @pl.when(s == 3)
        def _():
            each_pass(False, lambda n: (pass_on(n, 2), pass_on(n, 3)))

        @pl.when(s == 5)
        def _():
            mail.got("cot row")
            mail.go("cot relay")

        def arrived_last(n):
            for step in range(4):
                mail.got((n, "last", step, 0), (n, "last", step, 1))

        @pl.when(s == 6)
        def _():
            project_cotangent()
            each_pass(True, arrived_last)

        @pl.when(s == 7)
        def _():
            each_pass(False, arrived_last)

        def tile(first, units, j, blocks, ahead):
            rows = rows_of(first, units)
            held = [block_of(n, at, j + i, True) for i in range(blocks)]
            keys = jnp.concatenate([kv_ref[b, 0] for b in held], axis=0)
            values = jnp.concatenate([kv_ref[b, 1] for b in held], axis=0)
            sc = dot(keys, qw_ref[rows, :], NT)
            if ahead is not None:
                sc = jnp.where(mask(sc.shape[0], sc.shape[1], ahead), sc, LOW)
            top = m_row[:, rows]
            new = jnp.maximum(top, jnp.max(sc, axis=0, keepdims=True))
            alpha = jnp.exp2((top - new) * unit)
            p = jnp.exp2((sc - new) * unit)
            m_row[:, rows] = new
            l_row[:, rows] = l_row[:, rows] * alpha + jnp.sum(p, axis=0, keepdims=True)
            p = p.astype(BF)
            acc_ref[:, rows] = acc_ref[:, rows] * alpha + dot(values, p, TN)
            for slot, ks, us in parts(first, units, held):
                kept_ref[slot] = p[ks, us]
                top_ref[slot] = new[:, us]

        def pair(jp, carry):
            turns = (jnp.where(s >= 8, 1, 0), jnp.where(s < 2, 1, 2))
            over_pair(n, at, jp, tile, True, lambda: None, turns)

            @pl.when(jnp.logical_and(s == 0, jp == 0))
            def _():
                each_pass(True, front_end)
                each_pass(False, front)
                mail.go("cot row", "cot core")

            return carry

        lax.fori_loop(0, 2, pair, 0)
        return carry

    def project_cotangent():
        mail.got("cot core", "cot relay")
        gt_ref[...] = jnp.zeros_like(gt_ref)

        def project(i, w):
            cols = pl.ds(pl.multiple_of(i * WIDE, WIDE), WIDE)
            gt_ref[...] += dot(w[...], ca_ref[:, :, cols].reshape(BLOCK, WIDE), NT)

        over_weight(project, 0, w_hbm.shape[1] // WIDE)
        w_copy(0).start()
        w_copy(1).start()
        for i in range(GROUP):
            af_ref[pl.ds(i, BLOCK, stride=GROUP), :] = jnp.transpose(
                gt_ref[i * HEAD : (i + 1) * HEAD, :]
            )
        ga_ref[pl.ds(0, OWN * UNIT), :] = af_ref[...].astype(BF)
        gs.start()

    def each_pass(first, act):
        for n in range(2):

            @pl.when(y == (1 - n if first else n))
            def _():
                act(n)

    def start(n):
        mail.go((n, "beside", 0), (n, "beside", 1), (n, "third", 0, 0), (n, "third", 0, 1))

    def front(n):
        for d in range(2):
            mail.got((n, "beside", d))
            mail.go((n, "on", d), (n, "third", 1 + d, 0), (n, "third", 1 + d, 1))

    def front_end(n):
        mail.got((n, "on", 0), (n, "on", 1))
        mail.go((n, "third", 3, 0), (n, "third", 3, 1))

    each_pass(True, start)
    qw_ref[pl.ds(0, OWN * UNIT), :] = q_ref[...]
    m_row[...] = jnp.full_like(m_row, LOW)
    l_row[...] = jnp.zeros_like(l_row)
    acc_ref[...] = jnp.zeros_like(acc_ref)
    mail.got("pair")
    each_pass(False, start)
    qs.start()
    each_pass(True, front)
    lax.fori_loop(0, 10, forward_group, 0)

    def finish_forward(i, carry):
        rows = pl.ds(pl.multiple_of((i + 4) % 6 * 512, 512), 512)
        l = l_row[:, rows]
        attn_ref[rows, :] = jnp.transpose(acc_ref[:, rows] / l).astype(BF)
        m_row[:, rows] = m_row[:, rows] * unit + jnp.log2(l)

        @pl.when(i == 1)
        def _():
            attn_home.start()

        return carry

    lax.fori_loop(0, WORK // 512, finish_forward, 0)
    gs.wait_recv()

    def prepare(i, carry):
        rows = pl.ds(pl.multiple_of(i * 512, 512), 512)
        products = ga_ref[rows, :].astype(F32) * attn_ref[rows, :].astype(F32)
        l_row[:, rows] = jnp.sum(jnp.transpose(products), axis=0, keepdims=True)
        dqs_ref[rows, :] = jnp.zeros((512, HEAD), F32)
        return carry

    lax.fori_loop(0, WORK // 512, prepare, 0)

    def backward_group(s, carry):
        n = s % 2
        i = s // 2
        off = jnp.where(i == 0, 2, jnp.where(i == 1, 1, jnp.where(i == 2, 3, 0)))
        at = (jnp.where(n == 0, x, z) + off) % 4

        def tile(first, units, j, blocks, ahead):
            rows = rows_of(first, units)
            held = [block_of(n, at, j + i) for i in range(blocks)]
            keys = jnp.concatenate([kv_ref[b, 0] for b in held], axis=0)
            values = jnp.concatenate([kv_ref[b, 1] for b in held], axis=0)
            q = qw_ref[rows, :]
            ga = ga_ref[rows, :]
            lse = m_row[:, rows]
            pieces = [
                kept_ref[slot].astype(F32) * jnp.exp2(top_ref[slot] * unit - lse[:, us])
                for slot, ks, us in parts(first, units, held)
            ]
            p = jnp.concatenate(
                [
                    jnp.concatenate(pieces[k * units : (k + 1) * units], axis=1)
                    for k in range(blocks)
                ],
                axis=0,
            )
            ds = (p * (dot(values, ga, NT) - l_row[:, rows])).astype(BF)
            ks = pl.ds(pl.multiple_of(j % 2 * BLOCK, BLOCK), blocks * BLOCK)
            dv_ref[ks, :] += dot(p.astype(BF), ga, NN)
            dk_ref[ks, :] += dot(ds, q, NN)
            dqs_ref[rows, :] += dot(ds, keys, TN)

        def pair(jp, carry):
            dk_ref[...] = jnp.zeros_like(dk_ref)
            dv_ref[...] = jnp.zeros_like(dv_ref)

            def between():
                @pl.when(jnp.logical_and(s == 7, jp == 1))
                def _():
                    far_rows = pl.ds(OWN * UNIT, GIVE * UNIT)
                    dq_par[...] = (dqs_ref[far_rows, :] * scale).astype(BF)
                    dq_home.start()
                    relay(0, 2, 0)
                    relay(0, 2, 1)

            over_pair(n, at, jp, tile, False, between)
            for i in range(2):
                ks = pl.ds(i * BLOCK, BLOCK)
                j = inner(n, 2 * jp + i)
                p_ref[n, at, 0, j] = (dk_ref[ks, :] * scale).astype(BF)
                p_ref[n, at, 1, j] = dv_ref[ks, :].astype(BF)

            @pl.when(jnp.logical_and(s == 7, jp == 0))
            def _():
                arrived(1, 1)
                total_first(1, (0, 1))
                far(1, 2)
                near(1, 2, 0)

            return carry

        lax.fori_loop(0, 2, pair, 0)

        @pl.when(s == 0)
        def _():
            far(0, 1)

        @pl.when(s == 1)
        def _():
            far(1, 1)

        @pl.when(s == 2)
        def _():
            near(0, 1, 0)
            relay(0, 1, 0)
            output_projection(0)

        @pl.when(s == 3)
        def _():
            near(1, 1, 0)
            relay(1, 1, 0)

        @pl.when(s == 4)
        def _():
            near(0, 1, 1)
            relay(0, 1, 1)
            output_core(0)

        @pl.when(s == 5)
        def _():
            near(1, 1, 1)
            relay(1, 1, 1)
            output_projection(1)

        @pl.when(s == 6)
        def _():
            output_core(1)
            arrived(0, 1)
            total_first(0, range(4))
            far(0, 2)
            near(0, 2, 0)
            near(0, 2, 1)

        return carry

    lax.fori_loop(0, 8, backward_group, 0)
    total_first(1, (2, 3))
    near(1, 2, 1)
    dq_ref[...] = (dqs_ref[pl.ds(0, OWN * UNIT), :] * scale).astype(BF)
    relay(1, 2, 0)
    relay(1, 2, 1)
    total_second(0)

    @pl.when(y == 0)
    def _():
        mail.go("y")

    total_second(1)

    @pl.when(y == 1)
    def _():
        mail.go("y")

    mail.got(("row", 0), ("row", 1))
    o_ref[...] = (osum[up].astype(F32) + orow[...].astype(F32)).astype(BF)
    dq_home.wait_recv()

    def place_dq(i):
        rows = pl.ds(i * UNIT, UNIT)
        dq_ref[rows, :] = dq_far[rows, :]

    dq_home.each(dq_home.takes, place_dq)
    mail.got("y")
    gk_ref[...] = (s_ref[1 - y, 0].astype(F32) + y_ref[0].astype(F32)).astype(BF)
    gv_ref[...] = (s_ref[1 - y, 1].astype(F32) + y_ref[1].astype(F32)).astype(BF)
    mail.finish()
    for hand in (qs, gs, attn_home, dq_home):
        hand.wait_send()


COPIES = 1 + 3 + 2 * 20 + 2 * 2 * 6 + 1 + 6


def layer(unit, scale, k, v, cot, q, w):
    vm, dma = pltpu.VMEM, pltpu.SemaphoreType.DMA
    part = (BLOCK // 4, w.shape[1])
    return pl.pallas_call(
        functools.partial(layer_kernel, unit, scale),
        out_shape=(
            jax.ShapeDtypeStruct((OWN * UNIT, HEAD), BF),
            jax.ShapeDtypeStruct((BLOCK, HEAD), BF),
            jax.ShapeDtypeStruct((BLOCK, HEAD), BF),
            jax.ShapeDtypeStruct(part, BF),
        ),
        in_specs=vmem_specs(4) + [pl.BlockSpec(memory_space=pl.ANY)],
        out_specs=tuple(vmem_specs(4)),
        scratch_shapes=[
            vm((2, w.shape[0], WIDE), BF),
            dma((2,)),
            vm((NCTX, 2, BLOCK, HEAD), BF),
            vm((4,) + cot.shape, BF),
            vm((GROUP * HEAD, BLOCK), F32),
            vm((WORK, HEAD), BF),
            vm((WORK, HEAD), BF),
            vm((WORK, HEAD), BF),
            vm((SLOTS, BLOCK, UNIT), BF),
            vm((SLOTS, 1, UNIT), F32),
            vm((1, WORK), F32),
            vm((1, WORK), F32),
            vm((HEAD, WORK), F32),
            vm((GIVE * UNIT, HEAD), BF),
            vm((GIVE * UNIT, HEAD), BF),
            vm((GIVE * UNIT, HEAD), BF),
            vm((OWN * UNIT, HEAD), F32),
            vm((BLOCK, GROUP * HEAD), BF),
            vm((2,) + part, BF),
            vm((2,) + part, BF),
            vm(part, BF),
            vm((WORK, HEAD), F32),
            vm((2 * BLOCK, HEAD), F32),
            vm((2 * BLOCK, HEAD), F32),
            vm((2, 4, 2, 4, BLOCK, HEAD), BF),
            vm((2, 2, 4, BLOCK, HEAD), BF),
            vm((2, 2, 2, 4, BLOCK, HEAD), BF),
            vm((2, 4, 2, BLOCK, HEAD), BF),
            vm((2, 2, BLOCK, HEAD), BF),
            vm((2, 2, 2, BLOCK, HEAD), BF),
            vm((2, 2, BLOCK, HEAD), BF),
            vm((2, BLOCK, HEAD), BF),
            dma((COPIES,)),
            dma((COPIES,)),
            dma((4, GIVE)),
            dma((4, GIVE)),
        ],
        compiler_params=pltpu.CompilerParams(
            collective_id=0, has_side_effects=True, vmem_limit_bytes=VMEM_LIMIT
        ),
        name="layer",
    )(k, v, cot, q, w)


def results_kernel(*refs):
    n = len(refs) // 2
    for i in range(n):
        refs[n + i][...] = refs[i][...]


def results(*arrays):
    n = len(arrays)
    return pl.pallas_call(
        results_kernel,
        out_shape=tuple(jax.ShapeDtypeStruct(a.shape, a.dtype) for a in arrays),
        in_specs=vmem_specs(n),
        out_specs=tuple(vmem_specs(n)),
        compiler_params=pltpu.CompilerParams(vmem_limit_bytes=VMEM_LIMIT),
        name="results",
    )(*arrays)


def vmem_specs(n):
    return [pl.BlockSpec(memory_space=pltpu.VMEM)] * n


def local(queries, key_rows, value_matrix, out_weight, cotangent):
    rows, heads, head = queries.shape
    scale = 1.0 / math.sqrt(head)
    unit = scale * math.log2(math.e)
    made = layer(
        unit,
        scale,
        key_rows.reshape(rows, head),
        value_matrix.reshape(rows, head),
        cotangent,
        queries.reshape(rows * heads, head),
        out_weight,
    )
    grad_queries, grad_keys, grad_values, output = results(*made)
    return (
        output,
        grad_queries.reshape(rows, heads, head),
        grad_keys.reshape(rows, 1, head),
        grad_values.reshape(rows, 1, head),
    )


def solution(mesh):
    return jax.shard_map(
        local,
        mesh=mesh,
        in_specs=(
            P("ctx", "head", None),
            P("ctx", "head", None),
            P("ctx", "head", None),
            P("head", None),
            P(("ctx", "head"), None),
        ),
        out_specs=(
            P(("ctx", "head"), None),
            P("ctx", "head", None),
            P("ctx", "head", None),
            P("ctx", "head", None),
        ),
        check_vma=False,
    )
```

```python
import functools
import math

import jax
import jax.numpy as jnp
from jax import lax
from jax.experimental import pallas as pl
from jax.experimental.pallas import tpu as pltpu
from jax.sharding import PartitionSpec as P

BF = jnp.bfloat16
F32 = jnp.float32
MESH = pl.DeviceIdType.MESH
YS, ZS, XS = 2, 4, 4
NCTX = YS * ZS * XS
HEAD = 128
GROUP = 8
BLOCK = 256
UNIT = 256
UNIT_POS = UNIT // GROUP
OWN = BLOCK * GROUP // UNIT
GIVE = 4
WORK = (OWN + GIVE) * UNIT
LOW = -1e30
CUT = (0, 3, 5)
WIDE = 1024
SLOTS = 146
VMEM_LIMIT = 60 * 1024 * 1024

NT = (((1,), (1,)), ((), ()))
NN = (((1,), (0,)), ((), ()))
TN = (((0,), (0,)), ((), ()))


def dot(a, b, dims):
    return lax.dot_general(a, b, dims, preferred_element_type=F32)


def share():
    c = lax.axis_index("ctx")
    low = jnp.minimum(c, NCTX - 1 - c)
    given = jnp.where(
        low <= 2, 4, jnp.where(low <= 7, 3, jnp.where(low <= 11, 2, jnp.where(low <= 14, 1, 0)))
    )
    return c, c < NCTX // 2, given


def place():
    c = lax.axis_index("ctx")
    return c // (ZS * XS), (c // XS) % ZS, c % XS


def ctx_of(y, z, x):
    return (y * ZS + z) * XS + x


def turned_back(own, i):
    return (own + jnp.where(i == 0, 0, jnp.where(i == 1, 1, jnp.where(i == 2, 3, 2)))) % 4


def turned(own, i):
    return (own + jnp.where(i == 0, 2, jnp.where(i == 1, 1, jnp.where(i == 2, 3, 0)))) % 4


def neighbours():
    y, z, x = place()
    xs = [ctx_of(y, z, (x + d) % XS) for d in (1, XS - 1)]
    zs = [ctx_of(y, (z + d) % ZS, x) for d in (1, ZS - 1)]
    return ctx_of(1 - y, z, x), xs, zs


def greet(ctx_list, head_list):
    barrier = pltpu.get_barrier_semaphore()
    for other in ctx_list:
        pl.semaphore_signal(barrier, inc=1, device_id={"ctx": other}, device_id_type=MESH)
    for other in head_list:
        pl.semaphore_signal(barrier, inc=1, device_id={"head": other}, device_id_type=MESH)
    pl.semaphore_wait(barrier, len(ctx_list) + len(head_list))


class Courier:
    def __init__(self, send, recv):
        self.send, self.recv, self.made, self.count = send, recv, {}, 0

    def plan(self, name, axis, other, src, dst):
        n = self.count
        self.count += 1
        self.made[name] = lambda: pltpu.make_async_remote_copy(
            src_ref=src,
            dst_ref=dst,
            send_sem=self.send.at[n],
            recv_sem=self.recv.at[n],
            device_id={axis: other},
            device_id_type=MESH,
        )

    def go(self, *names):
        for name in names:
            self.made[name]().start()

    def got(self, *names):
        for name in names:
            self.made[name]().wait_recv()

    def sent(self, *names):
        for name in names:
            self.made.pop(name)().wait_send()

    def finish(self):
        self.sent(*list(self.made))


class Handover:
    def __init__(self, send, recv, src, src_unit, dst, dst_unit, from_low):
        c, is_low, given = share()
        self.given = given
        self.sends = is_low if from_low else jnp.logical_not(is_low)
        self.takes = jnp.logical_not(self.sends)

        def copy(i):
            return pltpu.make_async_remote_copy(
                src_ref=src.at[pl.ds((src_unit + i) * UNIT, UNIT)],
                dst_ref=dst.at[pl.ds((dst_unit + i) * UNIT, UNIT)],
                send_sem=send.at[i],
                recv_sem=recv.at[i],
                device_id={"ctx": NCTX - 1 - c},
                device_id_type=MESH,
            )

        self.copy = copy

    def each(self, who, act):
        for i in range(GIVE):

            @pl.when(jnp.logical_and(who, i < self.given))
            def _():
                act(i)

    def start(self):
        self.each(self.sends, lambda i: self.copy(i).start())

    def wait_recv(self):
        self.each(self.takes, lambda i: self.copy(i).wait_recv())

    def wait_send(self):
        self.each(self.sends, lambda i: self.copy(i).wait_send())


def layer_kernel(
    unit, scale,
    k_ref, v_ref, cot_ref, q_ref, w_hbm,
    dq_ref, gk_ref, gv_ref, o_ref,
    w_ref, wsem, kv_ref, ca_ref, gt_ref, qw_ref, ga_ref, attn_ref, kept_ref, top_ref, m_row, l_row, acc_ref,
    attn_far, dq_par, dq_far, af_ref, flat_ref, ocore, osum, orow,
    dqs_ref, dk_ref, dv_ref,
    p_ref, t_ref, r_ref, m_ref, t2_ref, r2_ref, s_ref, y_ref,
    send, recv, hsend, hrecv,
):
    y, z, x = place()
    c, is_low, given = share()
    h = lax.axis_index("head")
    core, row = h ^ 1, h ^ 2
    mine, up = h % 2, h // 2
    partner, xs, zs = neighbours()

    def w_copy(i):
        cols = pl.ds(pl.multiple_of(i * WIDE, WIDE), WIDE)
        return pltpu.make_async_copy(w_hbm.at[:, cols], w_ref.at[i % 2], wsem.at[i % 2])

    def over_weight(act, first, last):
        chunks = w_hbm.shape[1] // WIDE

        def chunk(i, carry):
            w_copy(i).wait()
            act(i, w_ref.at[i % 2])

            @pl.when(i + 2 < chunks)
            def _():
                w_copy(i + 2).start()

            return carry

        lax.fori_loop(first, last, chunk, 0)

    w_copy(0).start()
    w_copy(1).start()
    greet([partner] + xs + zs + [NCTX - 1 - c], [core, row])
    mail = Courier(send, recv)

    def hand(i, *what):
        return Handover(hsend.at[i], hrecv.at[i], *what)

    kv_ref[c, 0] = k_ref[...]
    kv_ref[c, 1] = v_ref[...]
    mail.plan("pair", "ctx", partner, kv_ref.at[c], kv_ref.at[c])
    mail.go("pair")
    qs = hand(0, q_ref, 0, qw_ref, OWN, False)
    gs = hand(1, ga_ref, 0, ga_ref, OWN, False)
    attn_home = hand(2, attn_ref, OWN, attn_far, 0, True)
    dq_home = hand(3, dq_par, 0, dq_far, 0, True)
    ca_ref[h] = cot_ref[...]
    for name, o, i in (("cot row", row, h), ("cot core", core, h), ("cot relay", core, row)):
        mail.plan(name, "head", o, ca_ref.at[i], ca_ref.at[i])

    routes = ((z, x, zs, xs), (x, z, xs, zs))
    for n, (a, b, an, bn) in enumerate(routes):

        def slot(i, j, n=n):
            return kv_ref.at[jnp.where(n == 0, 16 + i * 4 + j, j * 4 + i)]

        for d in range(2):
            mail.plan((n, "beside", d), "ctx", an[d], slot(a, b), slot(a, b))
            part = slot((a + (3, 1)[d]) % 4, b).at[d]
            mail.plan((n, "on", d), "ctx", an[d], part, part)
            for s, off in enumerate((0, 3, 1, 2)):
                i = (a + off) % 4
                mail.plan((n, "third", s, d), "ctx", bn[d], slot(i, b), slot(i, b))
                part = slot(i, (b + (3, 1)[d]) % 4).at[d]
                mail.plan((n, "last", s, d), "ctx", bn[d], part, part)

    def pass_on(n, s):
        for d in range(2):
            mail.got((n, "third", s, d))
            mail.go((n, "last", s, d))

    for n, (a, an, b, bn) in enumerate(((x, xs, z, zs), (z, zs, x, xs))):
        steps = (
            (1, p_ref.at[n], a, an, t_ref.at[n], r_ref.at[n]),
            (2, m_ref.at[n], b, bn, t2_ref.at[n], r2_ref.at[n]),
        )
        for stage, piece, at, to, t, r in steps:
            for d in range(2):
                nxt = (at + (1, 3)[d]) % 4
                mail.plan((n, stage, "far", d), "ctx", to[d], piece.at[(at + 2) % 4, d], t.at[d])
                mail.plan(
                    (n, stage, "near", d), "ctx", to[d], piece.at[nxt, 1 - d], r.at[d, 1 - d]
                )
                mail.plan((n, stage, "sum", d), "ctx", to[d], t.at[d], r.at[d, d])
    mail.plan("y", "ctx", partner, s_ref.at[y], y_ref)
    part_cols = [pl.ds(CUT[k] * WIDE, (CUT[k + 1] - CUT[k]) * WIDE) for k in range(2)]
    for k, cols in enumerate(part_cols):
        for i in range(2):
            src = ca_ref.at[2 * i + 1 - mine, :, cols]
            mail.plan(("core", k, i), "head", core, src, ocore.at[i, :, cols])
        mail.plan(("row", k), "head", row, osum.at[1 - up, :, cols], orow.at[:, cols])

    def far(n, stage):
        mail.go((n, stage, "far", 0), (n, stage, "far", 1))

    def near(n, stage, d):
        mail.go((n, stage, "near", d))

    def relay(n, stage, d):
        piece, at, t = (
            (p_ref.at[n], (x, z)[n], t_ref.at[n])
            if stage == 1
            else (m_ref.at[n], (z, x)[n], t2_ref.at[n])
        )
        nxt = (at + (1, 3)[d]) % 4
        mail.got((n, stage, "far", d))
        t[d] = (piece[nxt, d].astype(F32) + t[d].astype(F32)).astype(BF)
        mail.go((n, stage, "sum", d))

    def arrived(n, stage):
        for d in range(2):
            mail.got((n, stage, "near", d), (n, stage, "sum", d))

    def total_first(n):
        at = (x, z)[n]
        for j in range(4):
            for kv in range(2):
                m_ref[n, j, kv] = (
                    p_ref[n, at, kv, j].astype(F32)
                    + r_ref[n, 0, kv, j].astype(F32)
                    + r_ref[n, 1, kv, j].astype(F32)
                ).astype(BF)
        far(n, 2)
        near(n, 2, 0)
        near(n, 2, 1)

    def total_second(n):
        arrived(n, 2)
        at = (z, x)[n]
        s_ref[n] = (
            m_ref[n, at].astype(F32) + r2_ref[n, 0].astype(F32) + r2_ref[n, 1].astype(F32)
        ).astype(BF)

    def output_projection(k):
        if k == 0:
            attn_home.wait_recv()
            own = OWN * UNIT
            af_ref[...] = attn_ref[pl.ds(0, own), :].astype(F32)

            def place_far(i):
                rows = pl.ds(i * UNIT, UNIT)
                af_ref[rows, :] = attn_far[rows, :].astype(F32)

            attn_home.each(attn_home.takes, place_far)
            for i in range(GROUP):
                flat_ref[:, i * HEAD : (i + 1) * HEAD] = af_ref[
                    pl.ds(i, BLOCK, stride=GROUP), :
                ].astype(BF)
            mail.sent("cot row", "cot core", "cot relay")

        def project(i, w):
            cols = pl.ds(pl.multiple_of(i * WIDE, WIDE), WIDE)
            part = dot(flat_ref[...], w[...], NN).astype(BF)
            ca_ref[:, :, cols] = part.reshape(4, BLOCK // 4, WIDE)

        over_weight(project, CUT[k], CUT[k + 1])
        mail.go(("core", k, 0), ("core", k, 1))

    def output_core(k):
        cols = part_cols[k]
        for i in range(2):
            mail.got(("core", k, i))
            osum[i, :, cols] = (
                ca_ref[2 * i + mine, :, cols].astype(F32) + ocore[i, :, cols].astype(F32)
            ).astype(BF)
        mail.go(("row", k))

    begin = jnp.where(is_low, 0, given)
    taken = OWN + jnp.where(is_low, given, 0)

    def inner(n, i):
        return turned(jnp.where(n == 0, z, x), i)

    def block_of(n, at, i, own_first=False):
        j = turned_back(jnp.where(n == 0, z, x), i) if own_first else inner(n, i)
        return jnp.where(n == 0, 16 + 4 * j + at, 4 * at + j)

    def over_pair(n, at, jp, tile, own_first, between, turns=(0, 2)):
        last = jnp.maximum(
            block_of(n, at, 2 * jp, own_first), block_of(n, at, 2 * jp + 1, own_first)
        )

        def row_set(turn, carry):
            mine_now = turn == (0 if own_first else 1)
            u0 = jnp.where(mine_now, begin, OWN)
            u1 = jnp.where(mine_now, OWN, taken)
            qb = jnp.where(mine_now, c, NCTX - 1 - c)
            pos0 = jnp.where(mine_now, 0, OWN)
            twos = (u1 - u0) // 2
            odd = (u1 - u0) % 2
            whole = qb > last

            def full(i, carry):
                tile(u0 + 2 * i, 2, 2 * jp, 2, None)
                return carry

            lax.fori_loop(0, jnp.where(whole, twos, 0), full, 0)

            @pl.when(jnp.logical_and(whole, odd == 1))
            def _():
                tile(u1 - 1, 1, 2 * jp, 2, None)

            def single_block(j, carry):
                ahead = (qb - block_of(n, at, j, own_first)) * BLOCK
                some = jnp.logical_and(jnp.logical_not(whole), ahead >= 0)

                def part(i, carry):
                    u = u0 + 2 * i
                    tile(u, 2, j, 1, ahead + (u - pos0) * UNIT_POS)
                    return carry

                lax.fori_loop(0, jnp.where(some, twos, 0), part, 0)

                @pl.when(jnp.logical_and(some, odd == 1))
                def _():
                    u = u1 - 1
                    tile(u, 1, j, 1, ahead + (u - pos0) * UNIT_POS)

                return carry

            lax.fori_loop(2 * jp, 2 * jp + 2, single_block, 0)

            @pl.when(turn == 0)
            def _():
                between()

            return carry

        lax.fori_loop(turns[0], turns[1], row_set, 0)

    def slot_of(b, u):
        own = b * (OWN - begin) + u - begin
        far = (c + 1) * (OWN - begin) + b * (taken - OWN) + u - OWN
        return jnp.where(u < OWN, own, far)

    def parts(first, units, held):
        for k, b in enumerate(held):
            for i in range(units):
                yield (
                    slot_of(b, first + i),
                    slice(k * BLOCK, (k + 1) * BLOCK),
                    slice(i * UNIT, (i + 1) * UNIT),
                )

    def rows_of(first, units):
        return pl.ds(pl.multiple_of(first * UNIT, UNIT), units * UNIT)

    def mask(keys, n, ahead):
        qpos = ahead + lax.broadcasted_iota(jnp.int32, (keys, n), 1) // GROUP
        return lax.broadcasted_iota(jnp.int32, (keys, n), 0) <= qpos

    def forward_group(step, carry):
        s = jnp.where(step < 6, step, jnp.where(step < 8, step + 2, step - 2))
        n = (1 - y + s) % 2
        i = s % 8 // 2
        off = jnp.where(i == 0, 0, jnp.where(i == 1, 3, jnp.where(i == 2, 1, 2)))
        at = (jnp.where(n == 0, x, z) + off) % 4

        @pl.when(s == 1)
        def _():
            each_pass(False, front_end)
            each_pass(True, lambda n: (pass_on(n, 0), pass_on(n, 1)))

        @pl.when(s == 2)
        def _():
            each_pass(True, lambda n: (pass_on(n, 2), pass_on(n, 3)))
            each_pass(False, lambda n: (pass_on(n, 0), pass_on(n, 1)))
            qs.wait_recv()

        @pl.when(s == 3)
        def _():
            each_pass(False, lambda n: (pass_on(n, 2), pass_on(n, 3)))

        @pl.when(s == 5)
        def _():
            mail.got("cot row")
            mail.go("cot relay")

        def arrived_last(n):
            for i in range(4):
                mail.got((n, "last", i, 0), (n, "last", i, 1))

        @pl.when(s == 6)
        def _():
            project_cotangent()
            each_pass(True, arrived_last)

        @pl.when(s == 7)
        def _():
            each_pass(False, arrived_last)

        def tile(first, units, j, blocks, ahead):
            rows = rows_of(first, units)
            held = [block_of(n, at, j + i, True) for i in range(blocks)]
            keys = jnp.concatenate([kv_ref[b, 0] for b in held], axis=0)
            values = jnp.concatenate([kv_ref[b, 1] for b in held], axis=0)
            sc = dot(keys, qw_ref[rows, :], NT)
            if ahead is not None:
                sc = jnp.where(mask(sc.shape[0], sc.shape[1], ahead), sc, LOW)
            top = m_row[:, rows]
            new = jnp.maximum(top, jnp.max(sc, axis=0, keepdims=True))
            alpha = jnp.exp2((top - new) * unit)
            p = jnp.exp2((sc - new) * unit)
            m_row[:, rows] = new
            l_row[:, rows] = l_row[:, rows] * alpha + jnp.sum(p, axis=0, keepdims=True)
            p = p.astype(BF)
            acc_ref[:, rows] = acc_ref[:, rows] * alpha + dot(values, p, TN)
            for slot, ks, us in parts(first, units, held):
                kept_ref[slot] = p[ks, us]
                top_ref[slot] = new[:, us]

        def pair(jp, carry):
            turns = (jnp.where(s >= 8, 1, 0), jnp.where(s < 2, 1, 2))
            over_pair(n, at, jp, tile, True, lambda: None, turns)

            @pl.when(jnp.logical_and(s == 0, jp == 0))
            def _():
                each_pass(True, front_end)
                each_pass(False, front)
                mail.go("cot row", "cot core")

            return carry

        lax.fori_loop(0, 2, pair, 0)
        return carry

    def project_cotangent():
        mail.got("cot core", "cot relay")
        gt_ref[...] = jnp.zeros_like(gt_ref)

        def project(i, w):
            cols = pl.ds(pl.multiple_of(i * WIDE, WIDE), WIDE)
            gt_ref[...] += dot(w[...], ca_ref[:, :, cols].reshape(BLOCK, WIDE), NT)

        over_weight(project, 0, w_hbm.shape[1] // WIDE)
        w_copy(0).start()
        w_copy(1).start()
        for i in range(GROUP):
            af_ref[pl.ds(i, BLOCK, stride=GROUP), :] = jnp.transpose(
                gt_ref[i * HEAD : (i + 1) * HEAD, :]
            )
        ga_ref[pl.ds(0, OWN * UNIT), :] = af_ref[...].astype(BF)
        gs.start()

    def each_pass(first, act):
        for n in range(2):

            @pl.when(y == (1 - n if first else n))
            def _():
                act(n)

    def start(n):
        mail.go((n, "beside", 0), (n, "beside", 1), (n, "third", 0, 0), (n, "third", 0, 1))

    def front(n):
        for d in range(2):
            mail.got((n, "beside", d))
            mail.go((n, "on", d), (n, "third", 1 + d, 0), (n, "third", 1 + d, 1))

    def front_end(n):
        mail.got((n, "on", 0), (n, "on", 1))
        mail.go((n, "third", 3, 0), (n, "third", 3, 1))

    each_pass(True, start)
    qw_ref[pl.ds(0, OWN * UNIT), :] = q_ref[...]
    m_row[...] = jnp.full_like(m_row, LOW)
    l_row[...] = jnp.zeros_like(l_row)
    acc_ref[...] = jnp.zeros_like(acc_ref)
    mail.got("pair")
    each_pass(False, start)
    qs.start()
    each_pass(True, front)
    lax.fori_loop(0, 10, forward_group, 0)

    def finish_forward(i, carry):
        rows = pl.ds(pl.multiple_of((i + 4) % 6 * 512, 512), 512)
        l = l_row[:, rows]
        attn_ref[rows, :] = jnp.transpose(acc_ref[:, rows] / l).astype(BF)
        m_row[:, rows] = m_row[:, rows] * unit + jnp.log2(l)

        @pl.when(i == 1)
        def _():
            attn_home.start()

        return carry

    lax.fori_loop(0, WORK // 512, finish_forward, 0)
    gs.wait_recv()

    def prepare(i, carry):
        rows = pl.ds(pl.multiple_of(i * 512, 512), 512)
        products = ga_ref[rows, :].astype(F32) * attn_ref[rows, :].astype(F32)
        l_row[:, rows] = jnp.sum(jnp.transpose(products), axis=0, keepdims=True)
        dqs_ref[rows, :] = jnp.zeros((512, HEAD), F32)
        return carry

    lax.fori_loop(0, WORK // 512, prepare, 0)

    def backward_group(s, carry):
        n = s % 2
        i = s // 2
        off = jnp.where(i == 0, 2, jnp.where(i == 1, 1, jnp.where(i == 2, 3, 0)))
        at = (jnp.where(n == 0, x, z) + off) % 4

        def tile(first, units, j, blocks, ahead):
            rows = rows_of(first, units)
            held = [block_of(n, at, j + i) for i in range(blocks)]
            keys = jnp.concatenate([kv_ref[b, 0] for b in held], axis=0)
            values = jnp.concatenate([kv_ref[b, 1] for b in held], axis=0)
            q = qw_ref[rows, :]
            ga = ga_ref[rows, :]
            lse = m_row[:, rows]
            pieces = [
                kept_ref[slot].astype(F32) * jnp.exp2(top_ref[slot] * unit - lse[:, us])
                for slot, ks, us in parts(first, units, held)
            ]
            p = jnp.concatenate(
                [
                    jnp.concatenate(pieces[k * units : (k + 1) * units], axis=1)
                    for k in range(blocks)
                ],
                axis=0,
            )
            ds = (p * (dot(values, ga, NT) - l_row[:, rows])).astype(BF)
            ks = pl.ds(pl.multiple_of(j % 2 * BLOCK, BLOCK), blocks * BLOCK)
            dv_ref[ks, :] += dot(p.astype(BF), ga, NN)
            dk_ref[ks, :] += dot(ds, q, NN)
            dqs_ref[rows, :] += dot(ds, keys, TN)

        def pair(jp, carry):
            dk_ref[...] = jnp.zeros_like(dk_ref)
            dv_ref[...] = jnp.zeros_like(dv_ref)

            def between():
                @pl.when(jnp.logical_and(s == 7, jp == 1))
                def _():
                    far_rows = pl.ds(OWN * UNIT, GIVE * UNIT)
                    dq_par[...] = (dqs_ref[far_rows, :] * scale).astype(BF)
                    dq_home.start()

            over_pair(n, at, jp, tile, False, between)
            for i in range(2):
                ks = pl.ds(i * BLOCK, BLOCK)
                j = inner(n, 2 * jp + i)
                p_ref[n, at, 0, j] = (dk_ref[ks, :] * scale).astype(BF)
                p_ref[n, at, 1, j] = dv_ref[ks, :].astype(BF)

            @pl.when(jnp.logical_and(s == 7, jp == 0))
            def _():
                arrived(0, 1)
                total_first(0)

            return carry

        lax.fori_loop(0, 2, pair, 0)

        @pl.when(s == 0)
        def _():
            far(0, 1)

        @pl.when(s == 1)
        def _():
            far(1, 1)

        @pl.when(s == 2)
        def _():
            near(0, 1, 0)
            relay(0, 1, 0)
            output_projection(0)

        @pl.when(s == 3)
        def _():
            near(1, 1, 0)
            relay(1, 1, 0)

        @pl.when(s == 4)
        def _():
            near(0, 1, 1)
            relay(0, 1, 1)
            output_core(0)

        @pl.when(s == 5)
        def _():
            near(1, 1, 1)
            relay(1, 1, 1)
            output_projection(1)

        @pl.when(s == 6)
        def _():
            output_core(1)

        return carry

    lax.fori_loop(0, 8, backward_group, 0)
    arrived(1, 1)
    total_first(1)
    relay(0, 2, 0)
    relay(0, 2, 1)
    dq_ref[...] = (dqs_ref[pl.ds(0, OWN * UNIT), :] * scale).astype(BF)
    relay(1, 2, 0)
    relay(1, 2, 1)
    total_second(0)

    @pl.when(y == 0)
    def _():
        mail.go("y")

    total_second(1)

    @pl.when(y == 1)
    def _():
        mail.go("y")

    mail.got(("row", 0), ("row", 1))
    o_ref[...] = (osum[up].astype(F32) + orow[...].astype(F32)).astype(BF)
    dq_home.wait_recv()

    def place_dq(i):
        rows = pl.ds(i * UNIT, UNIT)
        dq_ref[rows, :] = dq_far[rows, :]

    dq_home.each(dq_home.takes, place_dq)
    mail.got("y")
    gk_ref[...] = (s_ref[1 - y, 0].astype(F32) + y_ref[0].astype(F32)).astype(BF)
    gv_ref[...] = (s_ref[1 - y, 1].astype(F32) + y_ref[1].astype(F32)).astype(BF)
    mail.finish()
    for hand in (qs, gs, attn_home, dq_home):
        hand.wait_send()


COPIES = 1 + 3 + 2 * 20 + 2 * 2 * 6 + 1 + 6


def layer(unit, scale, k, v, cot, q, w):
    vm, dma = pltpu.VMEM, pltpu.SemaphoreType.DMA
    part = (BLOCK // 4, w.shape[1])
    return pl.pallas_call(
        functools.partial(layer_kernel, unit, scale),
        out_shape=(
            jax.ShapeDtypeStruct((OWN * UNIT, HEAD), BF),
            jax.ShapeDtypeStruct((BLOCK, HEAD), BF),
            jax.ShapeDtypeStruct((BLOCK, HEAD), BF),
            jax.ShapeDtypeStruct(part, BF),
        ),
        in_specs=vmem_specs(4) + [pl.BlockSpec(memory_space=pl.ANY)],
        out_specs=tuple(vmem_specs(4)),
        scratch_shapes=[
            vm((2, w.shape[0], WIDE), BF),
            dma((2,)),
            vm((NCTX, 2, BLOCK, HEAD), BF),
            vm((4,) + cot.shape, BF),
            vm((GROUP * HEAD, BLOCK), F32),
            vm((WORK, HEAD), BF),
            vm((WORK, HEAD), BF),
            vm((WORK, HEAD), BF),
            vm((SLOTS, BLOCK, UNIT), BF),
            vm((SLOTS, 1, UNIT), F32),
            vm((1, WORK), F32),
            vm((1, WORK), F32),
            vm((HEAD, WORK), F32),
            vm((GIVE * UNIT, HEAD), BF),
            vm((GIVE * UNIT, HEAD), BF),
            vm((GIVE * UNIT, HEAD), BF),
            vm((OWN * UNIT, HEAD), F32),
            vm((BLOCK, GROUP * HEAD), BF),
            vm((2,) + part, BF),
            vm((2,) + part, BF),
            vm(part, BF),
            vm((WORK, HEAD), F32),
            vm((2 * BLOCK, HEAD), F32),
            vm((2 * BLOCK, HEAD), F32),
            vm((2, 4, 2, 4, BLOCK, HEAD), BF),
            vm((2, 2, 4, BLOCK, HEAD), BF),
            vm((2, 2, 2, 4, BLOCK, HEAD), BF),
            vm((2, 4, 2, BLOCK, HEAD), BF),
            vm((2, 2, BLOCK, HEAD), BF),
            vm((2, 2, 2, BLOCK, HEAD), BF),
            vm((2, 2, BLOCK, HEAD), BF),
            vm((2, BLOCK, HEAD), BF),
            dma((COPIES,)),
            dma((COPIES,)),
            dma((4, GIVE)),
            dma((4, GIVE)),
        ],
        compiler_params=pltpu.CompilerParams(
            collective_id=0, has_side_effects=True, vmem_limit_bytes=VMEM_LIMIT
        ),
        name="layer",
    )(k, v, cot, q, w)


def results_kernel(*refs):
    n = len(refs) // 2
    for i in range(n):
        refs[n + i][...] = refs[i][...]


def results(*arrays):
    n = len(arrays)
    return pl.pallas_call(
        results_kernel,
        out_shape=tuple(jax.ShapeDtypeStruct(a.shape, a.dtype) for a in arrays),
        in_specs=vmem_specs(n),
        out_specs=tuple(vmem_specs(n)),
        compiler_params=pltpu.CompilerParams(vmem_limit_bytes=VMEM_LIMIT),
        name="results",
    )(*arrays)


def vmem_specs(n):
    return [pl.BlockSpec(memory_space=pltpu.VMEM)] * n


def local(queries, key_rows, value_matrix, out_weight, cotangent):
    rows, heads, head = queries.shape
    scale = 1.0 / math.sqrt(head)
    unit = scale * math.log2(math.e)
    made = layer(
        unit,
        scale,
        key_rows.reshape(rows, head),
        value_matrix.reshape(rows, head),
        cotangent,
        queries.reshape(rows * heads, head),
        out_weight,
    )
    grad_queries, grad_keys, grad_values, output = results(*made)
    return (
        output,
        grad_queries.reshape(rows, heads, head),
        grad_keys.reshape(rows, 1, head),
        grad_values.reshape(rows, 1, head),
    )


def solution(mesh):
    return jax.shard_map(
        local,
        mesh=mesh,
        in_specs=(
            P("ctx", "head", None),
            P("ctx", "head", None),
            P("ctx", "head", None),
            P("head", None),
            P(("ctx", "head"), None),
        ),
        out_specs=(
            P(("ctx", "head"), None),
            P("ctx", "head", None),
            P("ctx", "head", None),
            P("ctx", "head", None),
        ),
        check_vma=False,
    )
```

```python
import functools
import math

import jax
import jax.numpy as jnp
from jax import lax
from jax.experimental import pallas as pl
from jax.experimental.pallas import tpu as pltpu
from jax.sharding import PartitionSpec as P

BF = jnp.bfloat16
F32 = jnp.float32
MESH = pl.DeviceIdType.MESH
YS, ZS, XS = 2, 4, 4
NCTX = YS * ZS * XS
HEAD = 128
GROUP = 8
BLOCK = 256
UNIT = 256
UNIT_POS = UNIT // GROUP
OWN = BLOCK * GROUP // UNIT
GIVE = 4
WORK = (OWN + GIVE) * UNIT
LOW = -1e30
CUT = (0, 3, 5)
WIDE = 1024
SLOTS = 146
VMEM_LIMIT = 60 * 1024 * 1024

NT = (((1,), (1,)), ((), ()))
NN = (((1,), (0,)), ((), ()))
TN = (((0,), (0,)), ((), ()))


def dot(a, b, dims):
    return lax.dot_general(a, b, dims, preferred_element_type=F32)


def share():
    c = lax.axis_index("ctx")
    low = jnp.minimum(c, NCTX - 1 - c)
    given = jnp.where(
        low <= 2, 4, jnp.where(low <= 7, 3, jnp.where(low <= 11, 2, jnp.where(low <= 14, 1, 0)))
    )
    return c, c < NCTX // 2, given


def place():
    c = lax.axis_index("ctx")
    return c // (ZS * XS), (c // XS) % ZS, c % XS


def ctx_of(y, z, x):
    return (y * ZS + z) * XS + x


def turned_back(own, i):
    return (own + jnp.where(i == 0, 0, jnp.where(i == 1, 1, jnp.where(i == 2, 3, 2)))) % 4


def turned(own, i):
    return (own + jnp.where(i == 0, 2, jnp.where(i == 1, 1, jnp.where(i == 2, 3, 0)))) % 4


def neighbours():
    y, z, x = place()
    xs = [ctx_of(y, z, (x + d) % XS) for d in (1, XS - 1)]
    zs = [ctx_of(y, (z + d) % ZS, x) for d in (1, ZS - 1)]
    return ctx_of(1 - y, z, x), xs, zs


def greet(ctx_list, head_list):
    barrier = pltpu.get_barrier_semaphore()
    for other in ctx_list:
        pl.semaphore_signal(barrier, inc=1, device_id={"ctx": other}, device_id_type=MESH)
    for other in head_list:
        pl.semaphore_signal(barrier, inc=1, device_id={"head": other}, device_id_type=MESH)
    pl.semaphore_wait(barrier, len(ctx_list) + len(head_list))


class Courier:
    def __init__(self, send, recv):
        self.send, self.recv, self.made, self.count = send, recv, {}, 0

    def plan(self, name, axis, other, src, dst):
        n = self.count
        self.count += 1
        self.made[name] = lambda: pltpu.make_async_remote_copy(
            src_ref=src,
            dst_ref=dst,
            send_sem=self.send.at[n],
            recv_sem=self.recv.at[n],
            device_id={axis: other},
            device_id_type=MESH,
        )

    def go(self, *names):
        for name in names:
            self.made[name]().start()

    def got(self, *names):
        for name in names:
            self.made[name]().wait_recv()

    def sent(self, *names):
        for name in names:
            self.made.pop(name)().wait_send()

    def finish(self):
        self.sent(*list(self.made))


class Handover:
    def __init__(self, send, recv, src, src_unit, dst, dst_unit, from_low):
        c, is_low, given = share()
        self.given = given
        self.sends = is_low if from_low else jnp.logical_not(is_low)
        self.takes = jnp.logical_not(self.sends)

        def copy(i):
            return pltpu.make_async_remote_copy(
                src_ref=src.at[pl.ds((src_unit + i) * UNIT, UNIT)],
                dst_ref=dst.at[pl.ds((dst_unit + i) * UNIT, UNIT)],
                send_sem=send.at[i],
                recv_sem=recv.at[i],
                device_id={"ctx": NCTX - 1 - c},
                device_id_type=MESH,
            )

        self.copy = copy

    def each(self, who, act):
        for i in range(GIVE):

            @pl.when(jnp.logical_and(who, i < self.given))
            def _():
                act(i)

    def start(self):
        self.each(self.sends, lambda i: self.copy(i).start())

    def wait_recv(self):
        self.each(self.takes, lambda i: self.copy(i).wait_recv())

    def wait_send(self):
        self.each(self.sends, lambda i: self.copy(i).wait_send())


def layer_kernel(
    unit, scale,
    k_ref, v_ref, cot_ref, q_ref, w_hbm,
    dq_ref, gk_ref, gv_ref, o_ref,
    w_ref, wsem, kv_ref, ca_ref, gt_ref, qw_ref, ga_ref, attn_ref, kept_ref, top_ref, m_row, l_row, acc_ref,
    attn_far, dq_par, dq_far, af_ref, flat_ref, ocore, osum, orow,
    dqs_ref, dk_ref, dv_ref,
    p_ref, t_ref, r_ref, m_ref, t2_ref, r2_ref, s_ref, y_ref,
    send, recv, hsend, hrecv,
):
    y, z, x = place()
    c, is_low, given = share()
    h = lax.axis_index("head")
    core, row = h ^ 1, h ^ 2
    mine, up = h % 2, h // 2
    partner, xs, zs = neighbours()

    def w_copy(i):
        cols = pl.ds(pl.multiple_of(i * WIDE, WIDE), WIDE)
        return pltpu.make_async_copy(w_hbm.at[:, cols], w_ref.at[i % 2], wsem.at[i % 2])

    def over_weight(act, first, last):
        chunks = w_hbm.shape[1] // WIDE

        def chunk(i, carry):
            w_copy(i).wait()
            act(i, w_ref.at[i % 2])

            @pl.when(i + 2 < chunks)
            def _():
                w_copy(i + 2).start()

            return carry

        lax.fori_loop(first, last, chunk, 0)

    w_copy(0).start()
    w_copy(1).start()
    greet([partner] + xs + zs + [NCTX - 1 - c], [core, row])
    mail = Courier(send, recv)

    def hand(i, *what):
        return Handover(hsend.at[i], hrecv.at[i], *what)

    kv_ref[c, 0] = k_ref[...]
    kv_ref[c, 1] = v_ref[...]
    mail.plan("pair", "ctx", partner, kv_ref.at[c], kv_ref.at[c])
    mail.go("pair")
    qs = hand(0, q_ref, 0, qw_ref, OWN, False)
    gs = hand(1, ga_ref, 0, ga_ref, OWN, False)
    attn_home = hand(2, attn_ref, OWN, attn_far, 0, True)
    dq_home = hand(3, dq_par, 0, dq_far, 0, True)
    ca_ref[h] = cot_ref[...]
    for name, o, i in (("cot row", row, h), ("cot core", core, h), ("cot relay", core, row)):
        mail.plan(name, "head", o, ca_ref.at[i], ca_ref.at[i])

    routes = ((z, x, zs, xs), (x, z, xs, zs))
    for n, (a, b, an, bn) in enumerate(routes):

        def slot(i, j, n=n):
            return kv_ref.at[jnp.where(n == 0, 16 + i * 4 + j, j * 4 + i)]

        for d in range(2):
            mail.plan((n, "beside", d), "ctx", an[d], slot(a, b), slot(a, b))
            part = slot((a + (3, 1)[d]) % 4, b).at[d]
            mail.plan((n, "on", d), "ctx", an[d], part, part)
            for s, off in enumerate((0, 3, 1, 2)):
                i = (a + off) % 4
                mail.plan((n, "third", s, d), "ctx", bn[d], slot(i, b), slot(i, b))
                part = slot(i, (b + (3, 1)[d]) % 4).at[d]
                mail.plan((n, "last", s, d), "ctx", bn[d], part, part)

    def pass_on(n, s):
        for d in range(2):
            mail.got((n, "third", s, d))
            mail.go((n, "last", s, d))

    for n, (a, an, b, bn) in enumerate(((x, xs, z, zs), (z, zs, x, xs))):
        steps = (
            (1, p_ref.at[n], a, an, t_ref.at[n], r_ref.at[n]),
            (2, m_ref.at[n], b, bn, t2_ref.at[n], r2_ref.at[n]),
        )
        for stage, piece, at, to, t, r in steps:
            for d in range(2):
                nxt = (at + (1, 3)[d]) % 4
                mail.plan((n, stage, "far", d), "ctx", to[d], piece.at[(at + 2) % 4, d], t.at[d])
                mail.plan(
                    (n, stage, "near", d), "ctx", to[d], piece.at[nxt, 1 - d], r.at[d, 1 - d]
                )
                mail.plan((n, stage, "sum", d), "ctx", to[d], t.at[d], r.at[d, d])
    mail.plan("y", "ctx", partner, s_ref.at[y], y_ref)
    part_cols = [pl.ds(CUT[k] * WIDE, (CUT[k + 1] - CUT[k]) * WIDE) for k in range(2)]
    for k, cols in enumerate(part_cols):
        for i in range(2):
            src = ca_ref.at[2 * i + 1 - mine, :, cols]
            mail.plan(("core", k, i), "head", core, src, ocore.at[i, :, cols])
        mail.plan(("row", k), "head", row, osum.at[1 - up, :, cols], orow.at[:, cols])

    def far(n, stage):
        mail.go((n, stage, "far", 0), (n, stage, "far", 1))

    def near(n, stage, d):
        mail.go((n, stage, "near", d))

    def relay(n, stage, d):
        piece, at, t = (
            (p_ref.at[n], (x, z)[n], t_ref.at[n])
            if stage == 1
            else (m_ref.at[n], (z, x)[n], t2_ref.at[n])
        )
        nxt = (at + (1, 3)[d]) % 4
        mail.got((n, stage, "far", d))
        t[d] = (piece[nxt, d].astype(F32) + t[d].astype(F32)).astype(BF)
        mail.go((n, stage, "sum", d))

    def arrived(n, stage):
        for d in range(2):
            mail.got((n, stage, "near", d), (n, stage, "sum", d))

    def total_first(n, places):
        at = (x, z)[n]
        for place_now in places:
            j = turned((z, x)[n], place_now)
            for kv in range(2):
                m_ref[n, j, kv] = (
                    p_ref[n, at, kv, j].astype(F32)
                    + r_ref[n, 0, kv, j].astype(F32)
                    + r_ref[n, 1, kv, j].astype(F32)
                ).astype(BF)

    def total_second(n):
        arrived(n, 2)
        at = (z, x)[n]
        s_ref[n] = (
            m_ref[n, at].astype(F32) + r2_ref[n, 0].astype(F32) + r2_ref[n, 1].astype(F32)
        ).astype(BF)

    def output_projection(k):
        if k == 0:
            attn_home.wait_recv()
            own = OWN * UNIT
            af_ref[...] = attn_ref[pl.ds(0, own), :].astype(F32)

            def place_far(i):
                rows = pl.ds(i * UNIT, UNIT)
                af_ref[rows, :] = attn_far[rows, :].astype(F32)

            attn_home.each(attn_home.takes, place_far)
            for i in range(GROUP):
                flat_ref[:, i * HEAD : (i + 1) * HEAD] = af_ref[
                    pl.ds(i, BLOCK, stride=GROUP), :
                ].astype(BF)
            mail.sent("cot row", "cot core", "cot relay")

        def project(i, w):
            cols = pl.ds(pl.multiple_of(i * WIDE, WIDE), WIDE)
            part = dot(flat_ref[...], w[...], NN).astype(BF)
            ca_ref[:, :, cols] = part.reshape(4, BLOCK // 4, WIDE)

        over_weight(project, CUT[k], CUT[k + 1])
        mail.go(("core", k, 0), ("core", k, 1))

    def output_core(k):
        cols = part_cols[k]
        for i in range(2):
            mail.got(("core", k, i))
            osum[i, :, cols] = (
                ca_ref[2 * i + mine, :, cols].astype(F32) + ocore[i, :, cols].astype(F32)
            ).astype(BF)
        mail.go(("row", k))

    begin = jnp.where(is_low, 0, given)
    taken = OWN + jnp.where(is_low, given, 0)

    def inner(n, i):
        return turned(jnp.where(n == 0, z, x), i)

    def block_of(n, at, i, own_first=False):
        j = turned_back(jnp.where(n == 0, z, x), i) if own_first else inner(n, i)
        return jnp.where(n == 0, 16 + 4 * j + at, 4 * at + j)

    def over_pair(n, at, jp, tile, own_first, between, turns=(0, 2)):
        last = jnp.maximum(
            block_of(n, at, 2 * jp, own_first), block_of(n, at, 2 * jp + 1, own_first)
        )

        def row_set(turn, carry):
            mine_now = turn == (0 if own_first else 1)
            u0 = jnp.where(mine_now, begin, OWN)
            u1 = jnp.where(mine_now, OWN, taken)
            qb = jnp.where(mine_now, c, NCTX - 1 - c)
            pos0 = jnp.where(mine_now, 0, OWN)
            twos = (u1 - u0) // 2
            odd = (u1 - u0) % 2
            whole = qb > last

            def full(i, carry):
                tile(u0 + 2 * i, 2, 2 * jp, 2, None)
                return carry

            lax.fori_loop(0, jnp.where(whole, twos, 0), full, 0)

            @pl.when(jnp.logical_and(whole, odd == 1))
            def _():
                tile(u1 - 1, 1, 2 * jp, 2, None)

            def single_block(j, carry):
                ahead = (qb - block_of(n, at, j, own_first)) * BLOCK
                some = jnp.logical_and(jnp.logical_not(whole), ahead >= 0)

                def part(i, carry):
                    u = u0 + 2 * i
                    tile(u, 2, j, 1, ahead + (u - pos0) * UNIT_POS)
                    return carry

                lax.fori_loop(0, jnp.where(some, twos, 0), part, 0)

                @pl.when(jnp.logical_and(some, odd == 1))
                def _():
                    u = u1 - 1
                    tile(u, 1, j, 1, ahead + (u - pos0) * UNIT_POS)

                return carry

            lax.fori_loop(2 * jp, 2 * jp + 2, single_block, 0)

            @pl.when(turn == 0)
            def _():
                between()

            return carry

        lax.fori_loop(turns[0], turns[1], row_set, 0)

    def slot_of(b, u):
        own = b * (OWN - begin) + u - begin
        far = (c + 1) * (OWN - begin) + b * (taken - OWN) + u - OWN
        return jnp.where(u < OWN, own, far)

    def parts(first, units, held):
        for k, b in enumerate(held):
            for i in range(units):
                yield (
                    slot_of(b, first + i),
                    slice(k * BLOCK, (k + 1) * BLOCK),
                    slice(i * UNIT, (i + 1) * UNIT),
                )

    def rows_of(first, units):
        return pl.ds(pl.multiple_of(first * UNIT, UNIT), units * UNIT)

    def mask(keys, n, ahead):
        qpos = ahead + lax.broadcasted_iota(jnp.int32, (keys, n), 1) // GROUP
        return lax.broadcasted_iota(jnp.int32, (keys, n), 0) <= qpos

    def forward_group(s, carry):
        n = (1 - y + s) % 2
        i = s % 8 // 2
        off = jnp.where(i == 0, 0, jnp.where(i == 1, 3, jnp.where(i == 2, 1, 2)))
        at = (jnp.where(n == 0, x, z) + off) % 4

        @pl.when(s == 1)
        def _():
            each_pass(False, front_end)
            each_pass(True, lambda n: (pass_on(n, 0), pass_on(n, 1)))

        @pl.when(s == 2)
        def _():
            each_pass(True, lambda n: (pass_on(n, 2), pass_on(n, 3)))
            each_pass(False, lambda n: (pass_on(n, 0), pass_on(n, 1)))
            qs.wait_recv()

        @pl.when(s == 3)
        def _():
            each_pass(False, lambda n: (pass_on(n, 2), pass_on(n, 3)))

        @pl.when(s == 5)
        def _():
            mail.got("cot row")
            mail.go("cot relay")

        def arrived_last(n):
            for step in range(4):
                mail.got((n, "last", step, 0), (n, "last", step, 1))

        @pl.when(s == 6)
        def _():
            project_cotangent()
            each_pass(True, arrived_last)

        @pl.when(s == 7)
        def _():
            each_pass(False, arrived_last)

        def tile(first, units, j, blocks, ahead):
            rows = rows_of(first, units)
            held = [block_of(n, at, j + i, True) for i in range(blocks)]
            keys = jnp.concatenate([kv_ref[b, 0] for b in held], axis=0)
            values = jnp.concatenate([kv_ref[b, 1] for b in held], axis=0)
            sc = dot(keys, qw_ref[rows, :], NT)
            if ahead is not None:
                sc = jnp.where(mask(sc.shape[0], sc.shape[1], ahead), sc, LOW)
            top = m_row[:, rows]
            new = jnp.maximum(top, jnp.max(sc, axis=0, keepdims=True))
            alpha = jnp.exp2((top - new) * unit)
            p = jnp.exp2((sc - new) * unit)
            m_row[:, rows] = new
            l_row[:, rows] = l_row[:, rows] * alpha + jnp.sum(p, axis=0, keepdims=True)
            p = p.astype(BF)
            acc_ref[:, rows] = acc_ref[:, rows] * alpha + dot(values, p, TN)
            for slot, ks, us in parts(first, units, held):
                kept_ref[slot] = p[ks, us]
                top_ref[slot] = new[:, us]

        def pair(jp, carry):
            turns = (jnp.where(s >= 8, 1, 0), jnp.where(s < 2, 1, 2))
            over_pair(n, at, jp, tile, True, lambda: None, turns)

            @pl.when(jnp.logical_and(s == 0, jp == 0))
            def _():
                each_pass(True, front_end)
                each_pass(False, front)
                mail.go("cot row", "cot core")

            return carry

        lax.fori_loop(0, 2, pair, 0)
        return carry

    def project_cotangent():
        mail.got("cot core", "cot relay")
        gt_ref[...] = jnp.zeros_like(gt_ref)

        def project(i, w):
            cols = pl.ds(pl.multiple_of(i * WIDE, WIDE), WIDE)
            gt_ref[...] += dot(w[...], ca_ref[:, :, cols].reshape(BLOCK, WIDE), NT)

        over_weight(project, 0, w_hbm.shape[1] // WIDE)
        w_copy(0).start()
        w_copy(1).start()
        for i in range(GROUP):
            af_ref[pl.ds(i, BLOCK, stride=GROUP), :] = jnp.transpose(
                gt_ref[i * HEAD : (i + 1) * HEAD, :]
            )
        ga_ref[pl.ds(0, OWN * UNIT), :] = af_ref[...].astype(BF)
        gs.start()

    def each_pass(first, act):
        for n in range(2):

            @pl.when(y == (1 - n if first else n))
            def _():
                act(n)

    def start(n):
        mail.go((n, "beside", 0), (n, "beside", 1), (n, "third", 0, 0), (n, "third", 0, 1))

    def front(n):
        for d in range(2):
            mail.got((n, "beside", d))
            mail.go((n, "on", d), (n, "third", 1 + d, 0), (n, "third", 1 + d, 1))

    def front_end(n):
        mail.got((n, "on", 0), (n, "on", 1))
        mail.go((n, "third", 3, 0), (n, "third", 3, 1))

    each_pass(True, start)
    qw_ref[pl.ds(0, OWN * UNIT), :] = q_ref[...]
    m_row[...] = jnp.full_like(m_row, LOW)
    l_row[...] = jnp.zeros_like(l_row)
    acc_ref[...] = jnp.zeros_like(acc_ref)
    mail.got("pair")
    each_pass(False, start)
    qs.start()
    each_pass(True, front)
    lax.fori_loop(0, 10, forward_group, 0)

    def finish_forward(i, carry):
        rows = pl.ds(pl.multiple_of((i + 4) % 6 * 512, 512), 512)
        l = l_row[:, rows]
        attn_ref[rows, :] = jnp.transpose(acc_ref[:, rows] / l).astype(BF)
        m_row[:, rows] = m_row[:, rows] * unit + jnp.log2(l)

        @pl.when(i == 1)
        def _():
            attn_home.start()

        return carry

    lax.fori_loop(0, WORK // 512, finish_forward, 0)
    gs.wait_recv()

    def prepare(i, carry):
        rows = pl.ds(pl.multiple_of(i * 512, 512), 512)
        products = ga_ref[rows, :].astype(F32) * attn_ref[rows, :].astype(F32)
        l_row[:, rows] = jnp.sum(jnp.transpose(products), axis=0, keepdims=True)
        dqs_ref[rows, :] = jnp.zeros((512, HEAD), F32)
        return carry

    lax.fori_loop(0, WORK // 512, prepare, 0)

    def pass_of(foreign, act):
        for n in range(2):

            @pl.when(y == (n if foreign else 1 - n))
            def _():
                act(n)

    def backward_group(s, carry):
        n = (y + s) % 2
        i = s // 2
        off = jnp.where(i == 0, 2, jnp.where(i == 1, 1, jnp.where(i == 2, 3, 0)))
        at = (jnp.where(n == 0, x, z) + off) % 4

        def tile(first, units, j, blocks, ahead):
            rows = rows_of(first, units)
            held = [block_of(n, at, j + i) for i in range(blocks)]
            keys = jnp.concatenate([kv_ref[b, 0] for b in held], axis=0)
            values = jnp.concatenate([kv_ref[b, 1] for b in held], axis=0)
            q = qw_ref[rows, :]
            ga = ga_ref[rows, :]
            lse = m_row[:, rows]
            pieces = [
                kept_ref[slot].astype(F32) * jnp.exp2(top_ref[slot] * unit - lse[:, us])
                for slot, ks, us in parts(first, units, held)
            ]
            p = jnp.concatenate(
                [
                    jnp.concatenate(pieces[k * units : (k + 1) * units], axis=1)
                    for k in range(blocks)
                ],
                axis=0,
            )
            ds = (p * (dot(values, ga, NT) - l_row[:, rows])).astype(BF)
            ks = pl.ds(pl.multiple_of(j % 2 * BLOCK, BLOCK), blocks * BLOCK)
            dv_ref[ks, :] += dot(p.astype(BF), ga, NN)
            dk_ref[ks, :] += dot(ds, q, NN)
            dqs_ref[rows, :] += dot(ds, keys, TN)

        def pair(jp, carry):
            dk_ref[...] = jnp.zeros_like(dk_ref)
            dv_ref[...] = jnp.zeros_like(dv_ref)

            def between():
                @pl.when(jnp.logical_and(s == 7, jp == 1))
                def _():
                    far_rows = pl.ds(OWN * UNIT, GIVE * UNIT)
                    dq_par[...] = (dqs_ref[far_rows, :] * scale).astype(BF)
                    dq_home.start()
                    pass_of(True, lambda n: (relay(n, 2, 0), relay(n, 2, 1)))

            over_pair(n, at, jp, tile, False, between)
            for i in range(2):
                ks = pl.ds(i * BLOCK, BLOCK)
                j = inner(n, 2 * jp + i)
                p_ref[n, at, 0, j] = (dk_ref[ks, :] * scale).astype(BF)
                p_ref[n, at, 1, j] = dv_ref[ks, :].astype(BF)

            @pl.when(jnp.logical_and(s == 7, jp == 0))
            def _():
                def act(n):
                    arrived(n, 1)
                    total_first(n, (0, 1))
                    far(n, 2)
                    near(n, 2, 0)

                pass_of(False, act)

            return carry

        lax.fori_loop(0, 2, pair, 0)

        def hand_on(foreign, d):
            pass_of(foreign, lambda n: (near(n, 1, d), relay(n, 1, d)))

        @pl.when(s == 0)
        def _():
            pass_of(True, lambda n: far(n, 1))

        @pl.when(s == 1)
        def _():
            pass_of(False, lambda n: far(n, 1))

        @pl.when(s == 2)
        def _():
            hand_on(True, 0)
            output_projection(0)

        @pl.when(s == 3)
        def _():
            hand_on(False, 0)

        @pl.when(s == 4)
        def _():
            hand_on(True, 1)
            output_core(0)

        @pl.when(s == 5)
        def _():
            hand_on(False, 1)
            output_projection(1)

        @pl.when(s == 6)
        def _():
            output_core(1)

            def act(n):
                arrived(n, 1)
                total_first(n, range(4))
                far(n, 2)
                near(n, 2, 0)
                near(n, 2, 1)

            pass_of(True, act)

        return carry

    lax.fori_loop(0, 8, backward_group, 0)
    pass_of(False, lambda n: (total_first(n, (2, 3)), near(n, 2, 1)))
    pass_of(True, total_second)
    mail.go("y")
    pass_of(False, lambda n: (relay(n, 2, 0), relay(n, 2, 1)))
    dq_ref[...] = (dqs_ref[pl.ds(0, OWN * UNIT), :] * scale).astype(BF)
    pass_of(False, total_second)
    mail.got(("row", 0), ("row", 1))
    o_ref[...] = (osum[up].astype(F32) + orow[...].astype(F32)).astype(BF)
    dq_home.wait_recv()

    def place_dq(i):
        rows = pl.ds(i * UNIT, UNIT)
        dq_ref[rows, :] = dq_far[rows, :]

    dq_home.each(dq_home.takes, place_dq)
    mail.got("y")
    gk_ref[...] = (s_ref[1 - y, 0].astype(F32) + y_ref[0].astype(F32)).astype(BF)
    gv_ref[...] = (s_ref[1 - y, 1].astype(F32) + y_ref[1].astype(F32)).astype(BF)
    mail.finish()
    for hand in (qs, gs, attn_home, dq_home):
        hand.wait_send()


COPIES = 1 + 3 + 2 * 20 + 2 * 2 * 6 + 1 + 6


def layer(unit, scale, k, v, cot, q, w):
    vm, dma = pltpu.VMEM, pltpu.SemaphoreType.DMA
    part = (BLOCK // 4, w.shape[1])
    return pl.pallas_call(
        functools.partial(layer_kernel, unit, scale),
        out_shape=(
            jax.ShapeDtypeStruct((OWN * UNIT, HEAD), BF),
            jax.ShapeDtypeStruct((BLOCK, HEAD), BF),
            jax.ShapeDtypeStruct((BLOCK, HEAD), BF),
            jax.ShapeDtypeStruct(part, BF),
        ),
        in_specs=vmem_specs(4) + [pl.BlockSpec(memory_space=pl.ANY)],
        out_specs=tuple(vmem_specs(4)),
        scratch_shapes=[
            vm((2, w.shape[0], WIDE), BF),
            dma((2,)),
            vm((NCTX, 2, BLOCK, HEAD), BF),
            vm((4,) + cot.shape, BF),
            vm((GROUP * HEAD, BLOCK), F32),
            vm((WORK, HEAD), BF),
            vm((WORK, HEAD), BF),
            vm((WORK, HEAD), BF),
            vm((SLOTS, BLOCK, UNIT), BF),
            vm((SLOTS, 1, UNIT), F32),
            vm((1, WORK), F32),
            vm((1, WORK), F32),
            vm((HEAD, WORK), F32),
            vm((GIVE * UNIT, HEAD), BF),
            vm((GIVE * UNIT, HEAD), BF),
            vm((GIVE * UNIT, HEAD), BF),
            vm((OWN * UNIT, HEAD), F32),
            vm((BLOCK, GROUP * HEAD), BF),
            vm((2,) + part, BF),
            vm((2,) + part, BF),
            vm(part, BF),
            vm((WORK, HEAD), F32),
            vm((2 * BLOCK, HEAD), F32),
            vm((2 * BLOCK, HEAD), F32),
            vm((2, 4, 2, 4, BLOCK, HEAD), BF),
            vm((2, 2, 4, BLOCK, HEAD), BF),
            vm((2, 2, 2, 4, BLOCK, HEAD), BF),
            vm((2, 4, 2, BLOCK, HEAD), BF),
            vm((2, 2, BLOCK, HEAD), BF),
            vm((2, 2, 2, BLOCK, HEAD), BF),
            vm((2, 2, BLOCK, HEAD), BF),
            vm((2, BLOCK, HEAD), BF),
            dma((COPIES,)),
            dma((COPIES,)),
            dma((4, GIVE)),
            dma((4, GIVE)),
        ],
        compiler_params=pltpu.CompilerParams(
            collective_id=0, has_side_effects=True, vmem_limit_bytes=VMEM_LIMIT
        ),
        name="layer",
    )(k, v, cot, q, w)


def results_kernel(*refs):
    n = len(refs) // 2
    for i in range(n):
        refs[n + i][...] = refs[i][...]


def results(*arrays):
    n = len(arrays)
    return pl.pallas_call(
        results_kernel,
        out_shape=tuple(jax.ShapeDtypeStruct(a.shape, a.dtype) for a in arrays),
        in_specs=vmem_specs(n),
        out_specs=tuple(vmem_specs(n)),
        compiler_params=pltpu.CompilerParams(vmem_limit_bytes=VMEM_LIMIT),
        name="results",
    )(*arrays)


def vmem_specs(n):
    return [pl.BlockSpec(memory_space=pltpu.VMEM)] * n


def local(queries, key_rows, value_matrix, out_weight, cotangent):
    rows, heads, head = queries.shape
    scale = 1.0 / math.sqrt(head)
    unit = scale * math.log2(math.e)
    made = layer(
        unit,
        scale,
        key_rows.reshape(rows, head),
        value_matrix.reshape(rows, head),
        cotangent,
        queries.reshape(rows * heads, head),
        out_weight,
    )
    grad_queries, grad_keys, grad_values, output = results(*made)
    return (
        output,
        grad_queries.reshape(rows, heads, head),
        grad_keys.reshape(rows, 1, head),
        grad_values.reshape(rows, 1, head),
    )


def solution(mesh):
    return jax.shard_map(
        local,
        mesh=mesh,
        in_specs=(
            P("ctx", "head", None),
            P("ctx", "head", None),
            P("ctx", "head", None),
            P("head", None),
            P(("ctx", "head"), None),
        ),
        out_specs=(
            P(("ctx", "head"), None),
            P("ctx", "head", None),
            P("ctx", "head", None),
            P("ctx", "head", None),
        ),
        check_vma=False,
    )
```

```python
import functools
import math

import jax
import jax.numpy as jnp
from jax import lax
from jax.experimental import pallas as pl
from jax.experimental.pallas import tpu as pltpu
from jax.sharding import PartitionSpec as P

BF = jnp.bfloat16
F32 = jnp.float32
MESH = pl.DeviceIdType.MESH
YS, ZS, XS = 2, 4, 4
NCTX = YS * ZS * XS
HEAD = 128
GROUP = 8
BLOCK = 256
UNIT = 256
UNIT_POS = UNIT // GROUP
OWN = BLOCK * GROUP // UNIT
GIVE = 4
WORK = (OWN + GIVE) * UNIT
LOW = -1e30
CUT = (0, 3, 5)
WIDE = 1024
SLOTS = 146
VMEM_LIMIT = 60 * 1024 * 1024

NT = (((1,), (1,)), ((), ()))
NN = (((1,), (0,)), ((), ()))
TN = (((0,), (0,)), ((), ()))


def dot(a, b, dims):
    return lax.dot_general(a, b, dims, preferred_element_type=F32)


def share():
    c = lax.axis_index("ctx")
    low = jnp.minimum(c, NCTX - 1 - c)
    given = jnp.where(
        low <= 2, 4, jnp.where(low <= 7, 3, jnp.where(low <= 11, 2, jnp.where(low <= 14, 1, 0)))
    )
    return c, c < NCTX // 2, given


def place():
    c = lax.axis_index("ctx")
    return c // (ZS * XS), (c // XS) % ZS, c % XS


def ctx_of(y, z, x):
    return (y * ZS + z) * XS + x


def turned_back(own, i):
    return (own + jnp.where(i == 0, 0, jnp.where(i == 1, 1, jnp.where(i == 2, 3, 2)))) % 4


def turned(own, i):
    return (own + jnp.where(i == 0, 2, jnp.where(i == 1, 1, jnp.where(i == 2, 3, 0)))) % 4


def neighbours():
    y, z, x = place()
    xs = [ctx_of(y, z, (x + d) % XS) for d in (1, XS - 1)]
    zs = [ctx_of(y, (z + d) % ZS, x) for d in (1, ZS - 1)]
    return ctx_of(1 - y, z, x), xs, zs


def greet(ctx_list, head_list):
    barrier = pltpu.get_barrier_semaphore()
    for other in ctx_list:
        pl.semaphore_signal(barrier, inc=1, device_id={"ctx": other}, device_id_type=MESH)
    for other in head_list:
        pl.semaphore_signal(barrier, inc=1, device_id={"head": other}, device_id_type=MESH)
    pl.semaphore_wait(barrier, len(ctx_list) + len(head_list))


class Courier:
    def __init__(self, send, recv):
        self.send, self.recv, self.made, self.count = send, recv, {}, 0

    def plan(self, name, axis, other, src, dst):
        n = self.count
        self.count += 1
        self.made[name] = lambda: pltpu.make_async_remote_copy(
            src_ref=src,
            dst_ref=dst,
            send_sem=self.send.at[n],
            recv_sem=self.recv.at[n],
            device_id={axis: other},
            device_id_type=MESH,
        )

    def go(self, *names):
        for name in names:
            self.made[name]().start()

    def got(self, *names):
        for name in names:
            self.made[name]().wait_recv()

    def sent(self, *names):
        for name in names:
            self.made.pop(name)().wait_send()

    def finish(self):
        self.sent(*list(self.made))


class Handover:
    def __init__(self, send, recv, src, src_unit, dst, dst_unit, from_low):
        c, is_low, given = share()
        self.given = given
        self.sends = is_low if from_low else jnp.logical_not(is_low)
        self.takes = jnp.logical_not(self.sends)

        def copy(i):
            return pltpu.make_async_remote_copy(
                src_ref=src.at[pl.ds((src_unit + i) * UNIT, UNIT)],
                dst_ref=dst.at[pl.ds((dst_unit + i) * UNIT, UNIT)],
                send_sem=send.at[i],
                recv_sem=recv.at[i],
                device_id={"ctx": NCTX - 1 - c},
                device_id_type=MESH,
            )

        self.copy = copy

    def each(self, who, act):
        for i in range(GIVE):

            @pl.when(jnp.logical_and(who, i < self.given))
            def _():
                act(i)

    def start(self):
        self.each(self.sends, lambda i: self.copy(i).start())

    def wait_recv(self):
        self.each(self.takes, lambda i: self.copy(i).wait_recv())

    def wait_send(self):
        self.each(self.sends, lambda i: self.copy(i).wait_send())


def layer_kernel(
    unit, scale,
    k_ref, v_ref, cot_ref, q_ref, w_hbm,
    dq_ref, gk_ref, gv_ref, o_ref,
    w_ref, wsem, kv_ref, ca_ref, gt_ref, qw_ref, ga_ref, attn_ref, kept_ref, top_ref, m_row, l_row, acc_ref,
    attn_far, dq_par, dq_far, af_ref, flat_ref, ocore, osum, orow,
    dqs_ref, dk_ref, dv_ref,
    p_ref, t_ref, r_ref, m_ref, t2_ref, r2_ref, s_ref, y_ref,
    send, recv, hsend, hrecv,
):
    y, z, x = place()
    c, is_low, given = share()
    h = lax.axis_index("head")
    core, row = h ^ 1, h ^ 2
    mine, up = h % 2, h // 2
    partner, xs, zs = neighbours()

    def w_copy(i):
        cols = pl.ds(pl.multiple_of(i * WIDE, WIDE), WIDE)
        return pltpu.make_async_copy(w_hbm.at[:, cols], w_ref.at[i % 2], wsem.at[i % 2])

    def over_weight(act, first, last):
        chunks = w_hbm.shape[1] // WIDE

        def chunk(i, carry):
            w_copy(i).wait()
            act(i, w_ref.at[i % 2])

            @pl.when(i + 2 < chunks)
            def _():
                w_copy(i + 2).start()

            return carry

        lax.fori_loop(first, last, chunk, 0)

    w_copy(0).start()
    w_copy(1).start()
    greet([partner] + xs + zs + [NCTX - 1 - c], [core, row])
    mail = Courier(send, recv)

    def hand(i, *what):
        return Handover(hsend.at[i], hrecv.at[i], *what)

    kv_ref[c, 0] = k_ref[...]
    kv_ref[c, 1] = v_ref[...]
    mail.plan("pair", "ctx", partner, kv_ref.at[c], kv_ref.at[c])
    mail.go("pair")
    qs = hand(0, q_ref, 0, qw_ref, OWN, False)
    gs = hand(1, ga_ref, 0, ga_ref, OWN, False)
    attn_home = hand(2, attn_ref, OWN, attn_far, 0, True)
    dq_home = hand(3, dq_par, 0, dq_far, 0, True)
    ca_ref[h] = cot_ref[...]
    for name, o, i in (("cot row", row, h), ("cot core", core, h), ("cot relay", core, row)):
        mail.plan(name, "head", o, ca_ref.at[i], ca_ref.at[i])

    routes = ((z, x, zs, xs), (x, z, xs, zs))
    for n, (a, b, an, bn) in enumerate(routes):

        def slot(i, j, n=n):
            return kv_ref.at[jnp.where(n == 0, 16 + i * 4 + j, j * 4 + i)]

        for d in range(2):
            mail.plan((n, "beside", d), "ctx", an[d], slot(a, b), slot(a, b))
            part = slot((a + (3, 1)[d]) % 4, b).at[d]
            mail.plan((n, "on", d), "ctx", an[d], part, part)
            for s, off in enumerate((0, 3, 1, 2)):
                i = (a + off) % 4
                mail.plan((n, "third", s, d), "ctx", bn[d], slot(i, b), slot(i, b))
                part = slot(i, (b + (3, 1)[d]) % 4).at[d]
                mail.plan((n, "last", s, d), "ctx", bn[d], part, part)

    def pass_on(n, s):
        for d in range(2):
            mail.got((n, "third", s, d))
            mail.go((n, "last", s, d))

    for n, (a, an, b, bn) in enumerate(((x, xs, z, zs), (z, zs, x, xs))):
        steps = (
            (1, p_ref.at[n], a, an, t_ref.at[n], r_ref.at[n]),
            (2, m_ref.at[n], b, bn, t2_ref.at[n], r2_ref.at[n]),
        )
        for stage, piece, at, to, t, r in steps:
            for d in range(2):
                nxt = (at + (1, 3)[d]) % 4
                mail.plan((n, stage, "far", d), "ctx", to[d], piece.at[(at + 2) % 4, d], t.at[d])
                mail.plan(
                    (n, stage, "near", d), "ctx", to[d], piece.at[nxt, 1 - d], r.at[d, 1 - d]
                )
                mail.plan((n, stage, "sum", d), "ctx", to[d], t.at[d], r.at[d, d])
    mail.plan("y", "ctx", partner, s_ref.at[y], y_ref)
    part_cols = [pl.ds(CUT[k] * WIDE, (CUT[k + 1] - CUT[k]) * WIDE) for k in range(2)]
    for k, cols in enumerate(part_cols):
        for i in range(2):
            src = ca_ref.at[2 * i + 1 - mine, :, cols]
            mail.plan(("core", k, i), "head", core, src, ocore.at[i, :, cols])
        mail.plan(("row", k), "head", row, osum.at[1 - up, :, cols], orow.at[:, cols])

    def far(n, stage):
        mail.go((n, stage, "far", 0), (n, stage, "far", 1))

    def near(n, stage, d):
        mail.go((n, stage, "near", d))

    def relay(n, stage, d):
        piece, at, t = (
            (p_ref.at[n], (x, z)[n], t_ref.at[n])
            if stage == 1
            else (m_ref.at[n], (z, x)[n], t2_ref.at[n])
        )
        nxt = (at + (1, 3)[d]) % 4
        mail.got((n, stage, "far", d))
        t[d] = (piece[nxt, d].astype(F32) + t[d].astype(F32)).astype(BF)
        mail.go((n, stage, "sum", d))

    def arrived(n, stage):
        for d in range(2):
            mail.got((n, stage, "near", d), (n, stage, "sum", d))

    def total_first(n, places):
        at = (x, z)[n]
        for place_now in places:
            j = turned((z, x)[n], place_now)
            for kv in range(2):
                m_ref[n, j, kv] = (
                    p_ref[n, at, kv, j].astype(F32)
                    + r_ref[n, 0, kv, j].astype(F32)
                    + r_ref[n, 1, kv, j].astype(F32)
                ).astype(BF)

    def total_second(n):
        arrived(n, 2)
        at = (z, x)[n]
        s_ref[n] = (
            m_ref[n, at].astype(F32) + r2_ref[n, 0].astype(F32) + r2_ref[n, 1].astype(F32)
        ).astype(BF)

    def output_projection(k):
        if k == 0:
            attn_home.wait_recv()
            own = OWN * UNIT
            af_ref[...] = attn_ref[pl.ds(0, own), :].astype(F32)

            def place_far(i):
                rows = pl.ds(i * UNIT, UNIT)
                af_ref[rows, :] = attn_far[rows, :].astype(F32)

            attn_home.each(attn_home.takes, place_far)
            for i in range(GROUP):
                flat_ref[:, i * HEAD : (i + 1) * HEAD] = af_ref[
                    pl.ds(i, BLOCK, stride=GROUP), :
                ].astype(BF)
            mail.sent("cot row", "cot core", "cot relay")

        def project(i, w):
            cols = pl.ds(pl.multiple_of(i * WIDE, WIDE), WIDE)
            part = dot(flat_ref[...], w[...], NN).astype(BF)
            ca_ref[:, :, cols] = part.reshape(4, BLOCK // 4, WIDE)

        over_weight(project, CUT[k], CUT[k + 1])
        mail.go(("core", k, 0), ("core", k, 1))

    def output_core(k):
        cols = part_cols[k]
        for i in range(2):
            mail.got(("core", k, i))
            osum[i, :, cols] = (
                ca_ref[2 * i + mine, :, cols].astype(F32) + ocore[i, :, cols].astype(F32)
            ).astype(BF)
        mail.go(("row", k))

    begin = jnp.where(is_low, 0, given)
    taken = OWN + jnp.where(is_low, given, 0)

    def inner(n, i):
        return turned(jnp.where(n == 0, z, x), i)

    def block_of(n, at, i, own_first=False):
        j = turned_back(jnp.where(n == 0, z, x), i) if own_first else inner(n, i)
        return jnp.where(n == 0, 16 + 4 * j + at, 4 * at + j)

    def over_pair(n, at, jp, tile, own_first, between, turns=(0, 2)):
        last = jnp.maximum(
            block_of(n, at, 2 * jp, own_first), block_of(n, at, 2 * jp + 1, own_first)
        )

        def row_set(turn, carry):
            mine_now = turn == (0 if own_first else 1)
            u0 = jnp.where(mine_now, begin, OWN)
            u1 = jnp.where(mine_now, OWN, taken)
            qb = jnp.where(mine_now, c, NCTX - 1 - c)
            pos0 = jnp.where(mine_now, 0, OWN)
            twos = (u1 - u0) // 2
            odd = (u1 - u0) % 2
            whole = qb > last

            def full(i, carry):
                tile(u0 + 2 * i, 2, 2 * jp, 2, None)
                return carry

            lax.fori_loop(0, jnp.where(whole, twos, 0), full, 0)

            @pl.when(jnp.logical_and(whole, odd == 1))
            def _():
                tile(u1 - 1, 1, 2 * jp, 2, None)

            def single_block(j, carry):
                ahead = (qb - block_of(n, at, j, own_first)) * BLOCK
                some = jnp.logical_and(jnp.logical_not(whole), ahead >= 0)

                def part(i, carry):
                    u = u0 + 2 * i
                    tile(u, 2, j, 1, ahead + (u - pos0) * UNIT_POS)
                    return carry

                lax.fori_loop(0, jnp.where(some, twos, 0), part, 0)

                @pl.when(jnp.logical_and(some, odd == 1))
                def _():
                    u = u1 - 1
                    tile(u, 1, j, 1, ahead + (u - pos0) * UNIT_POS)

                return carry

            lax.fori_loop(2 * jp, 2 * jp + 2, single_block, 0)

            @pl.when(turn == 0)
            def _():
                between()

            return carry

        lax.fori_loop(turns[0], turns[1], row_set, 0)

    def slot_of(b, u):
        own = b * (OWN - begin) + u - begin
        far = (c + 1) * (OWN - begin) + b * (taken - OWN) + u - OWN
        return jnp.where(u < OWN, own, far)

    def parts(first, units, held):
        for k, b in enumerate(held):
            for i in range(units):
                yield (
                    slot_of(b, first + i),
                    slice(k * BLOCK, (k + 1) * BLOCK),
                    slice(i * UNIT, (i + 1) * UNIT),
                )

    def rows_of(first, units):
        return pl.ds(pl.multiple_of(first * UNIT, UNIT), units * UNIT)

    def mask(keys, n, ahead):
        qpos = ahead + lax.broadcasted_iota(jnp.int32, (keys, n), 1) // GROUP
        return lax.broadcasted_iota(jnp.int32, (keys, n), 0) <= qpos

    def forward_group(s, carry):
        n = (1 - y + s) % 2
        i = s % 8 // 2
        off = jnp.where(i == 0, 0, jnp.where(i == 1, 3, jnp.where(i == 2, 1, 2)))
        at = (jnp.where(n == 0, x, z) + off) % 4

        @pl.when(s == 1)
        def _():
            each_pass(False, front_end)
            each_pass(True, lambda n: (pass_on(n, 0), pass_on(n, 1)))

        @pl.when(s == 2)
        def _():
            each_pass(True, lambda n: (pass_on(n, 2), pass_on(n, 3)))
            each_pass(False, lambda n: (pass_on(n, 0), pass_on(n, 1)))
            qs.wait_recv()

        @pl.when(s == 3)
        def _():
            each_pass(False, lambda n: (pass_on(n, 2), pass_on(n, 3)))

        @pl.when(s == 5)
        def _():
            mail.got("cot row")
            mail.go("cot relay")

        def arrived_last(n):
            for step in range(4):
                mail.got((n, "last", step, 0), (n, "last", step, 1))

        @pl.when(s == 6)
        def _():
            project_cotangent()
            each_pass(True, arrived_last)

        @pl.when(s == 7)
        def _():
            each_pass(False, arrived_last)

        def tile(first, units, j, blocks, ahead):
            rows = rows_of(first, units)
            held = [block_of(n, at, j + i, True) for i in range(blocks)]
            keys = jnp.concatenate([kv_ref[b, 0] for b in held], axis=0)
            values = jnp.concatenate([kv_ref[b, 1] for b in held], axis=0)
            sc = dot(keys, qw_ref[rows, :], NT)
            if ahead is not None:
                sc = jnp.where(mask(sc.shape[0], sc.shape[1], ahead), sc, LOW)
            top = m_row[:, rows]
            new = jnp.maximum(top, jnp.max(sc, axis=0, keepdims=True))
            alpha = jnp.exp2((top - new) * unit)
            p = jnp.exp2((sc - new) * unit)
            m_row[:, rows] = new
            l_row[:, rows] = l_row[:, rows] * alpha + jnp.sum(p, axis=0, keepdims=True)
            p = p.astype(BF)
            acc_ref[:, rows] = acc_ref[:, rows] * alpha + dot(values, p, TN)
            for slot, ks, us in parts(first, units, held):
                kept_ref[slot] = p[ks, us]
                top_ref[slot] = new[:, us]

        def pair(jp, carry):
            turns = (jnp.where(s >= 8, 1, 0), jnp.where(s < 2, 1, 2))
            over_pair(n, at, jp, tile, True, lambda: None, turns)

            @pl.when(jnp.logical_and(s == 0, jp == 0))
            def _():
                each_pass(True, front_end)
                each_pass(False, front)
                mail.go("cot row", "cot core")

            return carry

        lax.fori_loop(0, 2, pair, 0)
        return carry

    def project_cotangent():
        mail.got("cot core", "cot relay")
        gt_ref[...] = jnp.zeros_like(gt_ref)

        def project(i, w):
            cols = pl.ds(pl.multiple_of(i * WIDE, WIDE), WIDE)
            gt_ref[...] += dot(w[...], ca_ref[:, :, cols].reshape(BLOCK, WIDE), NT)

        over_weight(project, 0, w_hbm.shape[1] // WIDE)
        w_copy(0).start()
        w_copy(1).start()
        for i in range(GROUP):
            af_ref[pl.ds(i, BLOCK, stride=GROUP), :] = jnp.transpose(
                gt_ref[i * HEAD : (i + 1) * HEAD, :]
            )
        ga_ref[pl.ds(0, OWN * UNIT), :] = af_ref[...].astype(BF)
        gs.start()

    def each_pass(first, act):
        for n in range(2):

            @pl.when(y == (1 - n if first else n))
            def _():
                act(n)

    def start(n):
        mail.go((n, "beside", 0), (n, "beside", 1), (n, "third", 0, 0), (n, "third", 0, 1))

    def front(n):
        for d in range(2):
            mail.got((n, "beside", d))
            mail.go((n, "on", d), (n, "third", 1 + d, 0), (n, "third", 1 + d, 1))

    def front_end(n):
        mail.got((n, "on", 0), (n, "on", 1))
        mail.go((n, "third", 3, 0), (n, "third", 3, 1))

    each_pass(True, start)
    qw_ref[pl.ds(0, OWN * UNIT), :] = q_ref[...]
    m_row[...] = jnp.full_like(m_row, LOW)
    l_row[...] = jnp.zeros_like(l_row)
    acc_ref[...] = jnp.zeros_like(acc_ref)
    mail.got("pair")
    each_pass(False, start)
    qs.start()
    each_pass(True, front)
    lax.fori_loop(0, 10, forward_group, 0)

    def finish_forward(i, carry):
        rows = pl.ds(pl.multiple_of((i + 4) % 6 * 512, 512), 512)
        l = l_row[:, rows]
        attn_ref[rows, :] = jnp.transpose(acc_ref[:, rows] / l).astype(BF)
        m_row[:, rows] = m_row[:, rows] * unit + jnp.log2(l)

        @pl.when(i == 1)
        def _():
            attn_home.start()

        return carry

    lax.fori_loop(0, WORK // 512, finish_forward, 0)
    gs.wait_recv()

    def prepare(i, carry):
        rows = pl.ds(pl.multiple_of(i * 512, 512), 512)
        products = ga_ref[rows, :].astype(F32) * attn_ref[rows, :].astype(F32)
        l_row[:, rows] = jnp.sum(jnp.transpose(products), axis=0, keepdims=True)
        dqs_ref[rows, :] = jnp.zeros((512, HEAD), F32)
        return carry

    lax.fori_loop(0, WORK // 512, prepare, 0)

    def pass_of(foreign, act):
        for n in range(2):

            @pl.when(y == (n if foreign else 1 - n))
            def _():
                act(n)

    def backward_group(s, carry):
        n = (y + s) % 2
        i = s // 2
        off = jnp.where(i == 0, 2, jnp.where(i == 1, 1, jnp.where(i == 2, 3, 0)))
        at = (jnp.where(n == 0, x, z) + off) % 4

        def tile(first, units, j, blocks, ahead):
            rows = rows_of(first, units)
            held = [block_of(n, at, j + i) for i in range(blocks)]
            keys = jnp.concatenate([kv_ref[b, 0] for b in held], axis=0)
            values = jnp.concatenate([kv_ref[b, 1] for b in held], axis=0)
            q = qw_ref[rows, :]
            ga = ga_ref[rows, :]
            lse = m_row[:, rows]
            pieces = [
                kept_ref[slot].astype(F32) * jnp.exp2(top_ref[slot] * unit - lse[:, us])
                for slot, ks, us in parts(first, units, held)
            ]
            p = jnp.concatenate(
                [
                    jnp.concatenate(pieces[k * units : (k + 1) * units], axis=1)
                    for k in range(blocks)
                ],
                axis=0,
            )
            ds = (p * (dot(values, ga, NT) - l_row[:, rows])).astype(BF)
            ks = pl.ds(pl.multiple_of(j * BLOCK, BLOCK), blocks * BLOCK)
            dv_ref[ks, :] += dot(p.astype(BF), ga, NN)
            dk_ref[ks, :] += dot(ds, q, NN)
            dqs_ref[rows, :] += dot(ds, keys, TN)

        dk_ref[...] = jnp.zeros_like(dk_ref)
        dv_ref[...] = jnp.zeros_like(dv_ref)

        def quarter(i, carry):
            ends = s == 7
            jp = jnp.where(ends, i % 2, i // 2)
            turn = jnp.where(ends, i // 2, i % 2)
            over_pair(n, at, jp, tile, False, lambda: None, (turn, turn + 1))

            @pl.when(turn == 1)
            def _():
                for k in range(2):
                    ks = pl.ds(pl.multiple_of((2 * jp + k) * BLOCK, BLOCK), BLOCK)
                    j = inner(n, 2 * jp + k)
                    p_ref[n, at, 0, j] = (dk_ref[ks, :] * scale).astype(BF)
                    p_ref[n, at, 1, j] = dv_ref[ks, :].astype(BF)

            @pl.when(jnp.logical_and(ends, i == 1))
            def _():
                far_rows = pl.ds(OWN * UNIT, GIVE * UNIT)
                dq_par[...] = (dqs_ref[far_rows, :] * scale).astype(BF)
                dq_home.start()

            @pl.when(jnp.logical_and(ends, i == 2))
            def _():
                def act(n):
                    arrived(n, 1)
                    total_first(n, (0, 1))
                    far(n, 2)
                    near(n, 2, 0)

                pass_of(False, act)
                pass_of(True, lambda n: (relay(n, 2, 0), relay(n, 2, 1)))

            return carry

        lax.fori_loop(0, 4, quarter, 0)

        def hand_on(foreign, d):
            pass_of(foreign, lambda n: (near(n, 1, d), relay(n, 1, d)))

        @pl.when(s == 0)
        def _():
            pass_of(True, lambda n: far(n, 1))

        @pl.when(s == 1)
        def _():
            pass_of(False, lambda n: far(n, 1))

        @pl.when(s == 2)
        def _():
            hand_on(True, 0)
            output_projection(0)

        @pl.when(s == 3)
        def _():
            hand_on(False, 0)

        @pl.when(s == 4)
        def _():
            hand_on(True, 1)
            output_core(0)

        @pl.when(s == 5)
        def _():
            hand_on(False, 1)
            output_projection(1)

        @pl.when(s == 6)
        def _():
            output_core(1)

            def act(n):
                arrived(n, 1)
                total_first(n, range(4))
                far(n, 2)
                near(n, 2, 0)
                near(n, 2, 1)

            pass_of(True, act)

        return carry

    lax.fori_loop(0, 8, backward_group, 0)
    pass_of(False, lambda n: (total_first(n, (2, 3)), near(n, 2, 1)))
    pass_of(True, total_second)
    mail.go("y")
    pass_of(False, lambda n: (relay(n, 2, 0), relay(n, 2, 1)))
    dq_ref[...] = (dqs_ref[pl.ds(0, OWN * UNIT), :] * scale).astype(BF)
    pass_of(False, total_second)
    mail.got(("row", 0), ("row", 1))
    o_ref[...] = (osum[up].astype(F32) + orow[...].astype(F32)).astype(BF)
    dq_home.wait_recv()

    def place_dq(i):
        rows = pl.ds(i * UNIT, UNIT)
        dq_ref[rows, :] = dq_far[rows, :]

    dq_home.each(dq_home.takes, place_dq)
    mail.got("y")
    gk_ref[...] = (s_ref[1 - y, 0].astype(F32) + y_ref[0].astype(F32)).astype(BF)
    gv_ref[...] = (s_ref[1 - y, 1].astype(F32) + y_ref[1].astype(F32)).astype(BF)
    mail.finish()
    for hand in (qs, gs, attn_home, dq_home):
        hand.wait_send()


COPIES = 1 + 3 + 2 * 20 + 2 * 2 * 6 + 1 + 6


def layer(unit, scale, k, v, cot, q, w):
    vm, dma = pltpu.VMEM, pltpu.SemaphoreType.DMA
    part = (BLOCK // 4, w.shape[1])
    return pl.pallas_call(
        functools.partial(layer_kernel, unit, scale),
        out_shape=(
            jax.ShapeDtypeStruct((OWN * UNIT, HEAD), BF),
            jax.ShapeDtypeStruct((BLOCK, HEAD), BF),
            jax.ShapeDtypeStruct((BLOCK, HEAD), BF),
            jax.ShapeDtypeStruct(part, BF),
        ),
        in_specs=vmem_specs(4) + [pl.BlockSpec(memory_space=pl.ANY)],
        out_specs=tuple(vmem_specs(4)),
        scratch_shapes=[
            vm((2, w.shape[0], WIDE), BF),
            dma((2,)),
            vm((NCTX, 2, BLOCK, HEAD), BF),
            vm((4,) + cot.shape, BF),
            vm((GROUP * HEAD, BLOCK), F32),
            vm((WORK, HEAD), BF),
            vm((WORK, HEAD), BF),
            vm((WORK, HEAD), BF),
            vm((SLOTS, BLOCK, UNIT), BF),
            vm((SLOTS, 1, UNIT), F32),
            vm((1, WORK), F32),
            vm((1, WORK), F32),
            vm((HEAD, WORK), F32),
            vm((GIVE * UNIT, HEAD), BF),
            vm((GIVE * UNIT, HEAD), BF),
            vm((GIVE * UNIT, HEAD), BF),
            vm((OWN * UNIT, HEAD), F32),
            vm((BLOCK, GROUP * HEAD), BF),
            vm((2,) + part, BF),
            vm((2,) + part, BF),
            vm(part, BF),
            vm((WORK, HEAD), F32),
            vm((4 * BLOCK, HEAD), F32),
            vm((4 * BLOCK, HEAD), F32),
            vm((2, 4, 2, 4, BLOCK, HEAD), BF),
            vm((2, 2, 4, BLOCK, HEAD), BF),
            vm((2, 2, 2, 4, BLOCK, HEAD), BF),
            vm((2, 4, 2, BLOCK, HEAD), BF),
            vm((2, 2, BLOCK, HEAD), BF),
            vm((2, 2, 2, BLOCK, HEAD), BF),
            vm((2, 2, BLOCK, HEAD), BF),
            vm((2, BLOCK, HEAD), BF),
            dma((COPIES,)),
            dma((COPIES,)),
            dma((4, GIVE)),
            dma((4, GIVE)),
        ],
        compiler_params=pltpu.CompilerParams(
            collective_id=0, has_side_effects=True, vmem_limit_bytes=VMEM_LIMIT
        ),
        name="layer",
    )(k, v, cot, q, w)


def results_kernel(*refs):
    n = len(refs) // 2
    for i in range(n):
        refs[n + i][...] = refs[i][...]


def results(*arrays):
    n = len(arrays)
    return pl.pallas_call(
        results_kernel,
        out_shape=tuple(jax.ShapeDtypeStruct(a.shape, a.dtype) for a in arrays),
        in_specs=vmem_specs(n),
        out_specs=tuple(vmem_specs(n)),
        compiler_params=pltpu.CompilerParams(vmem_limit_bytes=VMEM_LIMIT),
        name="results",
    )(*arrays)


def vmem_specs(n):
    return [pl.BlockSpec(memory_space=pltpu.VMEM)] * n


def local(queries, key_rows, value_matrix, out_weight, cotangent):
    rows, heads, head = queries.shape
    scale = 1.0 / math.sqrt(head)
    unit = scale * math.log2(math.e)
    made = layer(
        unit,
        scale,
        key_rows.reshape(rows, head),
        value_matrix.reshape(rows, head),
        cotangent,
        queries.reshape(rows * heads, head),
        out_weight,
    )
    grad_queries, grad_keys, grad_values, output = results(*made)
    return (
        output,
        grad_queries.reshape(rows, heads, head),
        grad_keys.reshape(rows, 1, head),
        grad_values.reshape(rows, 1, head),
    )


def solution(mesh):
    return jax.shard_map(
        local,
        mesh=mesh,
        in_specs=(
            P("ctx", "head", None),
            P("ctx", "head", None),
            P("ctx", "head", None),
            P("head", None),
            P(("ctx", "head"), None),
        ),
        out_specs=(
            P(("ctx", "head"), None),
            P("ctx", "head", None),
            P("ctx", "head", None),
            P("ctx", "head", None),
        ),
        check_vma=False,
    )
```

```python
import functools
import math

import jax
import jax.numpy as jnp
from jax import lax
from jax.experimental import pallas as pl
from jax.experimental.pallas import tpu as pltpu
from jax.sharding import PartitionSpec as P

BF = jnp.bfloat16
F32 = jnp.float32
MESH = pl.DeviceIdType.MESH
YS, ZS, XS = 2, 4, 4
NCTX = YS * ZS * XS
HEAD = 128
GROUP = 8
BLOCK = 256
UNIT = 256
UNIT_POS = UNIT // GROUP
OWN = BLOCK * GROUP // UNIT
GIVE = 4
WORK = (OWN + GIVE) * UNIT
LOW = -1e30
CUT = (0, 3, 5)
WIDE = 1024
SLOTS = 146
VMEM_LIMIT = 60 * 1024 * 1024

NT = (((1,), (1,)), ((), ()))
NN = (((1,), (0,)), ((), ()))
TN = (((0,), (0,)), ((), ()))


def dot(a, b, dims):
    return lax.dot_general(a, b, dims, preferred_element_type=F32)


def share():
    c = lax.axis_index("ctx")
    low = jnp.minimum(c, NCTX - 1 - c)
    given = jnp.where(
        low <= 2, 4, jnp.where(low <= 7, 3, jnp.where(low <= 11, 2, jnp.where(low <= 14, 1, 0)))
    )
    return c, c < NCTX // 2, given


def place():
    c = lax.axis_index("ctx")
    return c // (ZS * XS), (c // XS) % ZS, c % XS


def ctx_of(y, z, x):
    return (y * ZS + z) * XS + x


def turned_back(own, i):
    return (own + jnp.where(i == 0, 0, jnp.where(i == 1, 1, jnp.where(i == 2, 3, 2)))) % 4


def turned(own, i):
    return (own + jnp.where(i == 0, 2, jnp.where(i == 1, 1, jnp.where(i == 2, 3, 0)))) % 4


def neighbours():
    y, z, x = place()
    xs = [ctx_of(y, z, (x + d) % XS) for d in (1, XS - 1)]
    zs = [ctx_of(y, (z + d) % ZS, x) for d in (1, ZS - 1)]
    return ctx_of(1 - y, z, x), xs, zs


def greet(ctx_list, head_list):
    barrier = pltpu.get_barrier_semaphore()
    for other in ctx_list:
        pl.semaphore_signal(barrier, inc=1, device_id={"ctx": other}, device_id_type=MESH)
    for other in head_list:
        pl.semaphore_signal(barrier, inc=1, device_id={"head": other}, device_id_type=MESH)
    pl.semaphore_wait(barrier, len(ctx_list) + len(head_list))


class Courier:
    def __init__(self, send, recv):
        self.send, self.recv, self.made, self.count = send, recv, {}, 0

    def plan(self, name, axis, other, src, dst):
        n = self.count
        self.count += 1
        self.made[name] = lambda: pltpu.make_async_remote_copy(
            src_ref=src,
            dst_ref=dst,
            send_sem=self.send.at[n],
            recv_sem=self.recv.at[n],
            device_id={axis: other},
            device_id_type=MESH,
        )

    def go(self, *names):
        for name in names:
            self.made[name]().start()

    def got(self, *names):
        for name in names:
            self.made[name]().wait_recv()

    def sent(self, *names):
        for name in names:
            self.made.pop(name)().wait_send()

    def finish(self):
        self.sent(*list(self.made))


class Handover:
    def __init__(self, send, recv, src, src_unit, dst, dst_unit, from_low):
        c, is_low, given = share()
        self.given = given
        self.sends = is_low if from_low else jnp.logical_not(is_low)
        self.takes = jnp.logical_not(self.sends)

        def copy(i):
            return pltpu.make_async_remote_copy(
                src_ref=src.at[pl.ds((src_unit + i) * UNIT, UNIT)],
                dst_ref=dst.at[pl.ds((dst_unit + i) * UNIT, UNIT)],
                send_sem=send.at[i],
                recv_sem=recv.at[i],
                device_id={"ctx": NCTX - 1 - c},
                device_id_type=MESH,
            )

        self.copy = copy

    def each(self, who, act):
        for i in range(GIVE):

            @pl.when(jnp.logical_and(who, i < self.given))
            def _():
                act(i)

    def start(self):
        self.each(self.sends, lambda i: self.copy(i).start())

    def wait_recv(self):
        self.each(self.takes, lambda i: self.copy(i).wait_recv())

    def wait_send(self):
        self.each(self.sends, lambda i: self.copy(i).wait_send())


def layer_kernel(
    unit, scale,
    k_ref, v_ref, cot_ref, q_ref, w_hbm,
    dq_ref, gk_ref, gv_ref, o_ref,
    w_ref, wsem, kv_ref, ca_ref, gt_ref, qw_ref, ga_ref, attn_ref, kept_ref, top_ref, m_row, l_row, acc_ref,
    attn_far, dq_par, dq_far, af_ref, flat_ref, ocore, osum, orow,
    dqs_ref, dk_ref, dv_ref,
    p_ref, t_ref, r_ref, m_ref, t2_ref, r2_ref, s_ref, y_ref,
    send, recv, hsend, hrecv,
):
    y, z, x = place()
    c, is_low, given = share()
    h = lax.axis_index("head")
    core, row = h ^ 1, h ^ 2
    mine, up = h % 2, h // 2
    partner, xs, zs = neighbours()

    def w_copy(i):
        cols = pl.ds(pl.multiple_of(i * WIDE, WIDE), WIDE)
        return pltpu.make_async_copy(w_hbm.at[:, cols], w_ref.at[i % 2], wsem.at[i % 2])

    def over_weight(act, first, last):
        chunks = w_hbm.shape[1] // WIDE

        def chunk(i, carry):
            w_copy(i).wait()
            act(i, w_ref.at[i % 2])

            @pl.when(i + 2 < chunks)
            def _():
                w_copy(i + 2).start()

            return carry

        lax.fori_loop(first, last, chunk, 0)

    w_copy(0).start()
    w_copy(1).start()
    greet([partner] + xs + zs + [NCTX - 1 - c], [core, row])
    mail = Courier(send, recv)

    def hand(i, *what):
        return Handover(hsend.at[i], hrecv.at[i], *what)

    kv_ref[c, 0] = k_ref[...]
    kv_ref[c, 1] = v_ref[...]
    mail.plan("pair", "ctx", partner, kv_ref.at[c], kv_ref.at[c])
    mail.go("pair")
    qs = hand(0, q_ref, 0, qw_ref, OWN, False)
    gs = hand(1, ga_ref, 0, ga_ref, OWN, False)
    attn_home = hand(2, attn_ref, OWN, attn_far, 0, True)
    dq_home = hand(3, dq_par, 0, dq_far, 0, True)
    ca_ref[h] = cot_ref[...]
    for name, o, i in (("cot row", row, h), ("cot core", core, h), ("cot relay", core, row)):
        mail.plan(name, "head", o, ca_ref.at[i], ca_ref.at[i])

    routes = ((z, x, zs, xs), (x, z, xs, zs))
    for n, (a, b, an, bn) in enumerate(routes):

        def slot(i, j, n=n):
            return kv_ref.at[jnp.where(n == 0, 16 + i * 4 + j, j * 4 + i)]

        for d in range(2):
            mail.plan((n, "beside", d), "ctx", an[d], slot(a, b), slot(a, b))
            part = slot((a + (3, 1)[d]) % 4, b).at[d]
            mail.plan((n, "on", d), "ctx", an[d], part, part)
            for s, off in enumerate((0, 3, 1, 2)):
                i = (a + off) % 4
                mail.plan((n, "third", s, d), "ctx", bn[d], slot(i, b), slot(i, b))
                part = slot(i, (b + (3, 1)[d]) % 4).at[d]
                mail.plan((n, "last", s, d), "ctx", bn[d], part, part)

    def pass_on(n, s):
        for d in range(2):
            mail.got((n, "third", s, d))
            mail.go((n, "last", s, d))

    for n, (a, an, b, bn) in enumerate(((x, xs, z, zs), (z, zs, x, xs))):
        steps = (
            (1, p_ref.at[n], a, an, t_ref.at[n], r_ref.at[n]),
            (2, m_ref.at[n], b, bn, t2_ref.at[n], r2_ref.at[n]),
        )
        for stage, piece, at, to, t, r in steps:
            for d in range(2):
                nxt = (at + (1, 3)[d]) % 4
                mail.plan((n, stage, "far", d), "ctx", to[d], piece.at[(at + 2) % 4, d], t.at[d])
                mail.plan(
                    (n, stage, "near", d), "ctx", to[d], piece.at[nxt, 1 - d], r.at[d, 1 - d]
                )
                mail.plan((n, stage, "sum", d), "ctx", to[d], t.at[d], r.at[d, d])
    mail.plan("y", "ctx", partner, s_ref.at[y], y_ref)
    part_cols = [pl.ds(CUT[k] * WIDE, (CUT[k + 1] - CUT[k]) * WIDE) for k in range(2)]
    for k, cols in enumerate(part_cols):
        for i in range(2):
            src = ca_ref.at[2 * i + 1 - mine, :, cols]
            mail.plan(("core", k, i), "head", core, src, ocore.at[i, :, cols])
        mail.plan(("row", k), "head", row, osum.at[1 - up, :, cols], orow.at[:, cols])

    def far(n, stage):
        mail.go((n, stage, "far", 0), (n, stage, "far", 1))

    def near(n, stage, d):
        mail.go((n, stage, "near", d))

    def relay(n, stage, d):
        piece, at, t = (
            (p_ref.at[n], (x, z)[n], t_ref.at[n])
            if stage == 1
            else (m_ref.at[n], (z, x)[n], t2_ref.at[n])
        )
        nxt = (at + (1, 3)[d]) % 4
        mail.got((n, stage, "far", d))
        t[d] = (piece[nxt, d].astype(F32) + t[d].astype(F32)).astype(BF)
        mail.go((n, stage, "sum", d))

    def arrived(n, stage):
        for d in range(2):
            mail.got((n, stage, "near", d), (n, stage, "sum", d))

    def total_first(n, places):
        at = (x, z)[n]
        for place_now in places:
            j = turned((z, x)[n], place_now)
            for kv in range(2):
                m_ref[n, j, kv] = (
                    p_ref[n, at, kv, j].astype(F32)
                    + r_ref[n, 0, kv, j].astype(F32)
                    + r_ref[n, 1, kv, j].astype(F32)
                ).astype(BF)

    def total_second(n):
        arrived(n, 2)
        at = (z, x)[n]
        s_ref[n] = (
            m_ref[n, at].astype(F32) + r2_ref[n, 0].astype(F32) + r2_ref[n, 1].astype(F32)
        ).astype(BF)

    def output_projection(k):
        if k == 0:
            attn_home.wait_recv()
            own = OWN * UNIT
            af_ref[...] = attn_ref[pl.ds(0, own), :].astype(F32)

            def place_far(i):
                rows = pl.ds(i * UNIT, UNIT)
                af_ref[rows, :] = attn_far[rows, :].astype(F32)

            attn_home.each(attn_home.takes, place_far)
            for i in range(GROUP):
                flat_ref[:, i * HEAD : (i + 1) * HEAD] = af_ref[
                    pl.ds(i, BLOCK, stride=GROUP), :
                ].astype(BF)
            mail.sent("cot row", "cot core", "cot relay")

        def project(i, w):
            cols = pl.ds(pl.multiple_of(i * WIDE, WIDE), WIDE)
            part = dot(flat_ref[...], w[...], NN).astype(BF)
            ca_ref[:, :, cols] = part.reshape(4, BLOCK // 4, WIDE)

        over_weight(project, CUT[k], CUT[k + 1])
        mail.go(("core", k, 0), ("core", k, 1))

    def output_core(k):
        cols = part_cols[k]
        for i in range(2):
            mail.got(("core", k, i))
            osum[i, :, cols] = (
                ca_ref[2 * i + mine, :, cols].astype(F32) + ocore[i, :, cols].astype(F32)
            ).astype(BF)
        mail.go(("row", k))

    begin = jnp.where(is_low, 0, given)
    taken = OWN + jnp.where(is_low, given, 0)

    def inner(n, i):
        return turned(jnp.where(n == 0, z, x), i)

    def block_of(n, at, i, own_first=False):
        j = turned_back(jnp.where(n == 0, z, x), i) if own_first else inner(n, i)
        return jnp.where(n == 0, 16 + 4 * j + at, 4 * at + j)

    def over_pair(n, at, jp, tile, own_first, between, turns=(0, 2)):
        last = jnp.maximum(
            block_of(n, at, 2 * jp, own_first), block_of(n, at, 2 * jp + 1, own_first)
        )

        def row_set(turn, carry):
            mine_now = turn == (0 if own_first else 1)
            u0 = jnp.where(mine_now, begin, OWN)
            u1 = jnp.where(mine_now, OWN, taken)
            qb = jnp.where(mine_now, c, NCTX - 1 - c)
            pos0 = jnp.where(mine_now, 0, OWN)
            twos = (u1 - u0) // 2
            odd = (u1 - u0) % 2
            whole = qb > last

            def full(i, carry):
                tile(u0 + 2 * i, 2, 2 * jp, 2, None)
                return carry

            lax.fori_loop(0, jnp.where(whole, twos, 0), full, 0)

            @pl.when(jnp.logical_and(whole, odd == 1))
            def _():
                tile(u1 - 1, 1, 2 * jp, 2, None)

            def single_block(j, carry):
                ahead = (qb - block_of(n, at, j, own_first)) * BLOCK
                some = jnp.logical_and(jnp.logical_not(whole), ahead >= 0)

                def part(i, carry):
                    u = u0 + 2 * i
                    tile(u, 2, j, 1, ahead + (u - pos0) * UNIT_POS)
                    return carry

                lax.fori_loop(0, jnp.where(some, twos, 0), part, 0)

                @pl.when(jnp.logical_and(some, odd == 1))
                def _():
                    u = u1 - 1
                    tile(u, 1, j, 1, ahead + (u - pos0) * UNIT_POS)

                return carry

            lax.fori_loop(2 * jp, 2 * jp + 2, single_block, 0)

            @pl.when(turn == 0)
            def _():
                between()

            return carry

        lax.fori_loop(turns[0], turns[1], row_set, 0)

    def slot_of(b, u):
        own = b * (OWN - begin) + u - begin
        far = (c + 1) * (OWN - begin) + b * (taken - OWN) + u - OWN
        return jnp.where(u < OWN, own, far)

    def parts(first, units, held):
        for k, b in enumerate(held):
            for i in range(units):
                yield (
                    slot_of(b, first + i),
                    slice(k * BLOCK, (k + 1) * BLOCK),
                    slice(i * UNIT, (i + 1) * UNIT),
                )

    def rows_of(first, units):
        return pl.ds(pl.multiple_of(first * UNIT, UNIT), units * UNIT)

    def mask(keys, n, ahead):
        qpos = ahead + lax.broadcasted_iota(jnp.int32, (keys, n), 1) // GROUP
        return lax.broadcasted_iota(jnp.int32, (keys, n), 0) <= qpos

    def forward_group(step, carry):
        s = jnp.where(step < 6, step, jnp.where(step < 8, step + 2, step - 2))
        n = (1 - y + s) % 2
        i = s % 8 // 2
        off = jnp.where(i == 0, 0, jnp.where(i == 1, 3, jnp.where(i == 2, 1, 2)))
        at = (jnp.where(n == 0, x, z) + off) % 4

        @pl.when(s == 1)
        def _():
            each_pass(False, front_end)
            each_pass(True, lambda n: (pass_on(n, 0), pass_on(n, 1)))

        @pl.when(s == 2)
        def _():
            each_pass(True, lambda n: (pass_on(n, 2), pass_on(n, 3)))
            each_pass(False, lambda n: (pass_on(n, 0), pass_on(n, 1)))
            qs.wait_recv()

        @pl.when(s == 3)
        def _():
            each_pass(False, lambda n: (pass_on(n, 2), pass_on(n, 3)))

        @pl.when(s == 5)
        def _():
            mail.got("cot row")
            mail.go("cot relay")

        def arrived_last(n):
            for i in range(4):
                mail.got((n, "last", i, 0), (n, "last", i, 1))

        @pl.when(s == 6)
        def _():
            project_cotangent()
            each_pass(True, arrived_last)

        @pl.when(s == 7)
        def _():
            each_pass(False, arrived_last)

        def tile(first, units, j, blocks, ahead):
            rows = rows_of(first, units)
            held = [block_of(n, at, j + i, True) for i in range(blocks)]
            keys = jnp.concatenate([kv_ref[b, 0] for b in held], axis=0)
            values = jnp.concatenate([kv_ref[b, 1] for b in held], axis=0)
            sc = dot(keys, qw_ref[rows, :], NT)
            if ahead is not None:
                sc = jnp.where(mask(sc.shape[0], sc.shape[1], ahead), sc, LOW)
            top = m_row[:, rows]
            new = jnp.maximum(top, jnp.max(sc, axis=0, keepdims=True))
            alpha = jnp.exp2((top - new) * unit)
            p = jnp.exp2((sc - new) * unit)
            m_row[:, rows] = new
            l_row[:, rows] = l_row[:, rows] * alpha + jnp.sum(p, axis=0, keepdims=True)
            p = p.astype(BF)
            acc_ref[:, rows] = acc_ref[:, rows] * alpha + dot(values, p, TN)
            for slot, ks, us in parts(first, units, held):
                kept_ref[slot] = p[ks, us]
                top_ref[slot] = new[:, us]

        def pair(jp, carry):
            turns = (jnp.where(s >= 8, 1, 0), jnp.where(s < 2, 1, 2))
            over_pair(n, at, jp, tile, True, lambda: None, turns)

            @pl.when(jnp.logical_and(s == 0, jp == 0))
            def _():
                each_pass(True, front_end)
                each_pass(False, front)
                mail.go("cot row", "cot core")

            return carry

        lax.fori_loop(0, 2, pair, 0)
        return carry

    def project_cotangent():
        mail.got("cot core", "cot relay")
        gt_ref[...] = jnp.zeros_like(gt_ref)

        def project(i, w):
            cols = pl.ds(pl.multiple_of(i * WIDE, WIDE), WIDE)
            gt_ref[...] += dot(w[...], ca_ref[:, :, cols].reshape(BLOCK, WIDE), NT)

        over_weight(project, 0, w_hbm.shape[1] // WIDE)
        w_copy(0).start()
        w_copy(1).start()
        for i in range(GROUP):
            af_ref[pl.ds(i, BLOCK, stride=GROUP), :] = jnp.transpose(
                gt_ref[i * HEAD : (i + 1) * HEAD, :]
            )
        ga_ref[pl.ds(0, OWN * UNIT), :] = af_ref[...].astype(BF)
        gs.start()

    def each_pass(first, act):
        for n in range(2):

            @pl.when(y == (1 - n if first else n))
            def _():
                act(n)

    def start(n):
        mail.go((n, "beside", 0), (n, "beside", 1), (n, "third", 0, 0), (n, "third", 0, 1))

    def front(n):
        for d in range(2):
            mail.got((n, "beside", d))
            mail.go((n, "on", d), (n, "third", 1 + d, 0), (n, "third", 1 + d, 1))

    def front_end(n):
        mail.got((n, "on", 0), (n, "on", 1))
        mail.go((n, "third", 3, 0), (n, "third", 3, 1))

    each_pass(True, start)
    qw_ref[pl.ds(0, OWN * UNIT), :] = q_ref[...]
    m_row[...] = jnp.full_like(m_row, LOW)
    l_row[...] = jnp.zeros_like(l_row)
    acc_ref[...] = jnp.zeros_like(acc_ref)
    mail.got("pair")
    each_pass(False, start)
    qs.start()
    each_pass(True, front)
    lax.fori_loop(0, 10, forward_group, 0)

    def finish_forward(i, carry):
        rows = pl.ds(pl.multiple_of((i + 4) % 6 * 512, 512), 512)
        l = l_row[:, rows]
        attn_ref[rows, :] = jnp.transpose(acc_ref[:, rows] / l).astype(BF)
        m_row[:, rows] = m_row[:, rows] * unit + jnp.log2(l)

        @pl.when(i == 1)
        def _():
            attn_home.start()

        return carry

    lax.fori_loop(0, WORK // 512, finish_forward, 0)
    gs.wait_recv()

    def prepare(i, carry):
        rows = pl.ds(pl.multiple_of(i * 512, 512), 512)
        products = ga_ref[rows, :].astype(F32) * attn_ref[rows, :].astype(F32)
        l_row[:, rows] = jnp.sum(jnp.transpose(products), axis=0, keepdims=True)
        dqs_ref[rows, :] = jnp.zeros((512, HEAD), F32)
        return carry

    lax.fori_loop(0, WORK // 512, prepare, 0)

    def pass_of(foreign, act):
        for n in range(2):

            @pl.when(y == (n if foreign else 1 - n))
            def _():
                act(n)

    def backward_group(s, carry):
        n = (y + s) % 2
        i = s // 2
        off = jnp.where(i == 0, 2, jnp.where(i == 1, 1, jnp.where(i == 2, 3, 0)))
        at = (jnp.where(n == 0, x, z) + off) % 4

        def tile(first, units, j, blocks, ahead):
            rows = rows_of(first, units)
            held = [block_of(n, at, j + i) for i in range(blocks)]
            keys = jnp.concatenate([kv_ref[b, 0] for b in held], axis=0)
            values = jnp.concatenate([kv_ref[b, 1] for b in held], axis=0)
            q = qw_ref[rows, :]
            ga = ga_ref[rows, :]
            lse = m_row[:, rows]
            pieces = [
                kept_ref[slot].astype(F32) * jnp.exp2(top_ref[slot] * unit - lse[:, us])
                for slot, ks, us in parts(first, units, held)
            ]
            p = jnp.concatenate(
                [
                    jnp.concatenate(pieces[k * units : (k + 1) * units], axis=1)
                    for k in range(blocks)
                ],
                axis=0,
            )
            ds = (p * (dot(values, ga, NT) - l_row[:, rows])).astype(BF)
            ks = pl.ds(pl.multiple_of(j % 2 * BLOCK, BLOCK), blocks * BLOCK)
            dv_ref[ks, :] += dot(p.astype(BF), ga, NN)
            dk_ref[ks, :] += dot(ds, q, NN)
            dqs_ref[rows, :] += dot(ds, keys, TN)

        def pair(jp, carry):
            dk_ref[...] = jnp.zeros_like(dk_ref)
            dv_ref[...] = jnp.zeros_like(dv_ref)

            def between():
                @pl.when(jnp.logical_and(s == 7, jp == 1))
                def _():
                    far_rows = pl.ds(OWN * UNIT, GIVE * UNIT)
                    dq_par[...] = (dqs_ref[far_rows, :] * scale).astype(BF)
                    dq_home.start()
                    pass_of(True, lambda n: (relay(n, 2, 0), relay(n, 2, 1)))

            over_pair(n, at, jp, tile, False, between)
            for i in range(2):
                ks = pl.ds(i * BLOCK, BLOCK)
                j = inner(n, 2 * jp + i)
                p_ref[n, at, 0, j] = (dk_ref[ks, :] * scale).astype(BF)
                p_ref[n, at, 1, j] = dv_ref[ks, :].astype(BF)

            @pl.when(jnp.logical_and(s == 7, jp == 0))
            def _():
                def act(n):
                    arrived(n, 1)
                    total_first(n, (0, 1))
                    far(n, 2)
                    near(n, 2, 0)

                pass_of(False, act)

            return carry

        lax.fori_loop(0, 2, pair, 0)

        def hand_on(foreign, d):
            pass_of(foreign, lambda n: (near(n, 1, d), relay(n, 1, d)))

        @pl.when(s == 0)
        def _():
            pass_of(True, lambda n: far(n, 1))

        @pl.when(s == 1)
        def _():
            pass_of(False, lambda n: far(n, 1))

        @pl.when(s == 2)
        def _():
            hand_on(True, 0)
            output_projection(0)

        @pl.when(s == 3)
        def _():
            hand_on(False, 0)

        @pl.when(s == 4)
        def _():
            hand_on(True, 1)
            output_core(0)

        @pl.when(s == 5)
        def _():
            hand_on(False, 1)
            output_projection(1)

        @pl.when(s == 6)
        def _():
            output_core(1)

            def act(n):
                arrived(n, 1)
                total_first(n, range(4))
                far(n, 2)
                near(n, 2, 0)
                near(n, 2, 1)

            pass_of(True, act)

        return carry

    lax.fori_loop(0, 8, backward_group, 0)
    pass_of(False, lambda n: (total_first(n, (2, 3)), near(n, 2, 1)))
    pass_of(True, total_second)
    mail.go("y")
    pass_of(False, lambda n: (relay(n, 2, 0), relay(n, 2, 1)))
    dq_ref[...] = (dqs_ref[pl.ds(0, OWN * UNIT), :] * scale).astype(BF)
    pass_of(False, total_second)
    mail.got(("row", 0), ("row", 1))
    o_ref[...] = (osum[up].astype(F32) + orow[...].astype(F32)).astype(BF)
    dq_home.wait_recv()

    def place_dq(i):
        rows = pl.ds(i * UNIT, UNIT)
        dq_ref[rows, :] = dq_far[rows, :]

    dq_home.each(dq_home.takes, place_dq)
    mail.got("y")
    gk_ref[...] = (s_ref[1 - y, 0].astype(F32) + y_ref[0].astype(F32)).astype(BF)
    gv_ref[...] = (s_ref[1 - y, 1].astype(F32) + y_ref[1].astype(F32)).astype(BF)
    mail.finish()
    for hand in (qs, gs, attn_home, dq_home):
        hand.wait_send()


COPIES = 1 + 3 + 2 * 20 + 2 * 2 * 6 + 1 + 6


def layer(unit, scale, k, v, cot, q, w):
    vm, dma = pltpu.VMEM, pltpu.SemaphoreType.DMA
    part = (BLOCK // 4, w.shape[1])
    return pl.pallas_call(
        functools.partial(layer_kernel, unit, scale),
        out_shape=(
            jax.ShapeDtypeStruct((OWN * UNIT, HEAD), BF),
            jax.ShapeDtypeStruct((BLOCK, HEAD), BF),
            jax.ShapeDtypeStruct((BLOCK, HEAD), BF),
            jax.ShapeDtypeStruct(part, BF),
        ),
        in_specs=vmem_specs(4) + [pl.BlockSpec(memory_space=pl.ANY)],
        out_specs=tuple(vmem_specs(4)),
        scratch_shapes=[
            vm((2, w.shape[0], WIDE), BF),
            dma((2,)),
            vm((NCTX, 2, BLOCK, HEAD), BF),
            vm((4,) + cot.shape, BF),
            vm((GROUP * HEAD, BLOCK), F32),
            vm((WORK, HEAD), BF),
            vm((WORK, HEAD), BF),
            vm((WORK, HEAD), BF),
            vm((SLOTS, BLOCK, UNIT), BF),
            vm((SLOTS, 1, UNIT), F32),
            vm((1, WORK), F32),
            vm((1, WORK), F32),
            vm((HEAD, WORK), F32),
            vm((GIVE * UNIT, HEAD), BF),
            vm((GIVE * UNIT, HEAD), BF),
            vm((GIVE * UNIT, HEAD), BF),
            vm((OWN * UNIT, HEAD), F32),
            vm((BLOCK, GROUP * HEAD), BF),
            vm((2,) + part, BF),
            vm((2,) + part, BF),
            vm(part, BF),
            vm((WORK, HEAD), F32),
            vm((2 * BLOCK, HEAD), F32),
            vm((2 * BLOCK, HEAD), F32),
            vm((2, 4, 2, 4, BLOCK, HEAD), BF),
            vm((2, 2, 4, BLOCK, HEAD), BF),
            vm((2, 2, 2, 4, BLOCK, HEAD), BF),
            vm((2, 4, 2, BLOCK, HEAD), BF),
            vm((2, 2, BLOCK, HEAD), BF),
            vm((2, 2, 2, BLOCK, HEAD), BF),
            vm((2, 2, BLOCK, HEAD), BF),
            vm((2, BLOCK, HEAD), BF),
            dma((COPIES,)),
            dma((COPIES,)),
            dma((4, GIVE)),
            dma((4, GIVE)),
        ],
        compiler_params=pltpu.CompilerParams(
            collective_id=0, has_side_effects=True, vmem_limit_bytes=VMEM_LIMIT
        ),
        name="layer",
    )(k, v, cot, q, w)


def results_kernel(*refs):
    n = len(refs) // 2
    for i in range(n):
        refs[n + i][...] = refs[i][...]


def results(*arrays):
    n = len(arrays)
    return pl.pallas_call(
        results_kernel,
        out_shape=tuple(jax.ShapeDtypeStruct(a.shape, a.dtype) for a in arrays),
        in_specs=vmem_specs(n),
        out_specs=tuple(vmem_specs(n)),
        compiler_params=pltpu.CompilerParams(vmem_limit_bytes=VMEM_LIMIT),
        name="results",
    )(*arrays)


def vmem_specs(n):
    return [pl.BlockSpec(memory_space=pltpu.VMEM)] * n


def local(queries, key_rows, value_matrix, out_weight, cotangent):
    rows, heads, head = queries.shape
    scale = 1.0 / math.sqrt(head)
    unit = scale * math.log2(math.e)
    made = layer(
        unit,
        scale,
        key_rows.reshape(rows, head),
        value_matrix.reshape(rows, head),
        cotangent,
        queries.reshape(rows * heads, head),
        out_weight,
    )
    grad_queries, grad_keys, grad_values, output = results(*made)
    return (
        output,
        grad_queries.reshape(rows, heads, head),
        grad_keys.reshape(rows, 1, head),
        grad_values.reshape(rows, 1, head),
    )


def solution(mesh):
    return jax.shard_map(
        local,
        mesh=mesh,
        in_specs=(
            P("ctx", "head", None),
            P("ctx", "head", None),
            P("ctx", "head", None),
            P("head", None),
            P(("ctx", "head"), None),
        ),
        out_specs=(
            P(("ctx", "head"), None),
            P("ctx", "head", None),
            P("ctx", "head", None),
            P("ctx", "head", None),
        ),
        check_vma=False,
    )
```
